32 devices in a mesh: frame: 4 (over y, core), space: 8 (over z, x).
Axes of the slice: x: 2, y: 2, z: 4, core: 2. Of those that a mesh axis runs over, the one named last changes fastest.
Arguments:
- frames_in: bfloat16 [8, 1024, 2048], P('frame', 'space'), may hold values from -6 to 6
- levels: int32 [8], P('frame'), may hold values from 1 to 899
- fresh: bfloat16 [1024, 2048], P('space'), may hold values from -6 to 6
- w_mod: bfloat16 [256, 4096], replicated, may hold values from -0.375 to 0.375
- w_qkv: bfloat16 [2048, 3072], P('space'), may hold values from -0.26516504 to 0.26516504
- q_gain: float32 [8], replicated, may hold values from 0.5 to 64
- w_out: bfloat16 [1024, 2048], P('space'), may hold values from -0.1875 to 0.1875
Outputs:
- frames_out: bfloat16 [8, 1024, 2048], P('frame', 'space')
The draws below stay inside these ranges and needn't reach their ends.
All inputs are finite; a program needn't handle non-finite values.
Results may differ from the reference program's by a relative error of at most 0.0075.
The reference program's roundings to bfloat16 on the way count: a program that leaves them out, or rounds other values in their place, can miss the bound.
Values may be sent and summed in bfloat16 or wider, within the bound.
A program may use at most 128 MiB of HBM per device.

```python
import math
import jax
import jax.numpy as jnp
from jax import lax

D = 2048
HEADS = 8
HD = 128
FREQ = 256
LEVELS = 1000
FRAMES = 8
HALF = 128
TOKENS = 1024


def draw_frames_in(key, part):
    key = jax.random.fold_in(key, 11)
    first_key, second_key = jax.random.split(key)
    common = jax.random.normal(first_key, (TOKENS, D), jnp.float32)
    noise = jax.random.normal(second_key, (FRAMES, TOKENS, D), jnp.float32)
    values = common[None] + 0.5 * noise
    return jnp.clip(values, -6.0, 6.0).astype(jnp.bfloat16)


def draw_w_mod(key, part):
    key = jax.random.fold_in(key, 12)
    values = jax.random.normal(key, (FREQ, 2 * D), jnp.float32)
    values = jnp.clip(values, -6.0, 6.0) * FREQ ** (-0.5)
    return values.astype(jnp.bfloat16)


def draw_w_qkv(key, part):
    key = jax.random.fold_in(key, 13)
    first_key = jax.random.fold_in(key, 0)
    inner = HEADS * HD
    base = jnp.clip(jax.random.normal(first_key, (D, 3 * inner), jnp.float32), -3.0, 3.0)
    query_part = base[:, :inner]
    key_part = 0.5 * query_part + 0.866 * base[:, inner:2 * inner]
    values = jnp.concatenate([query_part, key_part, base[:, 2 * inner:]], axis=1) * D ** (-0.5)
    return values.astype(jnp.bfloat16)


def draw_q_gain(key, part):
    key = jax.random.fold_in(key, 17)
    second_key = jax.random.fold_in(key, 1)
    values = jnp.exp(jax.random.uniform(second_key, (HEADS,), jnp.float32, math.log(0.5), math.log(8.0)))
    return values.astype(jnp.float32)


def with_ends(result, key, smallest, largest):
    shape = result.shape
    index_at = [jax.random.randint(jax.random.fold_in(key, axis), (), 0, shape[axis]) for axis in range(len(shape))]
    result = result.at[tuple(index_at)].set(smallest)
    longest = shape.index(max(shape))
    index_at[longest] = (index_at[longest] + 1) % shape[longest]
    return result.at[tuple(index_at)].set(largest)


def block_scale(own_key, extent, cuts, smallest, high):
    loudness = 1.0
    for position, shards_of in cuts:
        steps = jax.random.uniform(jax.random.fold_in(jax.random.fold_in(own_key, 6), position), (shards_of,), jnp.float32, smallest / len(cuts), high / len(cuts))
        loudness = loudness * jnp.repeat(jnp.exp(steps), extent[position] // shards_of).reshape((-1,) + (1,) * (len(extent) - 1 - position))
    return loudness


def bell_draw(key, dims, scale, bound, cuts=(), held_as=jnp.bfloat16):
    loudness = block_scale(key, dims, cuts, -0.22, 0.18) if cuts else 1.0
    array = jax.random.normal(key, dims, jnp.float32) * scale * loudness
    return jnp.minimum(jnp.maximum(array, -bound), bound).astype(held_as)


def setup_inputs(seed: int = 0) -> dict:
    key_of = jax.random.split(jax.random.key(seed), 8)
    return {
        "frames_in": draw_frames_in(jax.random.fold_in(key_of[7], 71), 0),
        "levels": with_ends(jax.random.randint(key_of[1], (FRAMES,), 1, 900), jax.random.fold_in(key_of[1], 1), 1, 899).astype(jnp.int32),
        "fresh": bell_draw(key_of[2], (TOKENS, D), 1.0, 6.0, ((0, 8),)),
        "w_mod": draw_w_mod(jax.random.fold_in(key_of[7], 71), 0),
        "w_qkv": draw_w_qkv(jax.random.fold_in(key_of[7], 71), 0),
        "q_gain": draw_q_gain(jax.random.fold_in(key_of[7], 71), 0),
        "w_out": bell_draw(key_of[6], (HEADS * HD, D), (HEADS * HD) ** -0.5, 0.1875, ((0, 8),)),
    }


def embed(levels):
    half = FREQ // 2
    freqs = jnp.exp(-math.log(10000.0) * jnp.arange(half, dtype=jnp.float32) / half)
    angles = levels.astype(jnp.float32)[:, None] * freqs[None, :]
    return jnp.concatenate([jnp.cos(angles), jnp.sin(angles)], axis=1).astype(jnp.bfloat16)

def alpha_bar(steps):
    frac = steps.astype(jnp.float32) / LEVELS
    return jnp.cos((frac + 0.008) / 1.008 * (math.pi / 2)) ** 2

def reference(frames_in, levels, fresh, w_mod, w_qkv, q_gain, w_out):
    mod = jnp.dot(embed(levels), w_mod, preferred_element_type=jnp.float32)
    shift = mod[:, :D]
    scale = mod[:, D:]
    x32 = frames_in.astype(jnp.float32)
    mean = lax.optimization_barrier(jnp.mean(x32, axis=-1, keepdims=True))
    var = lax.optimization_barrier(jnp.mean((x32 - mean) ** 2, axis=-1, keepdims=True))
    normed = (x32 - mean) * lax.rsqrt(var + 1e-06)
    xm = (normed * (1.0 + scale[:, None, :]) + shift[:, None, :]).astype(jnp.bfloat16)

    def project(rows):
        qkv = jnp.dot(rows, w_qkv, preferred_element_type=jnp.float32).reshape(TOKENS, 3, HEADS, HD)
        query = qkv[:, 0]
        key = qkv[:, 1]
        query = query * lax.rsqrt(lax.optimization_barrier(jnp.mean(query * query, axis=-1, keepdims=True)) + 1e-06) * q_gain[None, :, None]
        key = key * lax.rsqrt(lax.optimization_barrier(jnp.mean(key * key, axis=-1, keepdims=True)) + 1e-06)
        return (query.astype(jnp.bfloat16), key.astype(jnp.bfloat16), qkv[:, 2].astype(jnp.bfloat16))
    queries, keys, values = lax.map(project, xm)
    blocks = TOKENS // HALF
    inv = 1.0 / math.sqrt(HD)
    kk = jnp.arange(3 * HALF)[None, :]
    rr = jnp.arange(HALF)[:, None]
    band = jnp.abs(kk - rr - HALF) <= HALF
    order = jnp.arange(FRAMES)
    v_all = values.astype(jnp.float32).reshape(FRAMES, blocks, HALF, HEADS, HD)
    k_all = keys.astype(jnp.float32)
    results = []
    for frame in range(FRAMES):
        qb = queries[frame].astype(jnp.float32).reshape(blocks, HALF, HEADS, HD)
        kb = keys[frame].astype(jnp.float32).reshape(blocks, HALF, HEADS, HD)
        vb = values[frame].astype(jnp.float32).reshape(blocks, HALF, HEADS, HD)
        kwin = jnp.concatenate([jnp.roll(kb, 1, axis=0), kb, jnp.roll(kb, -1, axis=0)], axis=1)
        vwin = jnp.concatenate([jnp.roll(vb, 1, axis=0), vb, jnp.roll(vb, -1, axis=0)], axis=1)
        spatial = jnp.einsum('brhd,bkhd->bhrk', qb, kwin) * inv
        spatial = jnp.where(band[None, None], spatial, -1e+30)
        temporal = jnp.einsum('thd,gthd->thg', queries[frame].astype(jnp.float32), k_all) * inv
        causal = order < frame
        temporal = jnp.where(causal[None, None, :], temporal, -1e+30)
        temporal = temporal.reshape(blocks, HALF, HEADS, FRAMES).transpose(0, 2, 1, 3)
        top = jnp.maximum(lax.optimization_barrier(jnp.max(spatial, axis=-1)), lax.optimization_barrier(jnp.max(temporal, axis=-1)))
        p_space = jnp.where(band[None, None], jnp.exp(spatial - top[..., None]), 0.0)
        p_time = jnp.where(causal[None, None, None, :], jnp.exp(temporal - top[..., None]), 0.0)
        total = lax.optimization_barrier(jnp.sum(p_space, axis=-1)) + lax.optimization_barrier(jnp.sum(p_time, axis=-1))
        acc = jnp.einsum('bhrk,bkhd->brhd', p_space.astype(jnp.bfloat16).astype(jnp.float32), vwin)
        acc = acc + jnp.einsum('bhrg,gbrhd->brhd', p_time.astype(jnp.bfloat16).astype(jnp.float32), v_all)
        attended = (acc / total.transpose(0, 2, 1)[..., None]).astype(jnp.bfloat16).reshape(TOKENS, HEADS * HD)
        eps = x32[frame] + jnp.dot(attended, w_out, preferred_element_type=jnp.float32)
        now = levels[frame]
        later = jnp.maximum(now - LEVELS // FRAMES, 0)
        a_now = alpha_bar(now)
        a_later = alpha_bar(later)
        clean = (x32[frame] - jnp.sqrt(1.0 - a_now) * eps) / jnp.sqrt(a_now)
        results.append((jnp.sqrt(a_later) * clean + jnp.sqrt(1.0 - a_later) * eps).astype(jnp.bfloat16))
    return jnp.stack(results[1:] + [fresh], axis=0)
```

```python
import functools
import math

import jax
import jax.numpy as jnp
from jax import lax
from jax.experimental import pallas as pl
from jax.experimental.pallas import tpu as pltpu
from jax.sharding import PartitionSpec as P

LEVELS = 1000
FRAMES = 8
MESH = pl.DeviceIdType.MESH
VMEM_LIMIT = 56 * 1024 * 1024


def from_behind(array, axis, by):
    count = lax.axis_size(axis)
    pairs = [(i, i + by) for i in range(count) if 0 <= i + by < count]
    return lax.ppermute(array, axis, pairs)


def embed(levels, freq_count):
    half = freq_count // 2
    freqs = jnp.exp(-math.log(10000.0) * jnp.arange(half, dtype=jnp.float32) / half)
    angles = levels.astype(jnp.float32)[:, None] * freqs[None, :]
    return jnp.concatenate([jnp.cos(angles), jnp.sin(angles)], axis=1).astype(jnp.bfloat16)


def alpha_bar(steps):
    frac = steps.astype(jnp.float32) / LEVELS
    return jnp.cos((frac + 0.008) / 1.008 * (math.pi / 2)) ** 2


class Place:
    def __init__(self, space):
        self.space = space
        self.pairs = space // 2
        self.f = lax.axis_index("frame")
        self.s = lax.axis_index("space")
        self.pair = self.s // 2
        self.side = self.s % 2
        core = self.f % 2
        self.f_core = self.f + 1 - 2 * core
        self.f_far = (self.f + 2) % 4
        self.f_diag = (self.f_core + 2) % 4
        self.s_side = self.s + 1 - 2 * self.side

    def pair_at(self, k):
        return lax.rem(self.pair + k, self.pairs)

    def shard_at(self, q):
        return 2 * self.pair_at(q // 2) + lax.rem(self.side + q, 2)


def remote(src, dst, send_sem, recv_sem, device):
    return pltpu.make_async_remote_copy(
        src_ref=src,
        dst_ref=dst,
        send_sem=send_sem,
        recv_sem=recv_sem,
        device_id=device,
        device_id_type=MESH,
    )


def greet(at):
    barrier = pltpu.get_barrier_semaphore()

    def hello(f, s):
        pl.semaphore_signal(barrier, inc=1, device_id=(f, s), device_id_type=MESH)

    for k in range(1, at.pairs):
        hello(at.f, 2 * at.pair_at(k) + at.side)
    hello(at.f, at.s_side)
    hello(at.f_far, at.s)
    hello(at.f_core, at.s)
    pl.semaphore_wait(barrier, at.pairs + 2)


def qkv_kernel(
    space, gain_ref, xm_ref, w_ref, q_ref, kv_ref, xg, wg,
    local_sem, xm_send, xm_recv, send_a, send_r, send_x, send_y, send_c, send_d, recv,
):
    at = Place(space)
    rows = xm_ref.shape[0]
    heads = wg.shape[0]
    frames = q_ref.shape[0]
    block = rows // frames
    hd = q_ref.shape[3]
    f, s, side = at.f, at.s, at.side
    greet(at)

    def direct(k):
        return remote(
            w_ref.at[heads * side + f], wg.at[f, s], send_a.at[k], recv.at[f, s],
            (f, 2 * at.pair_at(k) + side),
        )

    def relay(k):
        return remote(
            wg.at[f, at.s_side], wg.at[f, at.s_side], send_r.at[k], recv.at[f, at.s_side],
            (f, 2 * at.pair_at(k) + side),
        )

    cross = remote(
        w_ref.at[heads * (1 - side) + f], wg.at[f, s], send_x, recv.at[f, s], (f, at.s_side)
    )
    rows_out = remote(xm_ref, xg.at[side], xm_send, xm_recv, (f, at.s_side))

    def to_far(t):
        return remote(wg.at[f, t], wg.at[f, t], send_y.at[t], recv.at[f, t], (at.f_far, s))

    def to_core(t):
        return remote(wg.at[f, t], wg.at[f, t], send_c.at[t], recv.at[f, t], (at.f_core, s))

    def far_to_core(t):
        g = at.f_far
        return remote(wg.at[g, t], wg.at[g, t], send_d.at[t], recv.at[g, t], (at.f_core, s))

    def arrived(g, t):
        remote(wg.at[g, t], wg.at[g, t], send_x, recv.at[g, t], (at.f_core, s)).wait_recv()

    cross.start()
    for k in range(1, at.pairs):
        direct(k).start()
    rows_out.start()
    own = pltpu.make_async_copy(w_ref.at[pl.ds(heads * side, heads)], wg.at[:, s], local_sem.at[0])
    own.start()
    own_rows = pltpu.make_async_copy(xm_ref, xg.at[side], local_sem.at[1])
    own_rows.start()

    def forward(q):
        t = at.shard_at(q)
        arrived(f, t)

        @pl.when(q == 1)
        def _():
            for k in range(1, at.pairs):
                relay(k).start()

        to_far(t).start()
        to_core(t).start()

    def forward_far(q):
        t = at.shard_at(q)
        arrived(at.f_far, t)
        far_to_core(t).start()

    @pl.loop(1, space)
    def _(q):
        forward(q)

        @pl.when(q >= 2)
        def _():
            forward_far(q - 1)

    forward_far(space - 1)

    @pl.loop(1, space)
    def _(q):
        t = at.shard_at(q)
        arrived(at.f_core, t)
        arrived(at.f_diag, t)

    own.wait()
    own_rows.wait()
    remote(xm_ref, xg.at[1 - side], xm_send, xm_recv, (f, at.s_side)).wait_recv()

    @pl.loop(0, heads)
    def _(h):
        gain = gain_ref[heads * side + h]
        w = wg[h].reshape(-1, 3 * hd)
        for x in range(2):
            out = jnp.dot(xg[x], w, preferred_element_type=jnp.float32)
            query = out[:, :hd]
            key = out[:, hd : 2 * hd]
            query = (
                query * lax.rsqrt(jnp.mean(query * query, axis=-1, keepdims=True) + 1e-06) * gain
            )
            key = key * lax.rsqrt(jnp.mean(key * key, axis=-1, keepdims=True) + 1e-06)
            query = query.astype(jnp.bfloat16)
            key = key.astype(jnp.bfloat16)
            value = out[:, 2 * hd :].astype(jnp.bfloat16)
            for i in range(frames):
                part = slice(i * block, (i + 1) * block)
                spot = pl.ds(x * block, block)
                q_ref[i, h, spot, :] = query[part]
                kv_ref[0, i, h, spot, :] = key[part]
                kv_ref[1, i, h, spot, :] = value[part]

    cross.wait_send()
    rows_out.wait_send()
    for k in range(1, at.pairs):
        direct(k).wait_send()
        relay(k).wait_send()

    @pl.loop(1, space)
    def _(q):
        t = at.shard_at(q)
        to_far(t).wait_send()
        to_core(t).wait_send()
        far_to_core(t).wait_send()


def attend_kernel(
    space, coef_ref, q_ref, kv_ref, wo_ref, x_ref, out_ref, win, past, wog, o_own, og,
    local_sem, halo_send, halo_recv, past_send, past_recv, o_send, o_recv,
    send_a, send_x, send_y, send_c, send_d, recv,
):
    at = Place(space)
    frames, heads, tokens, hd = q_ref.shape
    block = tokens // 2
    cols = wog.shape[0]
    f, s, side = at.f, at.s, at.side
    inv = 1.0 / math.sqrt(hd)
    greet(at)

    before = (f, 2 * at.pair_at(at.pairs - 1) + side)
    after = (f, 2 * at.pair_at(1) + side)
    down = remote(
        kv_ref.at[:, :, :, pl.ds(0, block)],
        win.at[:, :, :, pl.ds(3 * block, block)],
        halo_send.at[0], halo_recv.at[0], before,
    )
    up = remote(
        kv_ref.at[:, :, :, pl.ds(block, block)],
        win.at[:, :, :, pl.ds(0, block)],
        halo_send.at[1], halo_recv.at[1], after,
    )
    far = remote(kv_ref, past.at[f], past_send.at[0], past_recv.at[f], (at.f_far, s))
    near = remote(kv_ref, past.at[f], past_send.at[1], past_recv.at[f], (at.f_core, s))
    passed = remote(
        past.at[at.f_far], past.at[at.f_far], past_send.at[2], past_recv.at[at.f_far],
        (at.f_core, s),
    )
    down.start()
    up.start()
    far.start()
    near.start()
    own_win = pltpu.make_async_copy(kv_ref, win.at[:, :, :, pl.ds(block, tokens)], local_sem.at[0])
    own_win.start()
    own_past = pltpu.make_async_copy(kv_ref, past.at[f], local_sem.at[1])
    own_past.start()
    own_wo = pltpu.make_async_copy(wo_ref, wog.at[:, s], local_sem.at[2])
    own_wo.start()

    def direct(k):
        return remote(
            wo_ref.at[f], wog.at[f, s], send_a.at[k], recv.at[f, s],
            (f, 2 * at.pair_at(k) + side),
        )

    def to_side(k):
        t = 2 * at.pair_at(k) + side
        return remote(wog.at[f, t], wog.at[f, t], send_x.at[k], recv.at[f, t], (f, at.s_side))

    def to_far(t):
        return remote(wog.at[f, t], wog.at[f, t], send_y.at[t], recv.at[f, t], (at.f_far, s))

    def to_core(t):
        return remote(wog.at[f, t], wog.at[f, t], send_c.at[t], recv.at[f, t], (at.f_core, s))

    def far_to_core(t):
        g = at.f_far
        return remote(wog.at[g, t], wog.at[g, t], send_d.at[t], recv.at[g, t], (at.f_core, s))

    def arrived(g, t):
        remote(wog.at[g, t], wog.at[g, t], o_send, recv.at[g, t], (at.f_core, s)).wait_recv()

    first = remote(wo_ref.at[f], wog.at[f, s], send_x.at[0], recv.at[f, s], (f, at.s_side))
    first.start()
    for k in range(1, at.pairs):
        direct(k).start()

    @pl.loop(1, space)
    def _(q):
        t = at.shard_at(q)
        arrived(f, t)

        @pl.when(lax.rem(q, 2) == 0)
        def _():
            to_side(q // 2).start()

        to_far(t).start()
        to_core(t).start()

    remote(kv_ref, past.at[at.f_far], o_send, past_recv.at[at.f_far], (at.f_core, s)).wait_recv()
    passed.start()

    @pl.loop(1, space)
    def _(q):
        t = at.shard_at(q)
        arrived(at.f_far, t)
        far_to_core(t).start()

    down.wait_recv()
    up.wait_recv()
    own_win.wait()
    own_past.wait()
    for g in (at.f_core, at.f_diag):
        remote(kv_ref, past.at[g], o_send, past_recv.at[g], (at.f_core, s)).wait_recv()

    lead = lax.broadcasted_iota(jnp.int32, (block, 3 * block), 1)
    back = lax.broadcasted_iota(jnp.int32, (block, 3 * block), 0)
    band = jnp.abs(lead - back - block) <= block

    @pl.loop(0, 2 * frames)
    def _(n):
        i = n // 2
        b = lax.rem(n, 2)
        mine = f * frames + i
        tok = pl.ds(pl.multiple_of(b * block, block), block)
        wide = pl.ds(pl.multiple_of(b * block, block), 3 * block)
        for h in range(heads):
            q = q_ref[i, h, tok, :]
            score = (
                lax.dot_general(
                    q, win[0, i, h, wide, :], (((1,), (1,)), ((), ())),
                    preferred_element_type=jnp.float32,
                )
                * inv
            )
            score = jnp.where(band, score, -1e30)
            top = jnp.max(score, axis=-1, keepdims=True)
            q32 = q.astype(jnp.float32)
            times = []
            for g in range(4 * frames):
                k_g = past[g // frames, 0, g % frames, h, tok, :].astype(jnp.float32)
                t_g = jnp.sum(q32 * k_g, axis=-1, keepdims=True) * inv
                t_g = jnp.where(g < mine, t_g, -1e30)
                top = jnp.maximum(top, t_g)
                times.append(t_g)
            p = jnp.where(band, jnp.exp(score - top), 0.0)
            total = jnp.sum(p, axis=-1, keepdims=True)
            acc = jnp.dot(
                p.astype(jnp.bfloat16), win[1, i, h, wide, :], preferred_element_type=jnp.float32
            )
            for g in range(4 * frames):
                p_g = jnp.where(g < mine, jnp.exp(times[g] - top), 0.0)
                total = total + p_g
                v_g = past[g // frames, 1, g % frames, h, tok, :].astype(jnp.float32)
                acc = acc + p_g.astype(jnp.bfloat16).astype(jnp.float32) * v_g
            o_own[b, i, :, h * hd : (h + 1) * hd] = (acc / total).astype(jnp.bfloat16)

    swap = remote(o_own.at[1 - side], og.at[side], o_send, o_recv, (f, at.s_side))
    swap.start()
    keep = pltpu.make_async_copy(o_own.at[side], og.at[side], local_sem.at[3])
    keep.start()

    @pl.loop(1, space)
    def _(q):
        t = at.shard_at(q)
        arrived(at.f_core, t)
        arrived(at.f_diag, t)

    own_wo.wait()
    keep.wait()
    remote(o_own.at[0], og.at[1 - side], o_send, o_recv, (f, at.s_side)).wait_recv()

    width = wog.shape[3]
    for c in range(cols):
        w = wog[c].reshape(2, heads * hd, width)
        spot = slice(c * width, (c + 1) * width)
        for i in range(frames):
            proj = jnp.dot(og[0, i], w[0], preferred_element_type=jnp.float32)
            proj = proj + jnp.dot(og[1, i], w[1], preferred_element_type=jnp.float32)
            x32 = x_ref[i, :, spot].astype(jnp.float32)
            eps = x32 + proj
            clean = (x32 - coef_ref[i, 0] * eps) / coef_ref[i, 1]
            out_ref[i, :, spot] = (coef_ref[i, 2] * clean + coef_ref[i, 3] * eps).astype(
                jnp.bfloat16
            )

    for copy in (down, up, far, near, passed, first, swap):
        copy.wait_send()
    for k in range(1, at.pairs):
        direct(k).wait_send()
        to_side(k).wait_send()

    @pl.loop(1, space)
    def _(q):
        t = at.shard_at(q)
        to_far(t).wait_send()
        to_core(t).wait_send()
        far_to_core(t).wait_send()


def body(frames_in, levels, fresh, w_mod, w_qkv, q_gain, w_out):
    space = lax.axis_size("space")
    frame_count = lax.axis_size("frame")
    local_frames, rows, width = frames_in.shape
    heads = q_gain.shape[0]
    hd = w_qkv.shape[1] // (3 * heads)
    half = heads // 2
    bf16 = jnp.bfloat16
    vmem = pl.BlockSpec(memory_space=pltpu.VMEM)
    smem = pl.BlockSpec(memory_space=pltpu.SMEM)
    dma = pltpu.SemaphoreType.DMA

    mod = jnp.dot(embed(levels, w_mod.shape[0]), w_mod, preferred_element_type=jnp.float32)
    shift = mod[:, :width]
    scale = mod[:, width:]
    x32 = frames_in.astype(jnp.float32)
    mean = jnp.mean(x32, axis=-1, keepdims=True)
    var = jnp.mean((x32 - mean) ** 2, axis=-1, keepdims=True)
    normed = (x32 - mean) * lax.rsqrt(var + 1e-06)
    xm = (normed * (1.0 + scale[:, None, :]) + shift[:, None, :]).astype(bf16)
    xm = xm.reshape(local_frames * rows, width)

    depth = w_qkv.shape[0]
    w_heads = w_qkv.reshape(depth, 3, heads, hd).transpose(2, 0, 1, 3).reshape(heads, depth, 3 * hd)
    kv_shape = (2, local_frames, half, 2 * rows, hd)
    q, kv = pl.pallas_call(
        functools.partial(qkv_kernel, space),
        out_shape=(
            jax.ShapeDtypeStruct((local_frames, half, 2 * rows, hd), bf16),
            jax.ShapeDtypeStruct(kv_shape, bf16),
        ),
        in_specs=[smem, vmem, vmem],
        out_specs=(vmem, vmem),
        scratch_shapes=[
            pltpu.VMEM((2, local_frames * rows, width), bf16),
            pltpu.VMEM((half, space, depth, 3 * hd), bf16),
            dma((2,)), dma, dma,
            dma((space // 2,)), dma((space // 2,)), dma,
            dma((space,)), dma((space,)), dma((space,)), dma((frame_count, space)),
        ],
        compiler_params=pltpu.CompilerParams(
            collective_id=0, has_side_effects=True, vmem_limit_bytes=VMEM_LIMIT
        ),
        name="qkv",
    )(q_gain, xm, w_heads)

    later = jnp.maximum(levels - LEVELS // FRAMES, 0)
    a_now = alpha_bar(levels)
    a_later = alpha_bar(later)
    coefs = jnp.stack(
        [jnp.sqrt(1.0 - a_now), jnp.sqrt(a_now), jnp.sqrt(a_later), jnp.sqrt(1.0 - a_later)],
        axis=1,
    )
    cols = frame_count
    wo_depth = w_out.shape[0]
    wo = w_out.reshape(wo_depth, cols, width // cols).transpose(1, 0, 2)
    denoised = pl.pallas_call(
        functools.partial(attend_kernel, space),
        out_shape=jax.ShapeDtypeStruct(frames_in.shape, bf16),
        in_specs=[smem, vmem, vmem, vmem, vmem],
        out_specs=vmem,
        scratch_shapes=[
            pltpu.VMEM((2, local_frames, half, 4 * rows, hd), bf16),
            pltpu.VMEM((frame_count,) + kv_shape, bf16),
            pltpu.VMEM((cols, space, wo_depth, width // cols), bf16),
            pltpu.VMEM((2, local_frames, rows, half * hd), bf16),
            pltpu.VMEM((2, local_frames, rows, half * hd), bf16),
            dma((4,)), dma((2,)), dma((2,)), dma((3,)), dma((frame_count,)), dma, dma,
            dma((space // 2,)), dma((space // 2,)),
            dma((space,)), dma((space,)), dma((space,)), dma((frame_count, space)),
        ],
        compiler_params=pltpu.CompilerParams(
            collective_id=1, has_side_effects=True, vmem_limit_bytes=VMEM_LIMIT
        ),
        name="attend",
    )(coefs, q, kv, wo, frames_in)

    arriving = from_behind(denoised[0:1], "frame", -1)
    is_last = lax.axis_index("frame") == frame_count - 1
    tail = jnp.where(is_last, fresh[None], arriving)
    return jnp.concatenate([denoised[1:], tail], axis=0)


def solution(mesh):
    return jax.shard_map(
        body,
        mesh=mesh,
        in_specs=(
            P("frame", "space", None),
            P("frame"),
            P("space", None),
            P(),
            P("space", None),
            P(),
            P("space", None),
        ),
        out_specs=P("frame", "space", None),
        check_vma=False,
    )
```

```python
import functools
import math

import jax
import jax.numpy as jnp
from jax import lax
from jax.experimental import pallas as pl
from jax.experimental.pallas import tpu as pltpu
from jax.sharding import PartitionSpec as P

LEVELS = 1000
FRAMES = 8
MESH = pl.DeviceIdType.MESH
VMEM_LIMIT = 56 * 1024 * 1024


def from_behind(array, axis, by):
    count = lax.axis_size(axis)
    pairs = [(i, i + by) for i in range(count) if 0 <= i + by < count]
    return lax.ppermute(array, axis, pairs)


def embed(levels, freq_count):
    half = freq_count // 2
    freqs = jnp.exp(-math.log(10000.0) * jnp.arange(half, dtype=jnp.float32) / half)
    angles = levels.astype(jnp.float32)[:, None] * freqs[None, :]
    return jnp.concatenate([jnp.cos(angles), jnp.sin(angles)], axis=1).astype(jnp.bfloat16)


def alpha_bar(steps):
    frac = steps.astype(jnp.float32) / LEVELS
    return jnp.cos((frac + 0.008) / 1.008 * (math.pi / 2)) ** 2


class Place:
    def __init__(self, space):
        self.pairs = space // 2
        self.f = lax.axis_index("frame")
        self.s = lax.axis_index("space")
        self.pair = self.s // 2
        self.side = self.s % 2
        core = self.f % 2
        self.f_core = self.f + 1 - 2 * core
        self.f_far = (self.f + 2) % 4
        self.f_diag = (self.f_core + 2) % 4
        self.s_side = self.s + 1 - 2 * self.side

    def beside(self, step):
        return 2 * lax.rem(self.pair + step + self.pairs, self.pairs) + self.side

    def onward(self, way, act):
        if way == 0:
            pl.when(self.pair + 1 < self.pairs)(lambda: act(self.s + 2))
        else:
            pl.when(self.pair >= 1)(lambda: act(self.s - 2))

    def at_distance(self, k, both_sides, act):
        sides = (self.side, 1 - self.side) if both_sides else (self.side,)

        @pl.when(self.pair >= k)
        def _():
            for side in sides:
                act(2 * (self.pair - k) + side, 0)

        @pl.when(self.pair + k < self.pairs)
        def _():
            for side in sides:
                act(2 * (self.pair + k) + side, 1)


def remote(src, dst, send_sem, recv_sem, device):
    return pltpu.make_async_remote_copy(
        src_ref=src,
        dst_ref=dst,
        send_sem=send_sem,
        recv_sem=recv_sem,
        device_id=device,
        device_id_type=MESH,
    )


def step_kernel(
    space, gain_ref, coef_ref, shift_ref, scale_ref, x_ref, w_ref, wo_ref, out_ref,
    xg, wg, wog, win, past, q_own, o_own, og,
    own_w_sem, own_wo_sem, xm_send, xm_recv,
    w_cross, w_chain, w_far, w_core, w_pass, w_recv,
    wo_chain, wo_far, wo_side, wo_core, wo_recv,
    halo_send, halo_recv, past_send, past_recv, o_keep, o_send, o_recv,
):
    at = Place(space)
    frames, rows, width = x_ref.shape
    heads, hd = og.shape[1], og.shape[4]
    inner = 2 * heads * hd
    tokens = 2 * rows
    f, s, side = at.f, at.s, at.side
    inv = 1.0 / math.sqrt(hd)

    barrier = pltpu.get_barrier_semaphore()
    partners = (
        (f, at.beside(1)), (f, at.beside(-1)), (f, at.s_side), (at.f_far, s), (at.f_core, s)
    )
    for partner in partners:
        pl.semaphore_signal(barrier, inc=1, device_id=partner, device_id_type=MESH)
    pl.semaphore_wait(barrier, len(partners))

    def columns(g, head):
        return w_ref.at[:, pl.ds(pl.multiple_of(g * inner + head * hd, hd), hd)]

    def own_w(g, h):
        return pltpu.make_async_copy(
            columns(g, heads * side + h), wg.at[g, h, s], own_w_sem.at[g, h]
        )

    def w_move(g, col, t, sem, device):
        piece = wg.at[g, col, t]
        return remote(piece, piece, sem, w_recv.at[g, col, t], device)

    def w_cross_copy(g):
        return remote(
            columns(g, heads * (1 - side) + f), wg.at[g, f, s], w_cross.at[g],
            w_recv.at[g, f, s], (f, at.s_side),
        )

    def w_first(g, way, to):
        return remote(
            columns(g, heads * side + f), wg.at[g, f, s], w_chain.at[g, s, way],
            w_recv.at[g, f, s], (f, to),
        )

    def w_next(g, t, way, to):
        return w_move(g, f, t, w_chain.at[g, t, way], (f, to))

    def w_to_far(g, t):
        return w_move(g, f, t, w_far.at[g, t], (at.f_far, s))

    def w_to_core(g, t):
        return w_move(g, f, t, w_core.at[g, t], (at.f_core, s))

    def w_passed(g, t):
        return w_move(g, at.f_far, t, w_pass.at[g, t], (at.f_core, s))

    def w_arrived(g, col, t):
        w_move(g, col, t, w_cross.at[g], (at.f_core, s)).wait_recv()

    def w_start(g):
        w_cross_copy(g).start()
        for way in (0, 1):
            at.onward(way, lambda to: w_first(g, way, to).start())
        for h in range(heads):
            own_w(g, h).start()

    def w_share(g, t):
        w_to_far(g, t).start()
        w_to_core(g, t).start()

    def w_spread(g):
        def take(t, way):
            w_arrived(g, f, t)
            at.onward(way, lambda to: w_next(g, t, way, to).start())
            w_share(g, t)

        def take_far(t, way):
            w_arrived(g, at.f_far, t)
            w_passed(g, t).start()

        w_arrived(g, f, at.s_side)
        for way in (0, 1):
            at.onward(way, lambda to: w_next(g, at.s_side, way, to).start())
        w_share(g, at.s_side)

        @pl.loop(1, at.pairs)
        def _(k):
            at.at_distance(k, True, take)

            @pl.when(k == 1)
            def _():
                take_far(at.s_side, 0)

            @pl.when(k >= 2)
            def _():
                at.at_distance(k - 1, True, take_far)

        at.at_distance(at.pairs - 1, True, take_far)

    def others(act):
        @pl.loop(0, space)
        def _(t):
            pl.when(t != s)(lambda: act(t))

    def w_complete(g):
        def both(t):
            w_arrived(g, at.f_core, t)
            w_arrived(g, at.f_diag, t)

        others(both)
        for h in range(heads):
            own_w(g, h).wait()

    def w_finish(g):
        w_cross_copy(g).wait_send()
        for way in (0, 1):
            at.onward(way, lambda to: w_first(g, way, to).wait_send())
            at.onward(way, lambda to: w_next(g, at.s_side, way, to).wait_send())

        def chain(t, way):
            at.onward(way, lambda to: w_next(g, t, way, to).wait_send())

        @pl.loop(1, at.pairs)
        def _(k):
            at.at_distance(k, True, chain)

        def shared(t):
            w_to_far(g, t).wait_send()
            w_to_core(g, t).wait_send()
            w_passed(g, t).wait_send()

        others(shared)

    cols = wog.shape[0]
    part = width // cols

    def wo_block(col):
        return wo_ref.at[:, pl.ds(pl.multiple_of(col * part, part), part)]

    def own_wo(c):
        return pltpu.make_async_copy(wo_block(c), wog.at[c, s], own_wo_sem.at[c])

    def wo_move(col, t, sem, device):
        piece = wog.at[col, t]
        return remote(piece, piece, sem, wo_recv.at[col, t], device)

    def wo_first(way, to):
        return remote(
            wo_block(f), wog.at[f, s], wo_chain.at[s, way], wo_recv.at[f, s], (f, to)
        )

    def wo_own_side(n):
        col = (f, at.f_far)[n]
        return remote(
            wo_block(col), wog.at[col, s], wo_side.at[n, s], wo_recv.at[col, s], (f, at.s_side)
        )

    def wo_next(t, way, to):
        return wo_move(f, t, wo_chain.at[t, way], (f, to))

    def wo_to_far(t):
        return wo_move(f, t, wo_far.at[t], (at.f_far, s))

    def wo_to_side(n, t):
        return wo_move((f, at.f_far)[n], t, wo_side.at[n, t], (f, at.s_side))

    def wo_to_core(n, t):
        return wo_move((f, at.f_far)[n], t, wo_core.at[n, t], (at.f_core, s))

    def wo_arrived(col, t):
        wo_move(col, t, o_keep, (at.f_core, s)).wait_recv()

    def wo_start():
        for way in (0, 1):
            at.onward(way, lambda to: wo_first(way, to).start())
        for n in (0, 1):
            wo_own_side(n).start()
        for c in range(cols):
            own_wo(c).start()

    def wo_spread():
        def take(t, way):
            wo_arrived(f, t)
            at.onward(way, lambda to: wo_next(t, way, to).start())
            wo_to_far(t).start()
            wo_to_side(0, t).start()
            wo_to_core(0, t).start()

        @pl.loop(1, at.pairs)
        def _(k):
            at.at_distance(k, False, take)

    def wo_pass_far():
        def take(t, way):
            wo_arrived(at.f_far, t)
            wo_to_side(1, t).start()
            wo_to_core(1, t).start()

        @pl.loop(1, at.pairs)
        def _(k):
            at.at_distance(k, False, take)

    def wo_pass_side():
        @pl.loop(0, at.pairs)
        def _(p):
            t = 2 * p + 1 - side
            for n in (0, 1):
                wo_arrived((f, at.f_far)[n], t)
                wo_to_core(n, t).start()

    def wo_complete():
        def both(t):
            wo_arrived(at.f_core, t)
            wo_arrived(at.f_diag, t)

        others(both)
        for c in range(cols):
            own_wo(c).wait()

    def wo_finish():
        for way in (0, 1):
            at.onward(way, lambda to: wo_first(way, to).wait_send())
        for n in (0, 1):
            wo_own_side(n).wait_send()

        def chain(t, way):
            at.onward(way, lambda to: wo_next(t, way, to).wait_send())
            wo_to_far(t).wait_send()
            for n in (0, 1):
                wo_to_side(n, t).wait_send()

        @pl.loop(1, at.pairs)
        def _(k):
            at.at_distance(k, False, chain)

        def shared(t):
            for n in (0, 1):
                wo_to_core(n, t).wait_send()

        others(shared)

    def down(h):
        return remote(
            win.at[h, :, :, pl.ds(rows, rows)], win.at[h, :, :, pl.ds(3 * rows, rows)],
            halo_send.at[0, h], halo_recv.at[0, h], (f, at.beside(-1)),
        )

    def up(h):
        return remote(
            win.at[h, :, :, pl.ds(2 * rows, rows)], win.at[h, :, :, pl.ds(0, rows)],
            halo_send.at[1, h], halo_recv.at[1, h], (f, at.beside(1)),
        )

    def past_move(g, h, n, device):
        piece = past.at[g, h]
        return remote(piece, piece, past_send.at[n, h], past_recv.at[g, h], device)

    def past_far(h):
        return past_move(f, h, 0, (at.f_far, s))

    def past_core(h):
        return past_move(f, h, 1, (at.f_core, s))

    def past_passed(h):
        return past_move(at.f_far, h, 2, (at.f_core, s))

    def o_swap(h):
        return remote(
            o_own.at[1 - side, h], og.at[side, h], o_send.at[h], o_recv.at[h], (f, at.s_side)
        )

    w_start(1)
    w_start(2)

    @pl.loop(0, frames * rows // 32)
    def _(n):
        per = rows // 32
        i = n // per
        spot = pl.ds(pl.multiple_of(lax.rem(n, per) * 32, 32), 32)
        x32 = x_ref[i, spot, :].astype(jnp.float32)
        mean = jnp.mean(x32, axis=-1, keepdims=True)
        var = jnp.mean((x32 - mean) ** 2, axis=-1, keepdims=True)
        normed = (x32 - mean) * lax.rsqrt(var + 1e-06)
        xm = normed * (1.0 + scale_ref[pl.ds(i, 1), :]) + shift_ref[pl.ds(i, 1), :]
        xg[side, pl.ds(pl.multiple_of(n * 32, 32), 32), :] = xm.astype(jnp.bfloat16)

    rows_out = remote(xg.at[side], xg.at[side], xm_send, xm_recv, (f, at.s_side))
    rows_out.start()
    w_spread(1)
    w_start(0)
    wo_start()
    w_spread(2)
    w_complete(1)
    w_complete(2)
    remote(xg.at[side], xg.at[1 - side], xm_send, xm_recv, (f, at.s_side)).wait_recv()

    @pl.loop(0, heads)
    def _(h):
        w = jnp.concatenate(
            [wg[1, h].reshape(-1, hd), wg[2, h].reshape(-1, hd)], axis=1
        )
        for x in range(2):
            both = jnp.dot(xg[x], w, preferred_element_type=jnp.float32)
            key = both[:, :hd]
            key = key * lax.rsqrt(jnp.mean(key * key, axis=-1, keepdims=True) + 1e-06)
            key = key.astype(jnp.bfloat16)
            value = both[:, hd:].astype(jnp.bfloat16)
            for i in range(frames):
                own = slice(i * rows, (i + 1) * rows)
                for n, array in ((0, key), (1, value)):
                    win[h, n, i, (1 + x) * rows : (2 + x) * rows, :] = array[own]
                    past[f, h, n, i, x * rows : (x + 1) * rows, :] = array[own]
        down(h).start()
        up(h).start()
        past_far(h).start()
        past_core(h).start()

    w_spread(0)
    wo_spread()
    w_complete(0)

    @pl.loop(0, heads // 2)
    def _(hp):
        w = jnp.concatenate(
            [wg[0, 2 * hp].reshape(-1, hd), wg[0, 2 * hp + 1].reshape(-1, hd)], axis=1
        )
        for x in range(2):
            both = jnp.dot(xg[x], w, preferred_element_type=jnp.float32)
            for n in range(2):
                h = 2 * hp + n
                query = both[:, n * hd : (n + 1) * hd]
                query = (
                    query
                    * lax.rsqrt(jnp.mean(query * query, axis=-1, keepdims=True) + 1e-06)
                    * gain_ref[heads * side + h]
                ).astype(jnp.bfloat16)
                for i in range(frames):
                    q_own[h, i, x * rows : (x + 1) * rows, :] = query[i * rows : (i + 1) * rows]

    lead = lax.broadcasted_iota(jnp.int32, (rows, 3 * rows), 1)
    back = lax.broadcasted_iota(jnp.int32, (rows, 3 * rows), 0)
    band = jnp.abs(lead - back - rows) <= rows
    ones = jnp.ones((2 * hd, hd), jnp.bfloat16)

    @pl.loop(0, heads)
    def _(h):
        remote(
            past.at[f, h], past.at[at.f_far, h], o_keep, past_recv.at[at.f_far, h], (at.f_core, s)
        ).wait_recv()
        past_passed(h).start()
        down(h).wait_recv()
        up(h).wait_recv()
        for g in (at.f_core, at.f_diag):
            remote(
                past.at[f, h], past.at[g, h], o_keep, past_recv.at[g, h], (at.f_core, s)
            ).wait_recv()

        @pl.loop(0, 2 * frames)
        def _(n):
            i = n // 2
            b = lax.rem(n, 2)
            mine = f * frames + i
            tok = pl.ds(pl.multiple_of(b * rows, rows), rows)
            wide = pl.ds(pl.multiple_of(b * rows, rows), 3 * rows)
            q = q_own[h, i, tok, :]
            score = (
                lax.dot_general(
                    q, win[h, 0, i, wide, :], (((1,), (1,)), ((), ())),
                    preferred_element_type=jnp.float32,
                )
                * inv
            )
            score = jnp.where(band, score, -1e30)
            top = jnp.broadcast_to(jnp.max(score, axis=-1, keepdims=True), (rows, hd))
            q32 = q.astype(jnp.float32)
            times = []
            for g in range(4 * frames):
                prod = q32 * past[g // frames, h, 0, g % frames, tok, :].astype(jnp.float32)
                high = prod.astype(jnp.bfloat16)
                low = (prod - high.astype(jnp.float32)).astype(jnp.bfloat16)
                t_g = (
                    jnp.dot(
                        jnp.concatenate([high, low], axis=1), ones,
                        preferred_element_type=jnp.float32,
                    )
                    * inv
                )
                t_g = jnp.where(g < mine, t_g, -1e30)
                top = jnp.maximum(top, t_g)
                times.append(t_g)
            wide_top = jnp.concatenate([top] * (3 * rows // hd), axis=1)
            p = jnp.where(band, jnp.exp(score - wide_top), 0.0)
            total = jnp.sum(p, axis=-1, keepdims=True)
            acc = jnp.dot(
                p.astype(jnp.bfloat16), win[h, 1, i, wide, :], preferred_element_type=jnp.float32
            )
            for g in range(4 * frames):
                p_g = jnp.where(g < mine, jnp.exp(times[g] - top), 0.0)
                total = total + p_g
                v_g = past[g // frames, h, 1, g % frames, tok, :].astype(jnp.float32)
                acc = acc + p_g.astype(jnp.bfloat16).astype(jnp.float32) * v_g
            o_own[b, h, i, :, :] = (acc / total).astype(jnp.bfloat16)

        o_swap(h).start()
        og[side, h] = o_own[side, h]

        @pl.when(h == 0)
        def _():
            wo_pass_far()
            wo_pass_side()

    wo_complete()
    for h in range(heads):
        remote(
            o_own.at[0, h], og.at[1 - side, h], o_keep, o_recv.at[h], (f, at.s_side)
        ).wait_recv()

    for i in range(frames):
        attended = jnp.concatenate(
            [og[x, h, i] for x in range(2) for h in range(heads)], axis=1
        )
        for c in range(cols):
            spot = slice(c * part, (c + 1) * part)
            w = wog[c].reshape(inner, part)
            x32 = x_ref[i, :, spot].astype(jnp.float32)
            eps = x32 + jnp.dot(attended, w, preferred_element_type=jnp.float32)
            clean = (x32 - coef_ref[i, 0] * eps) / coef_ref[i, 1]
            out_ref[i, :, spot] = (coef_ref[i, 2] * clean + coef_ref[i, 3] * eps).astype(
                jnp.bfloat16
            )

    rows_out.wait_send()
    for g in range(3):
        w_finish(g)
    wo_finish()

    @pl.loop(0, heads)
    def _(h):
        for copy in (down(h), up(h), past_far(h), past_core(h), past_passed(h), o_swap(h)):
            copy.wait_send()


def body(frames_in, levels, fresh, w_mod, w_qkv, q_gain, w_out):
    space = lax.axis_size("space")
    groups = lax.axis_size("frame")
    frames, rows, width = frames_in.shape
    heads = q_gain.shape[0]
    hd = w_qkv.shape[1] // (3 * heads)
    half = heads // 2
    bf16 = jnp.bfloat16
    vmem = pl.BlockSpec(memory_space=pltpu.VMEM)
    smem = pl.BlockSpec(memory_space=pltpu.SMEM)
    hbm = pl.BlockSpec(memory_space=pl.ANY)
    dma = pltpu.SemaphoreType.DMA

    mod = jnp.dot(embed(levels, w_mod.shape[0]), w_mod, preferred_element_type=jnp.float32)
    shift = mod[:, :width]
    scale = mod[:, width:]
    later = jnp.maximum(levels - LEVELS // FRAMES, 0)
    a_now = alpha_bar(levels)
    a_later = alpha_bar(later)
    coefs = jnp.stack(
        [jnp.sqrt(1.0 - a_now), jnp.sqrt(a_now), jnp.sqrt(a_later), jnp.sqrt(1.0 - a_later)],
        axis=1,
    )
    depth = w_qkv.shape[0]
    wo_depth = w_out.shape[0]
    denoised = pl.pallas_call(
        functools.partial(step_kernel, space),
        out_shape=jax.ShapeDtypeStruct(frames_in.shape, bf16),
        in_specs=[smem, smem, vmem, vmem, vmem, hbm, hbm],
        out_specs=vmem,
        scratch_shapes=[
            pltpu.VMEM((2, frames * rows, width), bf16),
            pltpu.VMEM((3, half, space, depth, hd), bf16),
            pltpu.VMEM((groups, space, wo_depth, width // groups), bf16),
            pltpu.VMEM((half, 2, frames, 4 * rows, hd), bf16),
            pltpu.VMEM((groups, half, 2, frames, 2 * rows, hd), bf16),
            pltpu.VMEM((half, frames, 2 * rows, hd), bf16),
            pltpu.VMEM((2, half, frames, rows, hd), bf16),
            pltpu.VMEM((2, half, frames, rows, hd), bf16),
            dma((3, half)), dma((groups,)), dma, dma,
            dma((3,)), dma((3, space, 2)), dma((3, space)), dma((3, space)), dma((3, space)),
            dma((3, half, space)),
            dma((space, 2)), dma((space,)), dma((2, space)), dma((2, space)),
            dma((groups, space)),
            dma((2, half)), dma((2, half)), dma((3, half)), dma((groups, half)),
            dma, dma((half,)), dma((half,)),
        ],
        compiler_params=pltpu.CompilerParams(
            collective_id=0, has_side_effects=True, vmem_limit_bytes=VMEM_LIMIT
        ),
        name="step",
    )(q_gain, coefs, shift, scale, frames_in, w_qkv, w_out)

    arriving = from_behind(denoised[0:1], "frame", -1)
    is_last = lax.axis_index("frame") == groups - 1
    tail = jnp.where(is_last, fresh[None], arriving)
    return jnp.concatenate([denoised[1:], tail], axis=0)


def solution(mesh):
    return jax.shard_map(
        body,
        mesh=mesh,
        in_specs=(
            P("frame", "space", None),
            P("frame"),
            P("space", None),
            P(),
            P("space", None),
            P(),
            P("space", None),
        ),
        out_specs=P("frame", "space", None),
        check_vma=False,
    )
```

```python
import functools
import math

import jax
import jax.numpy as jnp
from jax import lax
from jax.experimental import pallas as pl
from jax.experimental.pallas import tpu as pltpu
from jax.sharding import PartitionSpec as P

LEVELS = 1000
FRAMES = 8
MESH = pl.DeviceIdType.MESH
VMEM_LIMIT = 56 * 1024 * 1024


def embed(levels, freq_count):
    half = freq_count // 2
    freqs = jnp.exp(-math.log(10000.0) * jnp.arange(half, dtype=jnp.float32) / half)
    angles = levels.astype(jnp.float32)[:, None] * freqs[None, :]
    return jnp.concatenate([jnp.cos(angles), jnp.sin(angles)], axis=1).astype(jnp.bfloat16)


def alpha_bar(steps):
    frac = steps.astype(jnp.float32) / LEVELS
    return jnp.cos((frac + 0.008) / 1.008 * (math.pi / 2)) ** 2


class Place:
    def __init__(self, space):
        self.pairs = space // 2
        self.f = lax.axis_index("frame")
        self.s = lax.axis_index("space")
        self.pair = self.s // 2
        self.side = self.s % 2
        core = self.f % 2
        self.f_core = self.f + 1 - 2 * core
        self.f_far = (self.f + 2) % 4
        self.f_diag = (self.f_core + 2) % 4
        self.s_side = self.s + 1 - 2 * self.side

    def beside(self, step):
        return 2 * lax.rem(self.pair + step + self.pairs, self.pairs) + self.side

    def onward(self, way, act):
        if way == 0:
            pl.when(self.pair + 1 < self.pairs)(lambda: act(self.s + 2))
        else:
            pl.when(self.pair >= 1)(lambda: act(self.s - 2))

    def at_distance(self, k, both_sides, act):
        sides = (self.side, 1 - self.side) if both_sides else (self.side,)

        @pl.when(self.pair >= k)
        def _():
            for side in sides:
                act(2 * (self.pair - k) + side, 0)

        @pl.when(self.pair + k < self.pairs)
        def _():
            for side in sides:
                act(2 * (self.pair + k) + side, 1)


def remote(src, dst, send_sem, recv_sem, device):
    return pltpu.make_async_remote_copy(
        src_ref=src,
        dst_ref=dst,
        send_sem=send_sem,
        recv_sem=recv_sem,
        device_id=device,
        device_id_type=MESH,
    )


def step_kernel(
    space, gain_ref, coef_ref, emb_ref, x_ref, fresh_ref, w_ref, wo_ref, w_mod_ref, out_ref,
    xg, wg, wog, win, past, q_own, o_own, og, mod, w_mod_own, leaving, arriving,
    own_w_sem, own_wo_sem, xm_send, xm_recv,
    w_cross, w_chain, w_far, w_core, w_pass, w_recv,
    wo_chain, wo_far, wo_side, wo_core, wo_recv,
    halo_send, halo_recv, past_send, past_recv, o_keep, o_send, o_recv,
    mod_sem, leave_send, leave_recv,
):
    at = Place(space)
    frames, rows, width = x_ref.shape
    heads, hd = og.shape[1], og.shape[4]
    inner = 2 * heads * hd
    tokens = 2 * rows
    f, s, side = at.f, at.s, at.side
    inv = 1.0 / math.sqrt(hd)

    barrier = pltpu.get_barrier_semaphore()
    partners = (
        (f, at.beside(1)), (f, at.beside(-1)), (f, at.s_side), (at.f_far, s), (at.f_core, s),
        (at.f_diag, s),
    )
    for partner in partners:
        pl.semaphore_signal(barrier, inc=1, device_id=partner, device_id_type=MESH)
    pl.semaphore_wait(barrier, len(partners))

    def columns(g, head):
        return w_ref.at[:, pl.ds(pl.multiple_of(g * inner + head * hd, hd), hd)]

    def own_w(g, h):
        return pltpu.make_async_copy(
            columns(g, heads * side + h), wg.at[g, h, s], own_w_sem.at[g, h]
        )

    def w_move(g, col, t, sem, device):
        piece = wg.at[g, col, t]
        return remote(piece, piece, sem, w_recv.at[g, col, t], device)

    def w_cross_copy(g):
        return remote(
            columns(g, heads * (1 - side) + f), wg.at[g, f, s], w_cross.at[g],
            w_recv.at[g, f, s], (f, at.s_side),
        )

    def w_first(g, way, to):
        return remote(
            columns(g, heads * side + f), wg.at[g, f, s], w_chain.at[g, s, way],
            w_recv.at[g, f, s], (f, to),
        )

    def w_next(g, t, way, to):
        return w_move(g, f, t, w_chain.at[g, t, way], (f, to))

    def w_to_far(g, t):
        return w_move(g, f, t, w_far.at[g, t], (at.f_far, s))

    def w_to_core(g, t):
        return w_move(g, f, t, w_core.at[g, t], (at.f_core, s))

    def w_passed(g, t):
        return w_move(g, at.f_far, t, w_pass.at[g, t], (at.f_core, s))

    def w_arrived(g, col, t):
        w_move(g, col, t, w_cross.at[g], (at.f_core, s)).wait_recv()

    def w_start(g):
        for way in (0, 1):
            at.onward(way, lambda to: w_first(g, way, to).start())
        for h in range(heads):
            own_w(g, h).start()

    def w_share(g, t):
        w_to_far(g, t).start()
        w_to_core(g, t).start()

    def w_spread(g):
        def take(t, way):
            w_arrived(g, f, t)
            at.onward(way, lambda to: w_next(g, t, way, to).start())
            w_share(g, t)

        def take_far(t, way):
            w_arrived(g, at.f_far, t)
            w_passed(g, t).start()

        w_arrived(g, f, at.s_side)
        for way in (0, 1):
            at.onward(way, lambda to: w_next(g, at.s_side, way, to).start())
        w_share(g, at.s_side)

        @pl.loop(1, at.pairs)
        def _(k):
            at.at_distance(k, True, take)

            @pl.when(k == 1)
            def _():
                take_far(at.s_side, 0)

            @pl.when(k >= 2)
            def _():
                at.at_distance(k - 1, True, take_far)

        at.at_distance(at.pairs - 1, True, take_far)

    def others(act):
        @pl.loop(0, space)
        def _(t):
            pl.when(t != s)(lambda: act(t))

    def w_complete(g):
        def both(t):
            w_arrived(g, at.f_core, t)
            w_arrived(g, at.f_diag, t)

        others(both)
        for h in range(heads):
            own_w(g, h).wait()

    def w_finish(g):
        w_cross_copy(g).wait_send()
        for way in (0, 1):
            at.onward(way, lambda to: w_first(g, way, to).wait_send())
            at.onward(way, lambda to: w_next(g, at.s_side, way, to).wait_send())

        def chain(t, way):
            at.onward(way, lambda to: w_next(g, t, way, to).wait_send())

        @pl.loop(1, at.pairs)
        def _(k):
            at.at_distance(k, True, chain)

        def shared(t):
            w_to_far(g, t).wait_send()
            w_to_core(g, t).wait_send()
            w_passed(g, t).wait_send()

        others(shared)

    cols = wog.shape[0]
    part = width // cols

    def wo_block(col):
        return wo_ref.at[:, pl.ds(pl.multiple_of(col * part, part), part)]

    def own_wo(c):
        return pltpu.make_async_copy(wo_block(c), wog.at[c, s], own_wo_sem.at[c])

    def wo_move(col, t, sem, device):
        piece = wog.at[col, t]
        return remote(piece, piece, sem, wo_recv.at[col, t], device)

    def wo_first(way, to):
        return remote(
            wo_block(f), wog.at[f, s], wo_chain.at[s, way], wo_recv.at[f, s], (f, to)
        )

    def wo_own_side(n):
        col = (f, at.f_far)[n]
        return remote(
            wo_block(col), wog.at[col, s], wo_side.at[n, s], wo_recv.at[col, s], (f, at.s_side)
        )

    def wo_next(t, way, to):
        return wo_move(f, t, wo_chain.at[t, way], (f, to))

    def wo_to_far(t):
        return wo_move(f, t, wo_far.at[t], (at.f_far, s))

    def wo_to_side(n, t):
        return wo_move((f, at.f_far)[n], t, wo_side.at[n, t], (f, at.s_side))

    def wo_to_core(n, t):
        return wo_move((f, at.f_far)[n], t, wo_core.at[n, t], (at.f_core, s))

    def wo_arrived(col, t):
        wo_move(col, t, o_keep, (at.f_core, s)).wait_recv()

    def wo_start():
        for way in (0, 1):
            at.onward(way, lambda to: wo_first(way, to).start())
        for n in (0, 1):
            wo_own_side(n).start()
        for c in range(cols):
            own_wo(c).start()

    def wo_spread():
        def take(t, way):
            wo_arrived(f, t)
            at.onward(way, lambda to: wo_next(t, way, to).start())
            wo_to_far(t).start()
            wo_to_side(0, t).start()
            wo_to_core(0, t).start()

        @pl.loop(1, at.pairs)
        def _(k):
            at.at_distance(k, False, take)

    def wo_pass_far():
        def take(t, way):
            wo_arrived(at.f_far, t)
            wo_to_side(1, t).start()
            wo_to_core(1, t).start()

        @pl.loop(1, at.pairs)
        def _(k):
            at.at_distance(k, False, take)

    def wo_pass_side():
        @pl.loop(0, at.pairs)
        def _(p):
            t = 2 * p + 1 - side
            for n in (0, 1):
                wo_arrived((f, at.f_far)[n], t)
                wo_to_core(n, t).start()

    def wo_complete():
        def both(t):
            wo_arrived(at.f_core, t)
            wo_arrived(at.f_diag, t)

        others(both)
        for c in range(cols):
            own_wo(c).wait()

    def wo_finish():
        for way in (0, 1):
            at.onward(way, lambda to: wo_first(way, to).wait_send())
        for n in (0, 1):
            wo_own_side(n).wait_send()

        def chain(t, way):
            at.onward(way, lambda to: wo_next(t, way, to).wait_send())
            wo_to_far(t).wait_send()
            for n in (0, 1):
                wo_to_side(n, t).wait_send()

        @pl.loop(1, at.pairs)
        def _(k):
            at.at_distance(k, False, chain)

        def shared(t):
            for n in (0, 1):
                wo_to_core(n, t).wait_send()

        others(shared)

    def down(h):
        return remote(
            win.at[h, :, :, pl.ds(rows, rows)], win.at[h, :, :, pl.ds(3 * rows, rows)],
            halo_send.at[0, h], halo_recv.at[0, h], (f, at.beside(-1)),
        )

    def up(h):
        return remote(
            win.at[h, :, :, pl.ds(2 * rows, rows)], win.at[h, :, :, pl.ds(0, rows)],
            halo_send.at[1, h], halo_recv.at[1, h], (f, at.beside(1)),
        )

    def past_move(g, h, x, n, device):
        piece = past.at[g, h, x]
        return remote(piece, piece, past_send.at[n, h, x], past_recv.at[g, h, x], device)

    def past_far(h, x):
        return past_move(f, h, x, 0, (at.f_far, s))

    def past_core(h, x):
        return past_move(f, h, x, 1, (at.f_core, s))

    def past_passed(h, x):
        return past_move(at.f_far, h, x, 2, (at.f_core, s))

    def past_arrived(g, h, x):
        piece = past.at[g, h, x]
        remote(piece, piece, o_keep, past_recv.at[g, h, x], (at.f_core, s)).wait_recv()

    def leave(c):
        return remote(
            leaving.at[c], arriving.at[c], leave_send.at[c], leave_recv.at[c],
            (lax.rem(f + 3, 4), s),
        )

    def o_swap(h):
        return remote(
            o_own.at[1 - side, h], og.at[side, h], o_send.at[h], o_recv.at[h], (f, at.s_side)
        )

    for g in (1, 2, 0):
        w_cross_copy(g).start()
    w_start(1)
    w_start(2)
    fetch = pltpu.make_async_copy(w_mod_ref, w_mod_own, mod_sem)
    fetch.start()
    fetch.wait()
    for c in range(0, 2 * width, width // 2):
        mod[:, c : c + width // 2] = jnp.dot(
            emb_ref[...], w_mod_own[:, c : c + width // 2], preferred_element_type=jnp.float32
        )

    @pl.loop(0, frames * rows // 32)
    def _(n):
        per = rows // 32
        i = n // per
        spot = pl.ds(pl.multiple_of(lax.rem(n, per) * 32, 32), 32)
        x32 = x_ref[i, spot, :].astype(jnp.float32)
        mean = jnp.mean(x32, axis=-1, keepdims=True)
        var = jnp.mean((x32 - mean) ** 2, axis=-1, keepdims=True)
        normed = (x32 - mean) * lax.rsqrt(var + 1e-06)
        xm = normed * (1.0 + mod[pl.ds(i, 1), width:]) + mod[pl.ds(i, 1), :width]
        xg[side, pl.ds(pl.multiple_of(n * 32, 32), 32), :] = xm.astype(jnp.bfloat16)

    rows_out = remote(xg.at[side], xg.at[side], xm_send, xm_recv, (f, at.s_side))
    rows_out.start()
    w_spread(1)
    w_start(0)
    w_spread(2)
    wo_start()
    w_complete(1)
    w_complete(2)

    def keys_values(x):
        @pl.loop(0, heads)
        def _(h):
            w = jnp.concatenate([wg[1, h].reshape(-1, hd), wg[2, h].reshape(-1, hd)], axis=1)
            both = jnp.dot(xg[x], w, preferred_element_type=jnp.float32)
            key = both[:, :hd]
            key = key * lax.rsqrt(jnp.mean(key * key, axis=-1, keepdims=True) + 1e-06)
            key = key.astype(jnp.bfloat16)
            value = both[:, hd:].astype(jnp.bfloat16)
            spot = pl.ds(pl.multiple_of((1 + x) * rows, rows), rows)
            for i in range(frames):
                own = slice(i * rows, (i + 1) * rows)
                for n, array in ((0, key), (1, value)):
                    win[h, n, i, spot, :] = array[own]
                    past[f, h, x, n, i] = array[own]
            pl.when(x == 0)(lambda: down(h).start())
            pl.when(x == 1)(lambda: up(h).start())
            past_far(h, x).start()
            past_core(h, x).start()

    keys_values(side)
    w_spread(0)
    remote(xg.at[side], xg.at[1 - side], xm_send, xm_recv, (f, at.s_side)).wait_recv()
    keys_values(1 - side)
    wo_spread()
    w_complete(0)

    @pl.loop(0, heads // 2)
    def _(hp):
        w = jnp.concatenate(
            [wg[0, 2 * hp].reshape(-1, hd), wg[0, 2 * hp + 1].reshape(-1, hd)], axis=1
        )
        for x in range(2):
            both = jnp.dot(xg[x], w, preferred_element_type=jnp.float32)
            for n in range(2):
                h = 2 * hp + n
                query = both[:, n * hd : (n + 1) * hd]
                query = (
                    query
                    * lax.rsqrt(jnp.mean(query * query, axis=-1, keepdims=True) + 1e-06)
                    * gain_ref[heads * side + h]
                ).astype(jnp.bfloat16)
                for i in range(frames):
                    q_own[h, i, x * rows : (x + 1) * rows, :] = query[i * rows : (i + 1) * rows]

    lead = lax.broadcasted_iota(jnp.int32, (rows, 3 * rows), 1)
    back = lax.broadcasted_iota(jnp.int32, (rows, 3 * rows), 0)
    band = jnp.abs(lead - back - rows) <= rows
    ones = jnp.ones((2 * hd, hd), jnp.bfloat16)

    @pl.loop(0, heads)
    def _(h):
        for x in range(2):
            past_arrived(at.f_far, h, x)
            past_passed(h, x).start()
        down(h).wait_recv()
        up(h).wait_recv()
        for g in (at.f_core, at.f_diag):
            for x in range(2):
                past_arrived(g, h, x)

        @pl.loop(0, 2 * frames)
        def _(n):
            i = lax.rem(n, frames)
            b = lax.rem(n // frames + 1 - side, 2)
            mine = f * frames + i
            tok = pl.ds(pl.multiple_of(b * rows, rows), rows)
            wide = pl.ds(pl.multiple_of(b * rows, rows), 3 * rows)
            q = q_own[h, i, tok, :]
            score = (
                lax.dot_general(
                    q, win[h, 0, i, wide, :], (((1,), (1,)), ((), ())),
                    preferred_element_type=jnp.float32,
                )
                * inv
            )
            score = jnp.where(band, score, -1e30)
            top = jnp.broadcast_to(jnp.max(score, axis=-1, keepdims=True), (rows, hd))
            q32 = q.astype(jnp.float32)
            times = []
            for g in range(4 * frames):
                prod = q32 * past[g // frames, h, b, 0, g % frames].astype(jnp.float32)
                high = prod.astype(jnp.bfloat16)
                low = (prod - high.astype(jnp.float32)).astype(jnp.bfloat16)
                t_g = (
                    jnp.dot(
                        jnp.concatenate([high, low], axis=1), ones,
                        preferred_element_type=jnp.float32,
                    )
                    * inv
                )
                t_g = jnp.where(g < mine, t_g, -1e30)
                top = jnp.maximum(top, t_g)
                times.append(t_g)
            wide_top = jnp.concatenate([top] * (3 * rows // hd), axis=1)
            p = jnp.where(band, jnp.exp(score - wide_top), 0.0)
            total = jnp.sum(p, axis=-1, keepdims=True)
            acc = jnp.dot(
                p.astype(jnp.bfloat16), win[h, 1, i, wide, :], preferred_element_type=jnp.float32
            )
            for g in range(4 * frames):
                p_g = jnp.where(g < mine, jnp.exp(times[g] - top), 0.0)
                total = total + p_g
                v_g = past[g // frames, h, b, 1, g % frames].astype(jnp.float32)
                acc = acc + p_g.astype(jnp.bfloat16).astype(jnp.float32) * v_g
            o_own[b, h, i, :, :] = (acc / total).astype(jnp.bfloat16)

            @pl.when(n == frames - 1)
            def _():
                o_swap(h).start()

        og[side, h] = o_own[side, h]

        @pl.when(h == 0)
        def _():
            wo_pass_far()
            wo_pass_side()

    wo_complete()
    for h in range(heads):
        remote(
            o_own.at[0, h], og.at[1 - side, h], o_keep, o_recv.at[h], (f, at.s_side)
        ).wait_recv()

    attended = jnp.concatenate(
        [og[x, h].reshape(frames * rows, hd) for x in range(2) for h in range(heads)], axis=1
    )
    for c in range(cols):
        spot = slice(c * part, (c + 1) * part)
        w = wog[c].reshape(inner, part)
        proj = jnp.dot(attended, w, preferred_element_type=jnp.float32)
        for i in range(frames):
            x32 = x_ref[i, :, spot].astype(jnp.float32)
            eps = x32 + proj[i * rows : (i + 1) * rows]
            clean = (x32 - coef_ref[0, i] * eps) / coef_ref[1, i]
            done = (coef_ref[2, i] * clean + coef_ref[3, i] * eps).astype(jnp.bfloat16)
            if i == 0:
                leaving[c] = done
                leave(c).start()
            else:
                out_ref[i - 1, :, spot] = done

    @pl.when(f == 3)
    def _():
        out_ref[frames - 1] = fresh_ref[...]

    for c in range(cols):
        leave(c).wait_recv()

        @pl.when(f != 3)
        def _():
            out_ref[frames - 1, :, c * part : (c + 1) * part] = arriving[c]

    for c in range(cols):
        leave(c).wait_send()
    rows_out.wait_send()
    for g in range(3):
        w_finish(g)
    wo_finish()

    @pl.loop(0, heads)
    def _(h):
        for copy in (down(h), up(h), o_swap(h)):
            copy.wait_send()
        for x in range(2):
            for copy in (past_far(h, x), past_core(h, x), past_passed(h, x)):
                copy.wait_send()


def body(frames_in, levels, fresh, w_mod, w_qkv, q_gain, w_out):
    space = lax.axis_size("space")
    groups = lax.axis_size("frame")
    frames, rows, width = frames_in.shape
    heads = q_gain.shape[0]
    hd = w_qkv.shape[1] // (3 * heads)
    half = heads // 2
    bf16 = jnp.bfloat16
    vmem = pl.BlockSpec(memory_space=pltpu.VMEM)
    smem = pl.BlockSpec(memory_space=pltpu.SMEM)
    hbm = pl.BlockSpec(memory_space=pl.ANY)
    dma = pltpu.SemaphoreType.DMA

    emb = embed(levels, w_mod.shape[0])
    emb = jnp.pad(emb, ((0, 16 - frames), (0, 0)))
    later = jnp.maximum(levels - LEVELS // FRAMES, 0)
    a_now = alpha_bar(levels)
    a_later = alpha_bar(later)
    coefs = jnp.stack(
        [jnp.sqrt(1.0 - a_now), jnp.sqrt(a_now), jnp.sqrt(a_later), jnp.sqrt(1.0 - a_later)]
    )
    depth = w_qkv.shape[0]
    wo_depth = w_out.shape[0]
    return pl.pallas_call(
        functools.partial(step_kernel, space),
        out_shape=jax.ShapeDtypeStruct(frames_in.shape, bf16),
        in_specs=[smem, smem, vmem, vmem, vmem, hbm, hbm, hbm],
        out_specs=vmem,
        scratch_shapes=[
            pltpu.VMEM((2, frames * rows, width), bf16),
            pltpu.VMEM((3, half, space, depth, hd), bf16),
            pltpu.VMEM((groups, space, wo_depth, width // groups), bf16),
            pltpu.VMEM((half, 2, frames, 4 * rows, hd), bf16),
            pltpu.VMEM((groups, half, 2, 2, frames, rows, hd), bf16),
            pltpu.VMEM((half, frames, 2 * rows, hd), bf16),
            pltpu.VMEM((2, half, frames, rows, hd), bf16),
            pltpu.VMEM((2, half, frames, rows, hd), bf16),
            pltpu.VMEM((16, 2 * width), jnp.float32),
            pltpu.VMEM(w_mod.shape, bf16),
            pltpu.VMEM((groups, rows, width // groups), bf16),
            pltpu.VMEM((groups, rows, width // groups), bf16),
            dma((3, half)), dma((groups,)), dma, dma,
            dma((3,)), dma((3, space, 2)), dma((3, space)), dma((3, space)), dma((3, space)),
            dma((3, half, space)),
            dma((space, 2)), dma((space,)), dma((2, space)), dma((2, space)),
            dma((groups, space)),
            dma((2, half)), dma((2, half)), dma((3, half, 2)), dma((groups, half, 2)),
            dma, dma((half,)), dma((half,)), dma, dma((groups,)), dma((groups,)),
        ],
        compiler_params=pltpu.CompilerParams(
            collective_id=0, has_side_effects=True, vmem_limit_bytes=VMEM_LIMIT
        ),
        name="step",
    )(q_gain, coefs, emb, frames_in, fresh, w_qkv, w_out, w_mod)


def solution(mesh):
    return jax.shard_map(
        body,
        mesh=mesh,
        in_specs=(
            P("frame", "space", None),
            P("frame"),
            P("space", None),
            P(),
            P("space", None),
            P(),
            P("space", None),
        ),
        out_specs=P("frame", "space", None),
        check_vma=False,
    )
```

```python
import functools
import math

import jax
import jax.numpy as jnp
from jax import lax
from jax.experimental import pallas as pl
from jax.experimental.pallas import tpu as pltpu
from jax.sharding import PartitionSpec as P

LEVELS = 1000
FRAMES = 8
MESH = pl.DeviceIdType.MESH
VMEM_LIMIT = 56 * 1024 * 1024


def embed(levels, freq_count):
    half = freq_count // 2
    freqs = jnp.exp(-math.log(10000.0) * jnp.arange(half, dtype=jnp.float32) / half)
    angles = levels.astype(jnp.float32)[:, None] * freqs[None, :]
    return jnp.concatenate([jnp.cos(angles), jnp.sin(angles)], axis=1).astype(jnp.bfloat16)


def alpha_bar(steps):
    frac = steps.astype(jnp.float32) / LEVELS
    return jnp.cos((frac + 0.008) / 1.008 * (math.pi / 2)) ** 2


class Place:
    def __init__(self, space):
        self.pairs = space // 2
        self.f = lax.axis_index("frame")
        self.s = lax.axis_index("space")
        self.pair = self.s // 2
        self.side = self.s % 2
        core = self.f % 2
        self.f_core = self.f + 1 - 2 * core
        self.f_far = (self.f + 2) % 4
        self.f_diag = (self.f_core + 2) % 4
        self.s_side = self.s + 1 - 2 * self.side

    def beside(self, step):
        return 2 * lax.rem(self.pair + step + self.pairs, self.pairs) + self.side

    def onward(self, way, act):
        if way == 0:
            pl.when(self.pair + 1 < self.pairs)(lambda: act(self.s + 2))
        else:
            pl.when(self.pair >= 1)(lambda: act(self.s - 2))

    def at_distance(self, k, both_sides, act):
        sides = (self.side, 1 - self.side) if both_sides else (self.side,)

        @pl.when(self.pair >= k)
        def _():
            for side in sides:
                act(2 * (self.pair - k) + side, 0)

        @pl.when(self.pair + k < self.pairs)
        def _():
            for side in sides:
                act(2 * (self.pair + k) + side, 1)


def remote(src, dst, send_sem, recv_sem, device):
    return pltpu.make_async_remote_copy(
        src_ref=src,
        dst_ref=dst,
        send_sem=send_sem,
        recv_sem=recv_sem,
        device_id=device,
        device_id_type=MESH,
    )


def step_kernel(
    space, gain_ref, coef_ref, emb_ref, x_ref, fresh_ref, w_ref, wo_ref, w_mod_ref, out_ref,
    xg, wg, wog, win, past, q_own, o_own, og, mod, w_mod_own, leaving, arriving,
    own_w_sem, own_wo_sem, xm_send, xm_recv,
    w_cross, w_chain, w_far, w_core, w_pass, w_recv,
    wo_chain, wo_far, wo_side, wo_core, wo_recv,
    halo_send, halo_recv, past_send, past_recv, o_keep, o_send, o_recv,
    mod_sem, leave_send, leave_recv,
):
    at = Place(space)
    frames, rows, width = x_ref.shape
    heads, hd = og.shape[1], og.shape[4]
    groups = wog.shape[0]
    assert rows == hd
    inner = 2 * heads * hd
    tokens = 2 * rows
    f, s, side = at.f, at.s, at.side
    inv = 1.0 / math.sqrt(hd)

    barrier = pltpu.get_barrier_semaphore()
    partners = (
        (f, at.beside(1)), (f, at.beside(-1)), (f, at.s_side), (at.f_far, s), (at.f_core, s),
        (at.f_diag, s),
    )
    for partner in partners:
        pl.semaphore_signal(barrier, inc=1, device_id=partner, device_id_type=MESH)
    pl.semaphore_wait(barrier, len(partners))

    def columns(g, head):
        return w_ref.at[:, pl.ds(pl.multiple_of(g * inner + head * hd, hd), hd)]

    def own_w(g, h):
        return pltpu.make_async_copy(
            columns(g, heads * side + h), wg.at[g, h, s], own_w_sem.at[g, h]
        )

    def w_move(g, col, t, sem, device):
        piece = wg.at[g, col, t]
        return remote(piece, piece, sem, w_recv.at[g, col, t], device)

    def w_cross_copy(g):
        return remote(
            columns(g, heads * (1 - side) + f), wg.at[g, f, s], w_cross.at[g],
            w_recv.at[g, f, s], (f, at.s_side),
        )

    def w_first(g, way, to):
        return remote(
            columns(g, heads * side + f), wg.at[g, f, s], w_chain.at[g, s, way],
            w_recv.at[g, f, s], (f, to),
        )

    def w_next(g, t, way, to):
        return w_move(g, f, t, w_chain.at[g, t, way], (f, to))

    def w_to_far(g, t):
        return w_move(g, f, t, w_far.at[g, t], (at.f_far, s))

    def w_to_core(g, t):
        return w_move(g, f, t, w_core.at[g, t], (at.f_core, s))

    def w_passed(g, t):
        return w_move(g, at.f_far, t, w_pass.at[g, t], (at.f_core, s))

    def w_arrived(g, col, t):
        w_move(g, col, t, w_cross.at[g], (at.f_core, s)).wait_recv()

    def w_start(g):
        for way in (0, 1):
            at.onward(way, lambda to: w_first(g, way, to).start())
        for h in range(heads):
            own_w(g, h).start()

    def w_share(g, t):
        w_to_far(g, t).start()
        w_to_core(g, t).start()

    def w_spread(g):
        def take(t, way):
            w_arrived(g, f, t)
            at.onward(way, lambda to: w_next(g, t, way, to).start())
            w_share(g, t)

        def take_far(t, way):
            w_arrived(g, at.f_far, t)
            w_passed(g, t).start()

        w_arrived(g, f, at.s_side)
        for way in (0, 1):
            at.onward(way, lambda to: w_next(g, at.s_side, way, to).start())
        w_share(g, at.s_side)

        @pl.loop(1, at.pairs)
        def _(k):
            at.at_distance(k, True, take)

            @pl.when(k == 1)
            def _():
                take_far(at.s_side, 0)

            @pl.when(k >= 2)
            def _():
                at.at_distance(k - 1, True, take_far)

        at.at_distance(at.pairs - 1, True, take_far)

    def others(act):
        @pl.loop(0, space)
        def _(t):
            pl.when(t != s)(lambda: act(t))

    def w_complete(g):
        def both(t):
            w_arrived(g, at.f_core, t)
            w_arrived(g, at.f_diag, t)

        others(both)
        for h in range(heads):
            own_w(g, h).wait()

    def w_finish(g):
        w_cross_copy(g).wait_send()
        for way in (0, 1):
            at.onward(way, lambda to: w_first(g, way, to).wait_send())
            at.onward(way, lambda to: w_next(g, at.s_side, way, to).wait_send())

        def chain(t, way):
            at.onward(way, lambda to: w_next(g, t, way, to).wait_send())

        @pl.loop(1, at.pairs)
        def _(k):
            at.at_distance(k, True, chain)

        def shared(t):
            w_to_far(g, t).wait_send()
            w_to_core(g, t).wait_send()
            w_passed(g, t).wait_send()

        others(shared)

    cols = wog.shape[0]
    part = width // cols

    def wo_block(col):
        return wo_ref.at[:, pl.ds(pl.multiple_of(col * part, part), part)]

    def own_wo(c):
        return pltpu.make_async_copy(wo_block(c), wog.at[c, s], own_wo_sem.at[c])

    def wo_move(col, t, sem, device):
        piece = wog.at[col, t]
        return remote(piece, piece, sem, wo_recv.at[col, t], device)

    def wo_first(way, to):
        return remote(
            wo_block(f), wog.at[f, s], wo_chain.at[s, way], wo_recv.at[f, s], (f, to)
        )

    def wo_own_side(n):
        col = (f, at.f_far)[n]
        return remote(
            wo_block(col), wog.at[col, s], wo_side.at[n, s], wo_recv.at[col, s], (f, at.s_side)
        )

    def wo_next(t, way, to):
        return wo_move(f, t, wo_chain.at[t, way], (f, to))

    def wo_to_far(t):
        return wo_move(f, t, wo_far.at[t], (at.f_far, s))

    def wo_to_side(n, t):
        return wo_move((f, at.f_far)[n], t, wo_side.at[n, t], (f, at.s_side))

    def wo_to_core(n, t):
        return wo_move((f, at.f_far)[n], t, wo_core.at[n, t], (at.f_core, s))

    def wo_arrived(col, t):
        wo_move(col, t, o_keep, (at.f_core, s)).wait_recv()

    def wo_start():
        for way in (0, 1):
            at.onward(way, lambda to: wo_first(way, to).start())
        for n in (0, 1):
            wo_own_side(n).start()
        for c in range(cols):
            own_wo(c).start()

    def wo_spread(k):
        def take(t, way):
            wo_arrived(f, t)
            at.onward(way, lambda to: wo_next(t, way, to).start())
            wo_to_far(t).start()
            wo_to_side(0, t).start()
            wo_to_core(0, t).start()

        at.at_distance(k, False, take)

    def wo_pass_far(k):
        def take(t, way):
            wo_arrived(at.f_far, t)
            wo_to_side(1, t).start()
            wo_to_core(1, t).start()

        at.at_distance(k, False, take)

    def wo_pass_side():
        @pl.loop(0, at.pairs)
        def _(p):
            t = 2 * p + 1 - side
            for n in (0, 1):
                wo_arrived((f, at.f_far)[n], t)
                wo_to_core(n, t).start()

    def wo_complete():
        def both(t):
            wo_arrived(at.f_core, t)
            wo_arrived(at.f_diag, t)

        others(both)
        for c in range(cols):
            own_wo(c).wait()

    def wo_finish():
        for way in (0, 1):
            at.onward(way, lambda to: wo_first(way, to).wait_send())
        for n in (0, 1):
            wo_own_side(n).wait_send()

        def chain(t, way):
            at.onward(way, lambda to: wo_next(t, way, to).wait_send())
            wo_to_far(t).wait_send()
            for n in (0, 1):
                wo_to_side(n, t).wait_send()

        @pl.loop(1, at.pairs)
        def _(k):
            at.at_distance(k, False, chain)

        def shared(t):
            for n in (0, 1):
                wo_to_core(n, t).wait_send()

        others(shared)

    def down(h):
        return remote(
            win.at[h, 1], win.at[h, 3],
            halo_send.at[0, h], halo_recv.at[0, h], (f, at.beside(-1)),
        )

    def up(h):
        return remote(
            win.at[h, 2], win.at[h, 0],
            halo_send.at[1, h], halo_recv.at[1, h], (f, at.beside(1)),
        )

    def past_move(g, h, x, n, device):
        piece = past.at[g, h, x]
        return remote(piece, piece, past_send.at[n, h, x], past_recv.at[g, h, x], device)

    def past_far(h, x):
        return past_move(f, h, x, 0, (at.f_far, s))

    def past_core(h, x):
        return past_move(f, h, x, 1, (at.f_core, s))

    def past_passed(h, x):
        return past_move(at.f_far, h, x, 2, (at.f_core, s))

    def past_arrived(g, h, x):
        piece = past.at[g, h, x]
        remote(piece, piece, o_keep, past_recv.at[g, h, x], (at.f_core, s)).wait_recv()

    def leave(c):
        return remote(
            leaving.at[c], arriving.at[c], leave_send.at[c], leave_recv.at[c],
            (lax.rem(f + 3, 4), s),
        )

    def o_swap(h):
        return remote(
            o_own.at[1 - side, h], og.at[side, h], o_send.at[h], o_recv.at[h], (f, at.s_side)
        )

    for g in (1, 2, 0):
        w_cross_copy(g).start()
    w_start(1)
    w_start(2)
    fetch = pltpu.make_async_copy(w_mod_ref, w_mod_own, mod_sem)
    fetch.start()
    fetch.wait()
    for c in range(0, 2 * width, width // 2):
        mod[:, c : c + width // 2] = jnp.dot(
            emb_ref[...], w_mod_own[:, c : c + width // 2], preferred_element_type=jnp.float32
        )

    @pl.loop(0, frames * rows // 32)
    def _(n):
        per = rows // 32
        i = n // per
        spot = pl.ds(pl.multiple_of(lax.rem(n, per) * 32, 32), 32)
        x32 = x_ref[i, spot, :].astype(jnp.float32)
        mean = jnp.mean(x32, axis=-1, keepdims=True)
        var = jnp.mean((x32 - mean) ** 2, axis=-1, keepdims=True)
        normed = (x32 - mean) * lax.rsqrt(var + 1e-06)
        xm = normed * (1.0 + mod[pl.ds(i, 1), width:]) + mod[pl.ds(i, 1), :width]
        xg[side, pl.ds(pl.multiple_of(n * 32, 32), 32), :] = xm.astype(jnp.bfloat16)

    rows_out = remote(xg.at[side], xg.at[side], xm_send, xm_recv, (f, at.s_side))
    rows_out.start()
    w_spread(1)
    w_start(0)
    w_spread(2)
    wo_start()
    w_complete(1)
    w_complete(2)

    def keys_values(x):
        @pl.loop(0, heads)
        def _(h):
            w = jnp.concatenate([wg[1, h].reshape(-1, hd), wg[2, h].reshape(-1, hd)], axis=1)
            both = jnp.dot(xg[x], w, preferred_element_type=jnp.float32)
            key = both[:, :hd]
            key = key * lax.rsqrt(jnp.mean(key * key, axis=-1, keepdims=True) + 1e-06)
            for i in range(frames):
                own = slice(i * rows, (i + 1) * rows)
                key_t = key[own].T.astype(jnp.bfloat16)
                value_t = both[own, hd:].T.astype(jnp.bfloat16)
                win[h, 1 + x, 0, i] = key[own].astype(jnp.bfloat16)
                win[h, 1 + x, 1, i] = value_t
                past[f, h, x, 0, i] = key_t
                past[f, h, x, 1, i] = value_t
            pl.when(x == 0)(lambda: down(h).start())
            pl.when(x == 1)(lambda: up(h).start())
            past_far(h, x).start()
            past_core(h, x).start()

    keys_values(side)
    w_spread(0)
    remote(xg.at[side], xg.at[1 - side], xm_send, xm_recv, (f, at.s_side)).wait_recv()
    keys_values(1 - side)
    w_complete(0)

    @pl.loop(0, heads // 2)
    def _(hp):
        w = jnp.concatenate(
            [wg[0, 2 * hp].reshape(-1, hd), wg[0, 2 * hp + 1].reshape(-1, hd)], axis=1
        )
        for x in range(2):
            both = jnp.dot(xg[x], w, preferred_element_type=jnp.float32)
            for n in range(2):
                h = 2 * hp + n
                query = both[:, n * hd : (n + 1) * hd]
                query = (
                    query
                    * lax.rsqrt(jnp.mean(query * query, axis=-1, keepdims=True) + 1e-06)
                    * gain_ref[heads * side + h]
                )
                for i in range(frames):
                    q_own[h, x, i] = query[i * rows : (i + 1) * rows].T.astype(jnp.bfloat16)

    stride = (at.pairs - 1 + heads - 1) // heads
    kk = lax.broadcasted_iota(jnp.int32, (rows, rows), 0)
    rr = lax.broadcasted_iota(jnp.int32, (rows, rows), 1)
    whole = kk >= 0
    band = jnp.concatenate([kk >= rr, whole, kk <= rr], axis=0)
    order = lax.broadcasted_iota(jnp.int32, (groups * frames, rows), 0)

    @pl.loop(0, heads)
    def _(h):
        for x in range(2):
            past_arrived(at.f_far, h, x)
            past_passed(h, x).start()
        down(h).wait_recv()
        up(h).wait_recv()
        for g in (at.f_core, at.f_diag):
            for x in range(2):
                past_arrived(g, h, x)

        @pl.loop(0, 2 * frames)
        def _(n):
            i = lax.rem(n, frames)
            b = lax.rem(n // frames + 1 - side, 2)
            mine = f * frames + i
            q = q_own[h, b, i]
            keys = jnp.concatenate([win[h, b + j, 0, i] for j in range(3)], axis=0)
            score = jnp.dot(keys, q, preferred_element_type=jnp.float32) * inv
            score = jnp.where(band, score, -1e30)
            q32 = q.astype(jnp.float32)
            time = jnp.full(order.shape, -1e30, jnp.float32)
            for g in range(groups * frames):
                k_g = past[g // frames, h, b, 0, g % frames].astype(jnp.float32)
                t_g = jnp.sum(q32 * k_g, axis=0, keepdims=True) * inv
                time = jnp.where(jnp.logical_and(order == g, order < mine), t_g, time)
            top = jnp.maximum(
                jnp.max(score, axis=0, keepdims=True), jnp.max(time, axis=0, keepdims=True)
            )
            p = jnp.where(band, jnp.exp(score - top), 0.0)
            p_time = jnp.where(order < mine, jnp.exp(time - top), 0.0)
            total = jnp.sum(p, axis=0, keepdims=True) + jnp.sum(p_time, axis=0, keepdims=True)
            values = jnp.concatenate([win[h, b + j, 1, i] for j in range(3)], axis=1)
            acc = jnp.dot(values, p.astype(jnp.bfloat16), preferred_element_type=jnp.float32)
            p_time = p_time.astype(jnp.bfloat16).astype(jnp.float32)
            for g in range(groups * frames):
                v_g = past[g // frames, h, b, 1, g % frames].astype(jnp.float32)
                acc = acc + p_time[g : g + 1] * v_g
            o_own[b, h, i, :, :] = (acc / total).T.astype(jnp.bfloat16)

            @pl.when(n == frames - 1)
            def _():
                o_swap(h).start()

        og[side, h] = o_own[side, h]

        @pl.loop(h * stride + 1, jnp.minimum((h + 1) * stride, at.pairs - 1) + 1)
        def _(k):
            wo_spread(k)
            pl.when(k >= 2)(lambda: wo_pass_far(k - 1))

    wo_pass_far(at.pairs - 1)
    wo_pass_side()
    wo_complete()
    for h in range(heads):
        remote(
            o_own.at[0, h], og.at[1 - side, h], o_keep, o_recv.at[h], (f, at.s_side)
        ).wait_recv()

    attended = jnp.concatenate(
        [og[x, h].reshape(frames * rows, hd) for x in range(2) for h in range(heads)], axis=1
    )
    for c in range(cols):
        spot = slice(c * part, (c + 1) * part)
        w = wog[c].reshape(inner, part)
        proj = jnp.dot(attended, w, preferred_element_type=jnp.float32)
        for i in range(frames):
            x32 = x_ref[i, :, spot].astype(jnp.float32)
            eps = x32 + proj[i * rows : (i + 1) * rows]
            clean = (x32 - coef_ref[0, i] * eps) / coef_ref[1, i]
            done = (coef_ref[2, i] * clean + coef_ref[3, i] * eps).astype(jnp.bfloat16)
            if i == 0:
                leaving[c] = done
                leave(c).start()
            else:
                out_ref[i - 1, :, spot] = done

    @pl.when(f == 3)
    def _():
        out_ref[frames - 1] = fresh_ref[...]

    for c in range(cols):
        leave(c).wait_recv()

        @pl.when(f != 3)
        def _():
            out_ref[frames - 1, :, c * part : (c + 1) * part] = arriving[c]

    for c in range(cols):
        leave(c).wait_send()
    rows_out.wait_send()
    for g in range(3):
        w_finish(g)
    wo_finish()

    @pl.loop(0, heads)
    def _(h):
        for copy in (down(h), up(h), o_swap(h)):
            copy.wait_send()
        for x in range(2):
            for copy in (past_far(h, x), past_core(h, x), past_passed(h, x)):
                copy.wait_send()


def body(frames_in, levels, fresh, w_mod, w_qkv, q_gain, w_out):
    space = lax.axis_size("space")
    groups = lax.axis_size("frame")
    frames, rows, width = frames_in.shape
    heads = q_gain.shape[0]
    hd = w_qkv.shape[1] // (3 * heads)
    half = heads // 2
    bf16 = jnp.bfloat16
    vmem = pl.BlockSpec(memory_space=pltpu.VMEM)
    smem = pl.BlockSpec(memory_space=pltpu.SMEM)
    hbm = pl.BlockSpec(memory_space=pl.ANY)
    dma = pltpu.SemaphoreType.DMA

    emb = embed(levels, w_mod.shape[0])
    emb = jnp.pad(emb, ((0, 16 - frames), (0, 0)))
    later = jnp.maximum(levels - LEVELS // FRAMES, 0)
    a_now = alpha_bar(levels)
    a_later = alpha_bar(later)
    coefs = jnp.stack(
        [jnp.sqrt(1.0 - a_now), jnp.sqrt(a_now), jnp.sqrt(a_later), jnp.sqrt(1.0 - a_later)]
    )
    depth = w_qkv.shape[0]
    wo_depth = w_out.shape[0]
    return pl.pallas_call(
        functools.partial(step_kernel, space),
        out_shape=jax.ShapeDtypeStruct(frames_in.shape, bf16),
        in_specs=[smem, smem, vmem, vmem, vmem, hbm, hbm, hbm],
        out_specs=vmem,
        scratch_shapes=[
            pltpu.VMEM((2, frames * rows, width), bf16),
            pltpu.VMEM((3, half, space, depth, hd), bf16),
            pltpu.VMEM((groups, space, wo_depth, width // groups), bf16),
            pltpu.VMEM((half, 4, 2, frames, rows, hd), bf16),
            pltpu.VMEM((groups, half, 2, 2, frames, rows, hd), bf16),
            pltpu.VMEM((half, 2, frames, hd, rows), bf16),
            pltpu.VMEM((2, half, frames, rows, hd), bf16),
            pltpu.VMEM((2, half, frames, rows, hd), bf16),
            pltpu.VMEM((16, 2 * width), jnp.float32),
            pltpu.VMEM(w_mod.shape, bf16),
            pltpu.VMEM((groups, rows, width // groups), bf16),
            pltpu.VMEM((groups, rows, width // groups), bf16),
            dma((3, half)), dma((groups,)), dma, dma,
            dma((3,)), dma((3, space, 2)), dma((3, space)), dma((3, space)), dma((3, space)),
            dma((3, half, space)),
            dma((space, 2)), dma((space,)), dma((2, space)), dma((2, space)),
            dma((groups, space)),
            dma((2, half)), dma((2, half)), dma((3, half, 2)), dma((groups, half, 2)),
            dma, dma((half,)), dma((half,)), dma, dma((groups,)), dma((groups,)),
        ],
        compiler_params=pltpu.CompilerParams(
            collective_id=0, has_side_effects=True, vmem_limit_bytes=VMEM_LIMIT
        ),
        name="step",
    )(q_gain, coefs, emb, frames_in, fresh, w_qkv, w_out, w_mod)


def solution(mesh):
    return jax.shard_map(
        body,
        mesh=mesh,
        in_specs=(
            P("frame", "space", None),
            P("frame"),
            P("space", None),
            P(),
            P("space", None),
            P(),
            P("space", None),
        ),
        out_specs=P("frame", "space", None),
        check_vma=False,
    )
```

```python
import functools
import math

import jax
import jax.numpy as jnp
from jax import lax
from jax.experimental import pallas as pl
from jax.experimental.pallas import tpu as pltpu
from jax.sharding import PartitionSpec as P

LEVELS = 1000
FRAMES = 8
MESH = pl.DeviceIdType.MESH
VMEM_LIMIT = 56 * 1024 * 1024


def embed(levels, freq_count):
    half = freq_count // 2
    freqs = jnp.exp(-math.log(10000.0) * jnp.arange(half, dtype=jnp.float32) / half)
    angles = levels.astype(jnp.float32)[:, None] * freqs[None, :]
    return jnp.concatenate([jnp.cos(angles), jnp.sin(angles)], axis=1).astype(jnp.bfloat16)


def alpha_bar(steps):
    frac = steps.astype(jnp.float32) / LEVELS
    return jnp.cos((frac + 0.008) / 1.008 * (math.pi / 2)) ** 2


class Place:
    def __init__(self, space):
        self.pairs = space // 2
        self.f = lax.axis_index("frame")
        self.s = lax.axis_index("space")
        self.pair = self.s // 2
        self.side = self.s % 2
        core = self.f % 2
        self.f_core = self.f + 1 - 2 * core
        self.f_far = (self.f + 2) % 4
        self.f_diag = (self.f_core + 2) % 4
        self.s_side = self.s + 1 - 2 * self.side

    def beside(self, step):
        return 2 * lax.rem(self.pair + step + self.pairs, self.pairs) + self.side

    def onward(self, way, act):
        if way == 0:
            pl.when(self.pair + 1 < self.pairs)(lambda: act(self.s + 2))
        else:
            pl.when(self.pair >= 1)(lambda: act(self.s - 2))

    def at_distance(self, k, both_sides, act):
        sides = (self.side, 1 - self.side) if both_sides else (self.side,)

        @pl.when(self.pair >= k)
        def _():
            for side in sides:
                act(2 * (self.pair - k) + side, 0)

        @pl.when(self.pair + k < self.pairs)
        def _():
            for side in sides:
                act(2 * (self.pair + k) + side, 1)


def remote(src, dst, send_sem, recv_sem, device):
    return pltpu.make_async_remote_copy(
        src_ref=src,
        dst_ref=dst,
        send_sem=send_sem,
        recv_sem=recv_sem,
        device_id=device,
        device_id_type=MESH,
    )


def step_kernel(
    space, gain_ref, coef_ref, emb_ref, x_ref, fresh_ref, w_ref, wo_ref, w_mod_ref, out_ref,
    xg, wg, wx, wog, win, past, q_own, o_own, og, mod, w_mod_own, leaving, arriving,
    own_w_sem, stage_sem, own_wo_sem, xm_send, xm_recv,
    w_cross, w_chain, w_far, w_core, w_pass, w_recv,
    wo_chain, wo_far, wo_side, wo_core, wo_recv,
    halo_send, halo_recv, past_send, past_recv, o_keep, o_send, o_recv,
    mod_sem, leave_send, leave_recv,
):
    at = Place(space)
    frames, rows, width = x_ref.shape
    heads, hd = og.shape[1], og.shape[4]
    groups = wog.shape[0]
    assert rows == hd
    inner = 2 * heads * hd
    tokens = 2 * rows
    f, s, side = at.f, at.s, at.side
    inv = 1.0 / math.sqrt(hd)

    def columns(j, head):
        return w_ref.at[:, pl.ds(pl.multiple_of((j + 1) % 3 * inner + head * hd, hd), hd)]

    def own_w(j, h):
        return pltpu.make_async_copy(
            columns(j, heads * side + h), wg.at[h, s, j], own_w_sem.at[j, h]
        )

    def stage(j):
        return pltpu.make_async_copy(
            columns(j, heads * (1 - side) + f), wx.at[j], stage_sem.at[j]
        )

    slots = (pl.ds(0, 2), pl.ds(2, 1))

    def w_move(g, col, t, sem, device):
        piece = wg.at[col, t, slots[g]]
        return remote(piece, piece, sem, w_recv.at[g, col, t], device)

    def w_cross_copy(g):
        return remote(
            wx.at[slots[g]], wg.at[f, s, slots[g]], w_cross.at[g], w_recv.at[g, f, s],
            (f, at.s_side),
        )

    def w_next(g, t, way, to):
        return w_move(g, f, t, w_chain.at[g, t, way], (f, to))

    def w_to_far(g, t):
        return w_move(g, f, t, w_far.at[g, t], (at.f_far, s))

    def w_to_core(g, t):
        return w_move(g, f, t, w_core.at[g, t], (at.f_core, s))

    def w_passed(g, t):
        return w_move(g, at.f_far, t, w_pass.at[g, t], (at.f_core, s))

    def w_arrived(g, col, t):
        w_move(g, col, t, w_cross.at[g], (at.f_core, s)).wait_recv()

    def w_onward(g, t):
        for way in (0, 1):
            at.onward(way, lambda to: w_next(g, t, way, to).start())

    def w_share(g, t):
        w_to_far(g, t).start()
        w_to_core(g, t).start()

    def w_begin(g):
        w_arrived(g, f, at.s_side)
        w_onward(g, at.s_side)
        w_share(g, at.s_side)

    def w_take_far(g, t):
        w_arrived(g, at.f_far, t)
        w_passed(g, t).start()

    def w_step(g, k):
        def take(t, way):
            w_arrived(g, f, t)
            at.onward(way, lambda to: w_next(g, t, way, to).start())
            w_share(g, t)

        at.at_distance(k, True, take)
        pl.when(k == 1)(lambda: w_take_far(g, at.s_side))
        pl.when(k >= 2)(
            lambda: at.at_distance(k - 1, True, lambda t, way: w_take_far(g, t))
        )

    def w_end(g):
        at.at_distance(at.pairs - 1, True, lambda t, way: w_take_far(g, t))

    def others(act):
        @pl.loop(0, space)
        def _(t):
            pl.when(t != s)(lambda: act(t))

    def w_complete(g):
        def both(t):
            w_arrived(g, at.f_core, t)
            w_arrived(g, at.f_diag, t)

        others(both)

    def w_finish(g):
        w_cross_copy(g).wait_send()
        for t in (s, at.s_side):
            for way in (0, 1):
                at.onward(way, lambda to: w_next(g, t, way, to).wait_send())

        def chain(t, way):
            at.onward(way, lambda to: w_next(g, t, way, to).wait_send())

        @pl.loop(1, at.pairs)
        def _(k):
            at.at_distance(k, True, chain)

        def shared(t):
            w_to_far(g, t).wait_send()
            w_to_core(g, t).wait_send()
            w_passed(g, t).wait_send()

        others(shared)

    cols = wog.shape[0]
    part = width // cols

    def wo_block(col):
        return wo_ref.at[:, pl.ds(pl.multiple_of(col * part, part), part)]

    def own_wo(c):
        return pltpu.make_async_copy(wo_block(c), wog.at[c, s], own_wo_sem.at[c])

    def wo_move(col, t, sem, device):
        piece = wog.at[col, t]
        return remote(piece, piece, sem, wo_recv.at[col, t], device)

    def wo_first(way, to):
        return remote(
            wo_block(f), wog.at[f, s], wo_chain.at[s, way], wo_recv.at[f, s], (f, to)
        )

    def wo_own_side(n):
        col = (f, at.f_far)[n]
        return remote(
            wo_block(col), wog.at[col, s], wo_side.at[n, s], wo_recv.at[col, s], (f, at.s_side)
        )

    def wo_next(t, way, to):
        return wo_move(f, t, wo_chain.at[t, way], (f, to))

    def wo_to_far(t):
        return wo_move(f, t, wo_far.at[t], (at.f_far, s))

    def wo_to_side(n, t):
        return wo_move((f, at.f_far)[n], t, wo_side.at[n, t], (f, at.s_side))

    def wo_to_core(n, t):
        return wo_move((f, at.f_far)[n], t, wo_core.at[n, t], (at.f_core, s))

    def wo_arrived(col, t):
        wo_move(col, t, o_keep, (at.f_core, s)).wait_recv()

    def wo_start():
        for way in (0, 1):
            at.onward(way, lambda to: wo_first(way, to).start())
        for n in (0, 1):
            wo_own_side(n).start()
        for c in range(cols):
            own_wo(c).start()

    def wo_spread(k):
        def take(t, way):
            wo_arrived(f, t)
            at.onward(way, lambda to: wo_next(t, way, to).start())
            wo_to_far(t).start()
            wo_to_side(0, t).start()
            wo_to_core(0, t).start()

        at.at_distance(k, False, take)

    def wo_pass_far(k):
        def take(t, way):
            wo_arrived(at.f_far, t)
            wo_to_side(1, t).start()
            wo_to_core(1, t).start()

        at.at_distance(k, False, take)

    def wo_pass_side():
        @pl.loop(0, at.pairs)
        def _(p):
            t = 2 * p + 1 - side
            for n in (0, 1):
                wo_arrived((f, at.f_far)[n], t)
                wo_to_core(n, t).start()

    def wo_complete():
        def both(t):
            wo_arrived(at.f_core, t)
            wo_arrived(at.f_diag, t)

        others(both)
        for c in range(cols):
            own_wo(c).wait()

    def wo_finish():
        for way in (0, 1):
            at.onward(way, lambda to: wo_first(way, to).wait_send())
        for n in (0, 1):
            wo_own_side(n).wait_send()

        def chain(t, way):
            at.onward(way, lambda to: wo_next(t, way, to).wait_send())
            wo_to_far(t).wait_send()
            for n in (0, 1):
                wo_to_side(n, t).wait_send()

        @pl.loop(1, at.pairs)
        def _(k):
            at.at_distance(k, False, chain)

        def shared(t):
            for n in (0, 1):
                wo_to_core(n, t).wait_send()

        others(shared)

    def down(h):
        return remote(
            win.at[h, 1], win.at[h, 3],
            halo_send.at[0, h], halo_recv.at[0, h], (f, at.beside(-1)),
        )

    def up(h):
        return remote(
            win.at[h, 2], win.at[h, 0],
            halo_send.at[1, h], halo_recv.at[1, h], (f, at.beside(1)),
        )

    def past_move(g, h, x, n, device):
        piece = past.at[g, h, x]
        return remote(piece, piece, past_send.at[n, h, x], past_recv.at[g, h, x], device)

    def past_far(h, x):
        return past_move(f, h, x, 0, (at.f_far, s))

    def past_core(h, x):
        return past_move(f, h, x, 1, (at.f_core, s))

    def past_passed(h, x):
        return past_move(at.f_far, h, x, 2, (at.f_core, s))

    def past_arrived(g, h, x):
        piece = past.at[g, h, x]
        remote(piece, piece, o_keep, past_recv.at[g, h, x], (at.f_core, s)).wait_recv()

    def leave(c):
        return remote(
            leaving.at[c], arriving.at[c], leave_send.at[c], leave_recv.at[c],
            (lax.rem(f + 3, 4), s),
        )

    def o_swap(h):
        return remote(
            o_own.at[1 - side, h], og.at[side, h], o_send.at[h], o_recv.at[h], (f, at.s_side)
        )

    for j in range(3):
        stage(j).start()
    for h in range(heads):
        for j in range(3):
            own_w(j, h).start()
    fetch = pltpu.make_async_copy(w_mod_ref, w_mod_own, mod_sem)
    fetch.start()

    barrier = pltpu.get_barrier_semaphore()
    partners = (
        (f, at.beside(1)), (f, at.beside(-1)), (f, at.s_side), (at.f_far, s), (at.f_core, s),
        (at.f_diag, s),
    )
    for partner in partners:
        pl.semaphore_signal(barrier, inc=1, device_id=partner, device_id_type=MESH)
    for j in range(3):
        stage(j).wait()
    for h in range(heads):
        for j in range(3):
            own_w(j, h).wait()
    fetch.wait()
    pl.semaphore_wait(barrier, len(partners))

    for g in range(2):
        w_cross_copy(g).start()
    w_onward(0, s)
    for c in range(0, 2 * width, width // 2):
        mod[:, c : c + width // 2] = jnp.dot(
            emb_ref[...], w_mod_own[:, c : c + width // 2], preferred_element_type=jnp.float32
        )

    def send_rows(i):
        own = xg.at[side, pl.ds(i * rows, rows)]
        return remote(own, own, xm_send.at[i], xm_recv.at[i], (f, at.s_side))

    @pl.loop(0, frames * rows // 32)
    def _(n):
        per = rows // 32
        i = n // per
        spot = pl.ds(pl.multiple_of(lax.rem(n, per) * 32, 32), 32)
        x32 = x_ref[i, spot, :].astype(jnp.float32)
        mean = jnp.mean(x32, axis=-1, keepdims=True)
        var = jnp.mean((x32 - mean) ** 2, axis=-1, keepdims=True)
        normed = (x32 - mean) * lax.rsqrt(var + 1e-06)
        xm = normed * (1.0 + mod[pl.ds(i, 1), width:]) + mod[pl.ds(i, 1), :width]
        xg[side, pl.ds(pl.multiple_of(n * 32, 32), 32), :] = xm.astype(jnp.bfloat16)

        for i in range(frames):
            pl.when(n == (i + 1) * per - 1)(lambda: send_rows(i).start())

    w_begin(0)

    @pl.loop(1, at.pairs)
    def _(k):
        w_step(0, k)
        pl.when(k == 1)(lambda: w_onward(1, s))

    wo_start()
    w_end(0)
    w_complete(0)

    def keys_values(x, between):
        @pl.loop(0, heads)
        def _(h):
            w = jnp.concatenate([wg[h, :, j].reshape(-1, hd) for j in range(2)], axis=1)
            both = jnp.dot(xg[x], w, preferred_element_type=jnp.float32)
            key = both[:, :hd]
            key = key * lax.rsqrt(jnp.mean(key * key, axis=-1, keepdims=True) + 1e-06)
            for i in range(frames):
                own = slice(i * rows, (i + 1) * rows)
                key_t = key[own].T.astype(jnp.bfloat16)
                value_t = both[own, hd:].T.astype(jnp.bfloat16)
                win[h, 1 + x, 0, i] = key[own].astype(jnp.bfloat16)
                win[h, 1 + x, 1, i] = value_t
                past[f, h, x, 0, i] = key_t
                past[f, h, x, 1, i] = value_t
            pl.when(x == 0)(lambda: down(h).start())
            pl.when(x == 1)(lambda: up(h).start())
            past_far(h, x).start()
            past_core(h, x).start()
            between(h)

    stride = (at.pairs - 1 + heads - 1) // heads

    def q_steps(h):
        @pl.loop(h * stride + 1, jnp.minimum((h + 1) * stride, at.pairs - 1) + 1)
        def _(k):
            w_step(1, k)

    wo_stride = (at.pairs - 1 + 2) // 3

    def wo_steps(n):
        for k in range(n * wo_stride + 1, min((n + 1) * wo_stride, at.pairs - 1) + 1):
            wo_spread(k)
            if k >= 2:
                wo_pass_far(k - 1)

    def past_pass(h, x):
        past_arrived(at.f_far, h, x)
        past_passed(h, x).start()

    w_begin(1)
    keys_values(side, q_steps)
    w_end(1)
    wo_steps(0)
    for i in range(frames):
        other = xg.at[1 - side, pl.ds(i * rows, rows)]
        remote(other, other, xm_send.at[i], xm_recv.at[i], (f, at.s_side)).wait_recv()
    keys_values(1 - side, lambda h: None)
    wo_steps(1)
    w_complete(1)
    for h in range(heads):
        past_pass(h, side)

    @pl.loop(0, heads // 2)
    def _(hp):
        w = jnp.concatenate(
            [wg[2 * hp + n, :, 2].reshape(-1, hd) for n in range(2)], axis=1
        )
        for x in range(2):
            both = jnp.dot(xg[x], w, preferred_element_type=jnp.float32)
            for n in range(2):
                h = 2 * hp + n
                query = both[:, n * hd : (n + 1) * hd]
                query = (
                    query
                    * lax.rsqrt(jnp.mean(query * query, axis=-1, keepdims=True) + 1e-06)
                    * gain_ref[heads * side + h]
                )
                for i in range(frames):
                    q_own[h, x, i] = query[i * rows : (i + 1) * rows].T.astype(jnp.bfloat16)

    wo_steps(2)
    for i in range(frames):
        send_rows(i).wait_send()
    for g in range(2):
        w_finish(g)

    kk = lax.broadcasted_iota(jnp.int32, (rows, rows), 0)
    rr = lax.broadcasted_iota(jnp.int32, (rows, rows), 1)
    whole = kk >= 0
    band = jnp.concatenate([kk >= rr, whole, kk <= rr], axis=0)
    order = lax.broadcasted_iota(jnp.int32, (groups * frames, rows), 0)

    @pl.loop(0, heads)
    def _(h):
        past_pass(h, 1 - side)
        down(h).wait_recv()
        up(h).wait_recv()
        for g in (at.f_core, at.f_diag):
            for x in range(2):
                past_arrived(g, h, x)

        @pl.loop(0, 2 * frames)
        def _(n):
            i = lax.rem(n, frames)
            b = lax.rem(n // frames + 1 - side, 2)
            mine = f * frames + i
            q = q_own[h, b, i]
            keys = jnp.concatenate([win[h, b + j, 0, i] for j in range(3)], axis=0)
            score = jnp.dot(keys, q, preferred_element_type=jnp.float32) * inv
            score = jnp.where(band, score, -1e30)
            q32 = q.astype(jnp.float32)
            time = jnp.full(order.shape, -1e30, jnp.float32)
            for g in range(groups * frames):
                k_g = past[g // frames, h, b, 0, g % frames].astype(jnp.float32)
                t_g = jnp.sum(q32 * k_g, axis=0, keepdims=True) * inv
                time = jnp.where(jnp.logical_and(order == g, order < mine), t_g, time)
            top = jnp.maximum(
                jnp.max(score, axis=0, keepdims=True), jnp.max(time, axis=0, keepdims=True)
            )
            p = jnp.where(band, jnp.exp(score - top), 0.0)
            p_time = jnp.where(order < mine, jnp.exp(time - top), 0.0)
            total = jnp.sum(p, axis=0, keepdims=True) + jnp.sum(p_time, axis=0, keepdims=True)
            values = jnp.concatenate([win[h, b + j, 1, i] for j in range(3)], axis=1)
            acc = jnp.dot(values, p.astype(jnp.bfloat16), preferred_element_type=jnp.float32)
            p_time = p_time.astype(jnp.bfloat16).astype(jnp.float32)
            for g in range(groups * frames):
                v_g = past[g // frames, h, b, 1, g % frames].astype(jnp.float32)
                acc = acc + p_time[g : g + 1] * v_g
            o_own[b, h, i, :, :] = (acc / total).T.astype(jnp.bfloat16)

            @pl.when(n == frames - 1)
            def _():
                o_swap(h).start()

        og[side, h] = o_own[side, h]

        @pl.when(h == 0)
        def _():
            wo_pass_far(at.pairs - 1)
            wo_pass_side()

    @pl.loop(0, heads)
    def _(h):
        for copy in (down(h), up(h)):
            copy.wait_send()
        for x in range(2):
            for copy in (past_far(h, x), past_core(h, x), past_passed(h, x)):
                copy.wait_send()

    wo_complete()
    for h in range(heads):
        remote(
            o_own.at[0, h], og.at[1 - side, h], o_keep, o_recv.at[h], (f, at.s_side)
        ).wait_recv()

    attended = jnp.concatenate(
        [og[x, h].reshape(frames * rows, hd) for x in range(2) for h in range(heads)], axis=1
    )
    for c in range(cols):
        spot = slice(c * part, (c + 1) * part)
        w = wog[c].reshape(inner, part)
        proj = jnp.dot(attended, w, preferred_element_type=jnp.float32)
        for i in range(frames):
            x32 = x_ref[i, :, spot].astype(jnp.float32)
            eps = x32 + proj[i * rows : (i + 1) * rows]
            clean = (x32 - coef_ref[0, i] * eps) / coef_ref[1, i]
            done = (coef_ref[2, i] * clean + coef_ref[3, i] * eps).astype(jnp.bfloat16)
            if i == 0:
                leaving[c] = done
                leave(c).start()
            else:
                out_ref[i - 1, :, spot] = done

    @pl.when(f == 3)
    def _():
        out_ref[frames - 1] = fresh_ref[...]

    wo_finish()
    for h in range(heads):
        o_swap(h).wait_send()
    for c in range(cols):
        leave(c).wait_recv()

        @pl.when(f != 3)
        def _():
            out_ref[frames - 1, :, c * part : (c + 1) * part] = arriving[c]

    for c in range(cols):
        leave(c).wait_send()


def body(frames_in, levels, fresh, w_mod, w_qkv, q_gain, w_out):
    space = lax.axis_size("space")
    groups = lax.axis_size("frame")
    frames, rows, width = frames_in.shape
    heads = q_gain.shape[0]
    hd = w_qkv.shape[1] // (3 * heads)
    half = heads // 2
    bf16 = jnp.bfloat16
    vmem = pl.BlockSpec(memory_space=pltpu.VMEM)
    smem = pl.BlockSpec(memory_space=pltpu.SMEM)
    hbm = pl.BlockSpec(memory_space=pl.ANY)
    dma = pltpu.SemaphoreType.DMA

    emb = embed(levels, w_mod.shape[0])
    emb = jnp.pad(emb, ((0, 16 - frames), (0, 0)))
    later = jnp.maximum(levels - LEVELS // FRAMES, 0)
    a_now = alpha_bar(levels)
    a_later = alpha_bar(later)
    coefs = jnp.stack(
        [jnp.sqrt(1.0 - a_now), jnp.sqrt(a_now), jnp.sqrt(a_later), jnp.sqrt(1.0 - a_later)]
    )
    depth = w_qkv.shape[0]
    wo_depth = w_out.shape[0]
    return pl.pallas_call(
        functools.partial(step_kernel, space),
        out_shape=jax.ShapeDtypeStruct(frames_in.shape, bf16),
        in_specs=[smem, smem, vmem, vmem, vmem, hbm, hbm, hbm],
        out_specs=vmem,
        scratch_shapes=[
            pltpu.VMEM((2, frames * rows, width), bf16),
            pltpu.VMEM((half, space, 3, depth, hd), bf16),
            pltpu.VMEM((3, depth, hd), bf16),
            pltpu.VMEM((groups, space, wo_depth, width // groups), bf16),
            pltpu.VMEM((half, 4, 2, frames, rows, hd), bf16),
            pltpu.VMEM((groups, half, 2, 2, frames, rows, hd), bf16),
            pltpu.VMEM((half, 2, frames, hd, rows), bf16),
            pltpu.VMEM((2, half, frames, rows, hd), bf16),
            pltpu.VMEM((2, half, frames, rows, hd), bf16),
            pltpu.VMEM((16, 2 * width), jnp.float32),
            pltpu.VMEM(w_mod.shape, bf16),
            pltpu.VMEM((groups, rows, width // groups), bf16),
            pltpu.VMEM((groups, rows, width // groups), bf16),
            dma((3, half)), dma((3,)), dma((groups,)), dma((frames,)), dma((frames,)),
            dma((2,)), dma((2, space, 2)), dma((2, space)), dma((2, space)), dma((2, space)),
            dma((2, half, space)),
            dma((space, 2)), dma((space,)), dma((2, space)), dma((2, space)),
            dma((groups, space)),
            dma((2, half)), dma((2, half)), dma((3, half, 2)), dma((groups, half, 2)),
            dma, dma((half,)), dma((half,)), dma, dma((groups,)), dma((groups,)),
        ],
        compiler_params=pltpu.CompilerParams(
            collective_id=0, has_side_effects=True, vmem_limit_bytes=VMEM_LIMIT
        ),
        name="step",
    )(q_gain, coefs, emb, frames_in, fresh, w_qkv, w_out, w_mod)


def solution(mesh):
    return jax.shard_map(
        body,
        mesh=mesh,
        in_specs=(
            P("frame", "space", None),
            P("frame"),
            P("space", None),
            P(),
            P("space", None),
            P(),
            P("space", None),
        ),
        out_specs=P("frame", "space", None),
        check_vma=False,
    )
```

```python
import functools
import math

import jax
import jax.numpy as jnp
from jax import lax
from jax.experimental import pallas as pl
from jax.experimental.pallas import tpu as pltpu
from jax.sharding import PartitionSpec as P

LEVELS = 1000
FRAMES = 8
MESH = pl.DeviceIdType.MESH
VMEM_LIMIT = 56 * 1024 * 1024


def embed(levels, freq_count):
    half = freq_count // 2
    freqs = jnp.exp(-math.log(10000.0) * jnp.arange(half, dtype=jnp.float32) / half)
    angles = levels.astype(jnp.float32)[:, None] * freqs[None, :]
    return jnp.concatenate([jnp.cos(angles), jnp.sin(angles)], axis=1).astype(jnp.bfloat16)


def alpha_bar(steps):
    frac = steps.astype(jnp.float32) / LEVELS
    return jnp.cos((frac + 0.008) / 1.008 * (math.pi / 2)) ** 2


class Place:
    def __init__(self, space):
        self.pairs = space // 2
        self.f = lax.axis_index("frame")
        self.s = lax.axis_index("space")
        self.pair = self.s // 2
        self.side = self.s % 2
        core = self.f % 2
        self.f_core = self.f + 1 - 2 * core
        self.f_far = (self.f + 2) % 4
        self.f_diag = (self.f_core + 2) % 4
        self.s_side = self.s + 1 - 2 * self.side

    def beside(self, step):
        return 2 * lax.rem(self.pair + step + self.pairs, self.pairs) + self.side

    def onward(self, way, act):
        if way == 0:
            pl.when(self.pair + 1 < self.pairs)(lambda: act(self.s + 2))
        else:
            pl.when(self.pair >= 1)(lambda: act(self.s - 2))

    def at_distance(self, k, both_sides, act):
        sides = (self.side, 1 - self.side) if both_sides else (self.side,)

        @pl.when(self.pair >= k)
        def _():
            for side in sides:
                act(2 * (self.pair - k) + side, 0)

        @pl.when(self.pair + k < self.pairs)
        def _():
            for side in sides:
                act(2 * (self.pair + k) + side, 1)


def remote(src, dst, send_sem, recv_sem, device):
    return pltpu.make_async_remote_copy(
        src_ref=src,
        dst_ref=dst,
        send_sem=send_sem,
        recv_sem=recv_sem,
        device_id=device,
        device_id_type=MESH,
    )


def step_kernel(
    space, gain_ref, coef_ref, emb_ref, x_ref, fresh_ref, w_ref, wo_ref, w_mod_ref, out_ref,
    xg, wg, wx, wog, win, past, q_own, o_own, og, mod, w_mod_own, leaving, arriving,
    own_w_sem, stage_sem, own_wo_sem, xm_send, xm_recv,
    w_cross, w_chain, w_far, w_core, w_pass, w_recv,
    wo_chain, wo_far, wo_side, wo_core, wo_recv,
    halo_send, halo_recv, past_send, past_recv, o_keep, o_send, o_recv,
    mod_sem, leave_send, leave_recv,
):
    at = Place(space)
    frames, rows, width = x_ref.shape
    heads, hd = og.shape[1], og.shape[4]
    groups = wog.shape[0]
    assert rows == hd
    inner = 2 * heads * hd
    tokens = 2 * rows
    f, s, side = at.f, at.s, at.side
    inv = 1.0 / math.sqrt(hd)

    def columns(j, head):
        return w_ref.at[:, pl.ds(pl.multiple_of((j + 1) % 3 * inner + head * hd, hd), hd)]

    def own_w(j, h):
        return pltpu.make_async_copy(
            columns(j, heads * side + h), wg.at[h, s, j], own_w_sem.at[j, h]
        )

    def stage(j):
        return pltpu.make_async_copy(
            columns(j, heads * (1 - side) + f), wx.at[j], stage_sem.at[j]
        )

    slots = (pl.ds(0, 2), pl.ds(2, 1))

    def w_move(g, col, t, sem, device):
        piece = wg.at[col, t, slots[g]]
        return remote(piece, piece, sem, w_recv.at[g, col, t], device)

    def w_cross_copy(g):
        return remote(
            wx.at[slots[g]], wg.at[f, s, slots[g]], w_cross.at[g], w_recv.at[g, f, s],
            (f, at.s_side),
        )

    def w_next(g, t, way, to):
        return w_move(g, f, t, w_chain.at[g, t, way], (f, to))

    def w_to_far(g, t):
        return w_move(g, f, t, w_far.at[g, t], (at.f_far, s))

    def w_to_core(g, t):
        return w_move(g, f, t, w_core.at[g, t], (at.f_core, s))

    def w_passed(g, t):
        return w_move(g, at.f_far, t, w_pass.at[g, t], (at.f_core, s))

    def w_arrived(g, col, t):
        w_move(g, col, t, w_cross.at[g], (at.f_core, s)).wait_recv()

    def w_onward(g, t):
        for way in (0, 1):
            at.onward(way, lambda to: w_next(g, t, way, to).start())

    def w_share(g, t):
        w_to_far(g, t).start()
        w_to_core(g, t).start()

    def w_begin(g):
        w_arrived(g, f, at.s_side)
        w_onward(g, at.s_side)
        w_share(g, at.s_side)

    def w_take_far(g, t):
        w_arrived(g, at.f_far, t)
        w_passed(g, t).start()

    def w_step(g, k):
        def take(t, way):
            w_arrived(g, f, t)
            at.onward(way, lambda to: w_next(g, t, way, to).start())
            w_share(g, t)

        at.at_distance(k, True, take)
        pl.when(k == 1)(lambda: w_take_far(g, at.s_side))
        pl.when(k >= 2)(
            lambda: at.at_distance(k - 1, True, lambda t, way: w_take_far(g, t))
        )

    def w_end(g):
        at.at_distance(at.pairs - 1, True, lambda t, way: w_take_far(g, t))

    def others(act):
        @pl.loop(0, space)
        def _(t):
            pl.when(t != s)(lambda: act(t))

    def w_complete(g):
        def both(t):
            w_arrived(g, at.f_core, t)
            w_arrived(g, at.f_diag, t)

        others(both)

    def w_finish(g):
        w_cross_copy(g).wait_send()
        for t in (s, at.s_side):
            for way in (0, 1):
                at.onward(way, lambda to: w_next(g, t, way, to).wait_send())

        def chain(t, way):
            at.onward(way, lambda to: w_next(g, t, way, to).wait_send())

        @pl.loop(1, at.pairs)
        def _(k):
            at.at_distance(k, True, chain)

        def shared(t):
            w_to_far(g, t).wait_send()
            w_to_core(g, t).wait_send()
            w_passed(g, t).wait_send()

        others(shared)

    cols = wog.shape[0]
    part = width // cols

    def wo_block(col):
        return wo_ref.at[:, pl.ds(pl.multiple_of(col * part, part), part)]

    def own_wo(c):
        return pltpu.make_async_copy(wo_block(c), wog.at[c, s], own_wo_sem.at[c])

    def wo_move(col, t, sem, device):
        piece = wog.at[col, t]
        return remote(piece, piece, sem, wo_recv.at[col, t], device)

    def wo_first(way, to):
        return remote(
            wo_block(f), wog.at[f, s], wo_chain.at[s, way], wo_recv.at[f, s], (f, to)
        )

    def wo_own_side(n):
        col = (f, at.f_far)[n]
        return remote(
            wo_block(col), wog.at[col, s], wo_side.at[n, s], wo_recv.at[col, s], (f, at.s_side)
        )

    def wo_next(t, way, to):
        return wo_move(f, t, wo_chain.at[t, way], (f, to))

    def wo_to_far(t):
        return wo_move(f, t, wo_far.at[t], (at.f_far, s))

    def wo_to_side(n, t):
        return wo_move((f, at.f_far)[n], t, wo_side.at[n, t], (f, at.s_side))

    def wo_to_core(n, t):
        return wo_move((f, at.f_far)[n], t, wo_core.at[n, t], (at.f_core, s))

    def wo_arrived(col, t):
        wo_move(col, t, o_keep, (at.f_core, s)).wait_recv()

    def wo_start():
        for way in (0, 1):
            at.onward(way, lambda to: wo_first(way, to).start())
        for n in (0, 1):
            wo_own_side(n).start()
        for c in range(cols):
            own_wo(c).start()

    def wo_spread(k):
        def take(t, way):
            wo_arrived(f, t)
            at.onward(way, lambda to: wo_next(t, way, to).start())
            wo_to_far(t).start()
            wo_to_side(0, t).start()
            wo_to_core(0, t).start()

        at.at_distance(k, False, take)

    def wo_pass_far(k):
        def take(t, way):
            wo_arrived(at.f_far, t)
            wo_to_side(1, t).start()
            wo_to_core(1, t).start()

        at.at_distance(k, False, take)

    def wo_pass_side():
        @pl.loop(0, at.pairs)
        def _(p):
            t = 2 * p + 1 - side
            for n in (0, 1):
                wo_arrived((f, at.f_far)[n], t)
                wo_to_core(n, t).start()

    def wo_complete():
        def both(t):
            wo_arrived(at.f_core, t)
            wo_arrived(at.f_diag, t)

        others(both)
        for c in range(cols):
            own_wo(c).wait()

    def wo_finish():
        for way in (0, 1):
            at.onward(way, lambda to: wo_first(way, to).wait_send())
        for n in (0, 1):
            wo_own_side(n).wait_send()

        def chain(t, way):
            at.onward(way, lambda to: wo_next(t, way, to).wait_send())
            wo_to_far(t).wait_send()
            for n in (0, 1):
                wo_to_side(n, t).wait_send()

        @pl.loop(1, at.pairs)
        def _(k):
            at.at_distance(k, False, chain)

        def shared(t):
            for n in (0, 1):
                wo_to_core(n, t).wait_send()

        others(shared)

    def down(h):
        return remote(
            win.at[h, 1], win.at[h, 3],
            halo_send.at[0, h], halo_recv.at[0, h], (f, at.beside(-1)),
        )

    def up(h):
        return remote(
            win.at[h, 2], win.at[h, 0],
            halo_send.at[1, h], halo_recv.at[1, h], (f, at.beside(1)),
        )

    def past_move(g, h, x, n, device):
        piece = past.at[g, h, x]
        return remote(piece, piece, past_send.at[n, h, x], past_recv.at[g, h, x], device)

    def past_far(h, x):
        return past_move(f, h, x, 0, (at.f_far, s))

    def past_core(h, x):
        return past_move(f, h, x, 1, (at.f_core, s))

    def past_passed(h, x):
        return past_move(at.f_far, h, x, 2, (at.f_core, s))

    def past_arrived(g, h, x):
        piece = past.at[g, h, x]
        remote(piece, piece, o_keep, past_recv.at[g, h, x], (at.f_core, s)).wait_recv()

    def leave(c):
        return remote(
            leaving.at[c], arriving.at[c], leave_send.at[c], leave_recv.at[c],
            (lax.rem(f + 3, 4), s),
        )

    def o_swap(h):
        return remote(
            o_own.at[1 - side, h], og.at[side, h], o_send.at[h], o_recv.at[h], (f, at.s_side)
        )

    for j in range(3):
        stage(j).start()
    for h in range(heads):
        for j in range(3):
            own_w(j, h).start()
    fetch = pltpu.make_async_copy(w_mod_ref, w_mod_own, mod_sem)
    fetch.start()

    barrier = pltpu.get_barrier_semaphore()
    partners = (
        (f, at.beside(1)), (f, at.beside(-1)), (f, at.s_side), (at.f_far, s), (at.f_core, s),
        (at.f_diag, s),
    )
    for partner in partners:
        pl.semaphore_signal(barrier, inc=1, device_id=partner, device_id_type=MESH)
    for j in range(3):
        stage(j).wait()
    for h in range(heads):
        for j in range(3):
            own_w(j, h).wait()
    fetch.wait()

    @pl.when(f < 2)
    def _():
        past[2:] = jnp.zeros_like(past[2:])

    pl.semaphore_wait(barrier, len(partners))

    for g in range(2):
        w_cross_copy(g).start()
    w_onward(0, s)
    for c in range(0, 2 * width, width // 2):
        mod[:, c : c + width // 2] = jnp.dot(
            emb_ref[...], w_mod_own[:, c : c + width // 2], preferred_element_type=jnp.float32
        )

    chunk = 32
    chunks = frames * rows // chunk

    def chunk_of(x, n):
        return xg.at[x, pl.ds(pl.multiple_of(n * chunk, chunk), chunk)]

    def send_rows(n):
        own = chunk_of(side, n)
        return remote(own, own, xm_send.at[n], xm_recv.at[n], (f, at.s_side))

    def normalize(n):
        i = n // (rows // chunk)
        spot = pl.ds(pl.multiple_of(lax.rem(n, rows // chunk) * chunk, chunk), chunk)
        x32 = x_ref[i, spot, :].astype(jnp.float32)
        mean = jnp.mean(x32, axis=-1, keepdims=True)
        var = jnp.mean((x32 - mean) ** 2, axis=-1, keepdims=True)
        normed = (x32 - mean) * lax.rsqrt(var + 1e-06)
        xm = normed * (1.0 + mod[pl.ds(i, 1), width:]) + mod[pl.ds(i, 1), :width]
        xg[side, pl.ds(pl.multiple_of(n * chunk, chunk), chunk), :] = xm.astype(jnp.bfloat16)
        send_rows(n).start()

    per_step = (chunks + at.pairs - 1) // at.pairs
    pl.loop(0, per_step)(normalize)
    w_begin(0)

    @pl.loop(1, at.pairs)
    def _(k):
        pl.loop(k * per_step, jnp.minimum((k + 1) * per_step, chunks))(normalize)
        w_step(0, k)
        pl.when(k == 1)(lambda: w_onward(1, s))

    wo_start()
    w_end(0)
    w_complete(0)

    def keys_values(x, between):
        @pl.loop(0, heads)
        def _(h):
            w = jnp.concatenate([wg[h, :, j].reshape(-1, hd) for j in range(2)], axis=1)
            both = jnp.dot(xg[x], w, preferred_element_type=jnp.float32)
            key = both[:, :hd]
            key = key * lax.rsqrt(jnp.mean(key * key, axis=-1, keepdims=True) + 1e-06)
            for i in range(frames):
                own = slice(i * rows, (i + 1) * rows)
                key_t = key[own].T.astype(jnp.bfloat16)
                value_t = both[own, hd:].T.astype(jnp.bfloat16)
                win[h, 1 + x, 0, i] = key[own].astype(jnp.bfloat16)
                win[h, 1 + x, 1, i] = value_t
                past[f, h, x, 0, i] = key_t
                past[f, h, x, 1, i] = value_t
            pl.when(x == 0)(lambda: down(h).start())
            pl.when(x == 1)(lambda: up(h).start())
            pl.when(f < 2)(lambda: past_far(h, x).start())
            past_core(h, x).start()
            between(h)

    stride = (at.pairs - 1 + heads - 1) // heads

    def q_steps(h):
        @pl.loop(h * stride + 1, jnp.minimum((h + 1) * stride, at.pairs - 1) + 1)
        def _(k):
            w_step(1, k)

    wo_stride = (at.pairs - 1 + 2) // 3

    def wo_steps(n):
        for k in range(n * wo_stride + 1, min((n + 1) * wo_stride, at.pairs - 1) + 1):
            wo_spread(k)
            if k >= 2:
                wo_pass_far(k - 1)

    def past_pass(h, x):
        past_arrived(at.f_far, h, x)
        past_passed(h, x).start()

    w_begin(1)
    keys_values(side, q_steps)
    w_end(1)
    wo_steps(0)
    @pl.loop(0, chunks)
    def _(n):
        other = chunk_of(1 - side, n)
        remote(other, other, xm_send.at[n], xm_recv.at[n], (f, at.s_side)).wait_recv()

    keys_values(1 - side, lambda h: None)
    wo_steps(1)
    w_complete(1)

    @pl.when(f >= 2)
    def _():
        for h in range(heads):
            past_pass(h, side)

    @pl.loop(0, heads // 2)
    def _(hp):
        w = jnp.concatenate(
            [wg[2 * hp + n, :, 2].reshape(-1, hd) for n in range(2)], axis=1
        )
        for x in range(2):
            both = jnp.dot(xg[x], w, preferred_element_type=jnp.float32)
            for n in range(2):
                h = 2 * hp + n
                query = both[:, n * hd : (n + 1) * hd]
                query = (
                    query
                    * lax.rsqrt(jnp.mean(query * query, axis=-1, keepdims=True) + 1e-06)
                    * gain_ref[heads * side + h]
                )
                for i in range(frames):
                    q_own[h, x, i] = query[i * rows : (i + 1) * rows].T.astype(jnp.bfloat16)

    wo_steps(2)
    pl.loop(0, chunks)(lambda n: send_rows(n).wait_send())
    for g in range(2):
        w_finish(g)

    kk = lax.broadcasted_iota(jnp.int32, (rows, rows), 0)
    rr = lax.broadcasted_iota(jnp.int32, (rows, rows), 1)
    whole = kk >= 0
    band = jnp.concatenate([kk >= rr, whole, kk <= rr], axis=0)
    order = lax.broadcasted_iota(jnp.int32, (groups * frames, rows), 0)

    @pl.loop(0, heads)
    def _(h):
        pl.when(f >= 2)(lambda: past_pass(h, 1 - side))
        down(h).wait_recv()
        up(h).wait_recv()
        for x in range(2):
            past_arrived(at.f_core, h, x)
            pl.when(f >= 2)(lambda: past_arrived(at.f_diag, h, x))

        @pl.loop(0, 2 * frames)
        def _(n):
            i = lax.rem(n, frames)
            b = lax.rem(n // frames + 1 - side, 2)
            mine = f * frames + i
            q = q_own[h, b, i]
            keys = jnp.concatenate([win[h, b + j, 0, i] for j in range(3)], axis=0)
            score = jnp.dot(keys, q, preferred_element_type=jnp.float32) * inv
            score = jnp.where(band, score, -1e30)
            q32 = q.astype(jnp.float32)
            time = jnp.full(order.shape, -1e30, jnp.float32)
            for g in range(groups * frames):
                k_g = past[g // frames, h, b, 0, g % frames].astype(jnp.float32)
                t_g = jnp.sum(q32 * k_g, axis=0, keepdims=True) * inv
                time = jnp.where(jnp.logical_and(order == g, order < mine), t_g, time)
            top = jnp.maximum(
                jnp.max(score, axis=0, keepdims=True), jnp.max(time, axis=0, keepdims=True)
            )
            p = jnp.where(band, jnp.exp(score - top), 0.0)
            p_time = jnp.where(order < mine, jnp.exp(time - top), 0.0)
            total = jnp.sum(p, axis=0, keepdims=True) + jnp.sum(p_time, axis=0, keepdims=True)
            values = jnp.concatenate([win[h, b + j, 1, i] for j in range(3)], axis=1)
            acc = jnp.dot(values, p.astype(jnp.bfloat16), preferred_element_type=jnp.float32)
            p_time = p_time.astype(jnp.bfloat16).astype(jnp.float32)
            for g in range(groups * frames):
                v_g = past[g // frames, h, b, 1, g % frames].astype(jnp.float32)
                acc = acc + p_time[g : g + 1] * v_g
            o_own[b, h, i, :, :] = (acc / total).T.astype(jnp.bfloat16)

            @pl.when(n == frames - 1)
            def _():
                o_swap(h).start()

        og[side, h] = o_own[side, h]

        @pl.when(h == 0)
        def _():
            wo_pass_far(at.pairs - 1)
            wo_pass_side()

    @pl.loop(0, heads)
    def _(h):
        for copy in (down(h), up(h)):
            copy.wait_send()
        for x in range(2):
            past_core(h, x).wait_send()
            pl.when(f < 2)(lambda: past_far(h, x).wait_send())
            pl.when(f >= 2)(lambda: past_passed(h, x).wait_send())

    wo_complete()
    for h in range(heads):
        remote(
            o_own.at[0, h], og.at[1 - side, h], o_keep, o_recv.at[h], (f, at.s_side)
        ).wait_recv()

    attended = jnp.concatenate(
        [og[x, h].reshape(frames * rows, hd) for x in range(2) for h in range(heads)], axis=1
    )
    for c in range(cols):
        spot = slice(c * part, (c + 1) * part)
        w = wog[c].reshape(inner, part)
        proj = jnp.dot(attended, w, preferred_element_type=jnp.float32)
        for i in range(frames):
            x32 = x_ref[i, :, spot].astype(jnp.float32)
            eps = x32 + proj[i * rows : (i + 1) * rows]
            clean = (x32 - coef_ref[0, i] * eps) / coef_ref[1, i]
            done = (coef_ref[2, i] * clean + coef_ref[3, i] * eps).astype(jnp.bfloat16)
            if i == 0:
                leaving[c] = done
                leave(c).start()
            else:
                out_ref[i - 1, :, spot] = done

    @pl.when(f == 3)
    def _():
        out_ref[frames - 1] = fresh_ref[...]

    wo_finish()
    for h in range(heads):
        o_swap(h).wait_send()
    for c in range(cols):
        leave(c).wait_recv()

        @pl.when(f != 3)
        def _():
            out_ref[frames - 1, :, c * part : (c + 1) * part] = arriving[c]

    for c in range(cols):
        leave(c).wait_send()


def body(frames_in, levels, fresh, w_mod, w_qkv, q_gain, w_out):
    space = lax.axis_size("space")
    groups = lax.axis_size("frame")
    frames, rows, width = frames_in.shape
    heads = q_gain.shape[0]
    hd = w_qkv.shape[1] // (3 * heads)
    half = heads // 2
    bf16 = jnp.bfloat16
    vmem = pl.BlockSpec(memory_space=pltpu.VMEM)
    smem = pl.BlockSpec(memory_space=pltpu.SMEM)
    hbm = pl.BlockSpec(memory_space=pl.ANY)
    dma = pltpu.SemaphoreType.DMA

    emb = embed(levels, w_mod.shape[0])
    emb = jnp.pad(emb, ((0, 16 - frames), (0, 0)))
    later = jnp.maximum(levels - LEVELS // FRAMES, 0)
    a_now = alpha_bar(levels)
    a_later = alpha_bar(later)
    coefs = jnp.stack(
        [jnp.sqrt(1.0 - a_now), jnp.sqrt(a_now), jnp.sqrt(a_later), jnp.sqrt(1.0 - a_later)]
    )
    depth = w_qkv.shape[0]
    wo_depth = w_out.shape[0]
    return pl.pallas_call(
        functools.partial(step_kernel, space),
        out_shape=jax.ShapeDtypeStruct(frames_in.shape, bf16),
        in_specs=[smem, smem, vmem, vmem, vmem, hbm, hbm, hbm],
        out_specs=vmem,
        scratch_shapes=[
            pltpu.VMEM((2, frames * rows, width), bf16),
            pltpu.VMEM((half, space, 3, depth, hd), bf16),
            pltpu.VMEM((3, depth, hd), bf16),
            pltpu.VMEM((groups, space, wo_depth, width // groups), bf16),
            pltpu.VMEM((half, 4, 2, frames, rows, hd), bf16),
            pltpu.VMEM((groups, half, 2, 2, frames, rows, hd), bf16),
            pltpu.VMEM((half, 2, frames, hd, rows), bf16),
            pltpu.VMEM((2, half, frames, rows, hd), bf16),
            pltpu.VMEM((2, half, frames, rows, hd), bf16),
            pltpu.VMEM((16, 2 * width), jnp.float32),
            pltpu.VMEM(w_mod.shape, bf16),
            pltpu.VMEM((groups, rows, width // groups), bf16),
            pltpu.VMEM((groups, rows, width // groups), bf16),
            dma((3, half)), dma((3,)), dma((groups,)),
            dma((frames * rows // 32,)), dma((frames * rows // 32,)),
            dma((2,)), dma((2, space, 2)), dma((2, space)), dma((2, space)), dma((2, space)),
            dma((2, half, space)),
            dma((space, 2)), dma((space,)), dma((2, space)), dma((2, space)),
            dma((groups, space)),
            dma((2, half)), dma((2, half)), dma((3, half, 2)), dma((groups, half, 2)),
            dma, dma((half,)), dma((half,)), dma, dma((groups,)), dma((groups,)),
        ],
        compiler_params=pltpu.CompilerParams(
            collective_id=0, has_side_effects=True, vmem_limit_bytes=VMEM_LIMIT
        ),
        name="step",
    )(q_gain, coefs, emb, frames_in, fresh, w_qkv, w_out, w_mod)


def solution(mesh):
    return jax.shard_map(
        body,
        mesh=mesh,
        in_specs=(
            P("frame", "space", None),
            P("frame"),
            P("space", None),
            P(),
            P("space", None),
            P(),
            P("space", None),
        ),
        out_specs=P("frame", "space", None),
        check_vma=False,
    )
```

```python
import functools
import math

import jax
import jax.numpy as jnp
from jax import lax
from jax.experimental import pallas as pl
from jax.experimental.pallas import tpu as pltpu
from jax.sharding import PartitionSpec as P

LEVELS = 1000
FRAMES = 8
MESH = pl.DeviceIdType.MESH
VMEM_LIMIT = 56 * 1024 * 1024


def embed(levels, freq_count):
    half = freq_count // 2
    freqs = jnp.exp(-math.log(10000.0) * jnp.arange(half, dtype=jnp.float32) / half)
    angles = levels.astype(jnp.float32)[:, None] * freqs[None, :]
    return jnp.concatenate([jnp.cos(angles), jnp.sin(angles)], axis=1).astype(jnp.bfloat16)


def alpha_bar(steps):
    frac = steps.astype(jnp.float32) / LEVELS
    return jnp.cos((frac + 0.008) / 1.008 * (math.pi / 2)) ** 2


class Place:
    def __init__(self, space):
        self.pairs = space // 2
        self.f = lax.axis_index("frame")
        self.s = lax.axis_index("space")
        self.pair = self.s // 2
        self.side = self.s % 2
        core = self.f % 2
        self.f_core = self.f + 1 - 2 * core
        self.f_far = (self.f + 2) % 4
        self.f_diag = (self.f_core + 2) % 4
        self.s_side = self.s + 1 - 2 * self.side

    def beside(self, step):
        return 2 * lax.rem(self.pair + step + self.pairs, self.pairs) + self.side

    def onward(self, way, act):
        if way == 0:
            pl.when(self.pair + 1 < self.pairs)(lambda: act(self.s + 2))
        else:
            pl.when(self.pair >= 1)(lambda: act(self.s - 2))

    def at_distance(self, k, both_sides, act):
        sides = (self.side, 1 - self.side) if both_sides else (self.side,)

        @pl.when(self.pair >= k)
        def _():
            for side in sides:
                act(2 * (self.pair - k) + side, 0)

        @pl.when(self.pair + k < self.pairs)
        def _():
            for side in sides:
                act(2 * (self.pair + k) + side, 1)


def remote(src, dst, send_sem, recv_sem, device):
    return pltpu.make_async_remote_copy(
        src_ref=src,
        dst_ref=dst,
        send_sem=send_sem,
        recv_sem=recv_sem,
        device_id=device,
        device_id_type=MESH,
    )


def step_kernel(
    space, gain_ref, coef_ref, emb_ref, x_ref, fresh_ref, w_ref, wo_ref, w_mod_ref, out_ref,
    xg, wg, wx, wog, win, past, q_own, o_own, og, mod, w_mod_own, leaving, arriving,
    own_w_sem, stage_sem, own_wo_sem, xm_send, xm_recv,
    w_cross, w_chain, w_far, w_core, w_pass, w_recv,
    wo_chain, wo_far, wo_side, wo_core, wo_recv,
    halo_send, halo_recv, past_send, past_recv, o_keep, o_send, o_recv,
    mod_sem, leave_send, leave_recv,
):
    at = Place(space)
    frames, rows, width = x_ref.shape
    heads, hd = og.shape[1], og.shape[4]
    groups = wog.shape[0]
    assert rows == hd
    inner = 2 * heads * hd
    tokens = 2 * rows
    f, s, side = at.f, at.s, at.side
    inv = 1.0 / math.sqrt(hd)

    def columns(j, head):
        return w_ref.at[:, pl.ds(pl.multiple_of((j + 1) % 3 * inner + head * hd, hd), hd)]

    def own_w(j, h):
        return pltpu.make_async_copy(
            columns(j, heads * side + h), wg.at[h, s, j], own_w_sem.at[j, h]
        )

    def stage(j):
        return pltpu.make_async_copy(
            columns(j, heads * (1 - side) + f), wx.at[j], stage_sem.at[j]
        )

    slots = (pl.ds(0, 2), pl.ds(2, 1))

    def w_move(g, col, t, sem, device):
        piece = wg.at[col, t, slots[g]]
        return remote(piece, piece, sem, w_recv.at[g, col, t], device)

    def w_cross_copy(g):
        return remote(
            wx.at[slots[g]], wg.at[f, s, slots[g]], w_cross.at[g], w_recv.at[g, f, s],
            (f, at.s_side),
        )

    def w_next(g, t, way, to):
        return w_move(g, f, t, w_chain.at[g, t, way], (f, to))

    def w_to_far(g, t):
        return w_move(g, f, t, w_far.at[g, t], (at.f_far, s))

    def w_to_core(g, t):
        return w_move(g, f, t, w_core.at[g, t], (at.f_core, s))

    def w_passed(g, t):
        return w_move(g, at.f_far, t, w_pass.at[g, t], (at.f_core, s))

    def w_arrived(g, col, t):
        w_move(g, col, t, w_cross.at[g], (at.f_core, s)).wait_recv()

    def w_onward(g, t):
        for way in (0, 1):
            at.onward(way, lambda to: w_next(g, t, way, to).start())

    def w_share(g, t):
        w_to_far(g, t).start()
        w_to_core(g, t).start()

    def w_begin(g):
        w_arrived(g, f, at.s_side)
        w_onward(g, at.s_side)
        w_share(g, at.s_side)

    def w_take_far(g, t):
        w_arrived(g, at.f_far, t)
        w_passed(g, t).start()

    def w_step(g, k):
        def take(t, way):
            w_arrived(g, f, t)
            at.onward(way, lambda to: w_next(g, t, way, to).start())
            w_share(g, t)

        at.at_distance(k, True, take)
        pl.when(k == 1)(lambda: w_take_far(g, at.s_side))
        pl.when(k >= 2)(
            lambda: at.at_distance(k - 1, True, lambda t, way: w_take_far(g, t))
        )

    def w_end(g):
        at.at_distance(at.pairs - 1, True, lambda t, way: w_take_far(g, t))

    def others(act):
        @pl.loop(0, space)
        def _(t):
            pl.when(t != s)(lambda: act(t))

    def w_complete(g):
        def both(t):
            w_arrived(g, at.f_core, t)
            w_arrived(g, at.f_diag, t)

        others(both)

    def w_finish(g):
        w_cross_copy(g).wait_send()
        for t in (s, at.s_side):
            for way in (0, 1):
                at.onward(way, lambda to: w_next(g, t, way, to).wait_send())

        def chain(t, way):
            at.onward(way, lambda to: w_next(g, t, way, to).wait_send())

        @pl.loop(1, at.pairs)
        def _(k):
            at.at_distance(k, True, chain)

        def shared(t):
            w_to_far(g, t).wait_send()
            w_to_core(g, t).wait_send()
            w_passed(g, t).wait_send()

        others(shared)

    cols = wog.shape[0]
    part = width // cols

    def wo_block(col):
        return wo_ref.at[:, pl.ds(pl.multiple_of(col * part, part), part)]

    def own_wo(c):
        return pltpu.make_async_copy(wo_block(c), wog.at[c, s], own_wo_sem.at[c])

    def wo_move(col, t, sem, device):
        piece = wog.at[col, t]
        return remote(piece, piece, sem, wo_recv.at[col, t], device)

    def wo_first(way, to):
        return remote(
            wo_block(f), wog.at[f, s], wo_chain.at[s, way], wo_recv.at[f, s], (f, to)
        )

    def wo_own_side(n):
        col = (f, at.f_far)[n]
        return remote(
            wo_block(col), wog.at[col, s], wo_side.at[n, s], wo_recv.at[col, s], (f, at.s_side)
        )

    def wo_next(t, way, to):
        return wo_move(f, t, wo_chain.at[t, way], (f, to))

    def wo_to_far(t):
        return wo_move(f, t, wo_far.at[t], (at.f_far, s))

    def wo_to_side(n, t):
        return wo_move((f, at.f_far)[n], t, wo_side.at[n, t], (f, at.s_side))

    def wo_to_core(n, t):
        return wo_move((f, at.f_far)[n], t, wo_core.at[n, t], (at.f_core, s))

    def wo_arrived(col, t):
        wo_move(col, t, o_keep, (at.f_core, s)).wait_recv()

    def wo_start():
        for way in (0, 1):
            at.onward(way, lambda to: wo_first(way, to).start())
        for c in range(cols):
            own_wo(c).start()

    def wo_spread(k):
        def take(t, way):
            wo_arrived(f, t)
            at.onward(way, lambda to: wo_next(t, way, to).start())
            wo_to_far(t).start()
            wo_to_core(0, t).start()

        at.at_distance(k, False, take)

    def wo_over():
        for n in (0, 1):
            wo_own_side(n).start()

        @pl.loop(1, at.pairs)
        def _(k):
            at.at_distance(k, False, lambda t, way: wo_to_side(0, t).start())

    def wo_pass_far(k):
        def take(t, way):
            wo_arrived(at.f_far, t)
            wo_to_side(1, t).start()
            wo_to_core(1, t).start()

        at.at_distance(k, False, take)

    def wo_pass_side(k):
        def take(p):
            t = 2 * p + 1 - side
            for n in (0, 1):
                wo_arrived((f, at.f_far)[n], t)
                wo_to_core(n, t).start()

        pl.when(at.pair >= k)(lambda: take(at.pair - k))
        pl.when(jnp.logical_and(at.pair + k < at.pairs, k > 0))(lambda: take(at.pair + k))

    def wo_complete():
        def both(t):
            wo_arrived(at.f_core, t)
            wo_arrived(at.f_diag, t)

        others(both)
        for c in range(cols):
            own_wo(c).wait()

    def wo_finish():
        for way in (0, 1):
            at.onward(way, lambda to: wo_first(way, to).wait_send())
        for n in (0, 1):
            wo_own_side(n).wait_send()

        def chain(t, way):
            at.onward(way, lambda to: wo_next(t, way, to).wait_send())
            wo_to_far(t).wait_send()
            for n in (0, 1):
                wo_to_side(n, t).wait_send()

        @pl.loop(1, at.pairs)
        def _(k):
            at.at_distance(k, False, chain)

        def shared(t):
            for n in (0, 1):
                wo_to_core(n, t).wait_send()

        others(shared)

    def down(h):
        return remote(
            win.at[h, 1], win.at[h, 3],
            halo_send.at[0, h], halo_recv.at[0, h], (f, at.beside(-1)),
        )

    def up(h):
        return remote(
            win.at[h, 2], win.at[h, 0],
            halo_send.at[1, h], halo_recv.at[1, h], (f, at.beside(1)),
        )

    def past_move(g, h, x, n, device):
        piece = past.at[g, h, x]
        return remote(piece, piece, past_send.at[n, h, x], past_recv.at[g, h, x], device)

    def past_far(h, x):
        return past_move(f, h, x, 0, (at.f_far, s))

    def past_core(h, x):
        return past_move(f, h, x, 1, (at.f_core, s))

    def past_passed(h, x):
        return past_move(at.f_far, h, x, 2, (at.f_core, s))

    def past_arrived(g, h, x):
        piece = past.at[g, h, x]
        remote(piece, piece, o_keep, past_recv.at[g, h, x], (at.f_core, s)).wait_recv()

    def leave(c):
        return remote(
            leaving.at[c], arriving.at[c], leave_send.at[c], leave_recv.at[c],
            (lax.rem(f + 3, 4), s),
        )

    def o_swap(h):
        return remote(
            o_own.at[1 - side, h], og.at[side, h], o_send.at[h], o_recv.at[h], (f, at.s_side)
        )

    for j in range(3):
        stage(j).start()
    for h in range(heads):
        for j in range(3):
            own_w(j, h).start()
    fetch = pltpu.make_async_copy(w_mod_ref, w_mod_own, mod_sem)
    fetch.start()

    barrier = pltpu.get_barrier_semaphore()
    partners = (
        (f, at.beside(1)), (f, at.beside(-1)), (f, at.s_side), (at.f_far, s), (at.f_core, s),
        (at.f_diag, s),
    )
    for partner in partners:
        pl.semaphore_signal(barrier, inc=1, device_id=partner, device_id_type=MESH)
    for j in range(3):
        stage(j).wait()
    for h in range(heads):
        for j in range(3):
            own_w(j, h).wait()
    fetch.wait()

    @pl.when(f < 2)
    def _():
        past[2:] = jnp.zeros_like(past[2:])

    pl.semaphore_wait(barrier, len(partners))

    for g in range(2):
        w_cross_copy(g).start()
    w_onward(0, s)
    for c in range(0, 2 * width, width // 2):
        mod[:, c : c + width // 2] = jnp.dot(
            emb_ref[...], w_mod_own[:, c : c + width // 2], preferred_element_type=jnp.float32
        )

    chunk = 32
    chunks = frames * rows // chunk

    def chunk_of(x, n):
        return xg.at[x, pl.ds(pl.multiple_of(n * chunk, chunk), chunk)]

    def send_rows(n):
        own = chunk_of(side, n)
        return remote(own, own, xm_send.at[n], xm_recv.at[n], (f, at.s_side))

    def normalize(n):
        i = n // (rows // chunk)
        spot = pl.ds(pl.multiple_of(lax.rem(n, rows // chunk) * chunk, chunk), chunk)
        x32 = x_ref[i, spot, :].astype(jnp.float32)
        mean = jnp.mean(x32, axis=-1, keepdims=True)
        var = jnp.mean((x32 - mean) ** 2, axis=-1, keepdims=True)
        normed = (x32 - mean) * lax.rsqrt(var + 1e-06)
        xm = normed * (1.0 + mod[pl.ds(i, 1), width:]) + mod[pl.ds(i, 1), :width]
        xg[side, pl.ds(pl.multiple_of(n * chunk, chunk), chunk), :] = xm.astype(jnp.bfloat16)
        send_rows(n).start()

    per_step = (chunks + at.pairs - 1) // at.pairs
    pl.loop(0, per_step)(normalize)
    w_begin(0)

    @pl.loop(1, at.pairs)
    def _(k):
        pl.loop(k * per_step, jnp.minimum((k + 1) * per_step, chunks))(normalize)
        w_step(0, k)
        pl.when(k == 1)(lambda: w_onward(1, s))

    wo_start()
    w_end(0)
    w_complete(0)

    def keys_values(x, between):
        @pl.loop(0, heads)
        def _(h):
            w = jnp.concatenate([wg[h, :, j].reshape(-1, hd) for j in range(2)], axis=1)
            both = jnp.dot(xg[x], w, preferred_element_type=jnp.float32)
            key = both[:, :hd]
            key = key * lax.rsqrt(jnp.mean(key * key, axis=-1, keepdims=True) + 1e-06)
            for i in range(frames):
                own = slice(i * rows, (i + 1) * rows)
                key_t = key[own].T.astype(jnp.bfloat16)
                value_t = both[own, hd:].T.astype(jnp.bfloat16)
                win[h, 1 + x, 0, i] = key[own].astype(jnp.bfloat16)
                win[h, 1 + x, 1, i] = value_t
                past[f, h, x, 0, i] = key_t
                past[f, h, x, 1, i] = value_t
            pl.when(x == 0)(lambda: down(h).start())
            pl.when(x == 1)(lambda: up(h).start())
            pl.when(f < 2)(lambda: past_far(h, x).start())
            past_core(h, x).start()
            between(h)

    stride = (at.pairs - 1 + heads - 1) // heads

    def q_steps(h):
        @pl.loop(h * stride + 1, jnp.minimum((h + 1) * stride, at.pairs - 1) + 1)
        def _(k):
            w_step(1, k)
            wo_spread(k)

    def past_pass(h, x):
        past_arrived(at.f_far, h, x)
        past_passed(h, x).start()

    w_begin(1)
    keys_values(side, q_steps)
    w_end(1)
    @pl.loop(0, chunks)
    def _(n):
        other = chunk_of(1 - side, n)
        remote(other, other, xm_send.at[n], xm_recv.at[n], (f, at.s_side)).wait_recv()

    wo_over()
    keys_values(1 - side, lambda h: None)
    pl.loop(1, at.pairs)(wo_pass_far)
    w_complete(1)

    @pl.when(f >= 2)
    def _():
        for h in range(heads):
            past_pass(h, side)

    @pl.loop(0, heads // 2)
    def _(hp):
        w = jnp.concatenate(
            [wg[2 * hp + n, :, 2].reshape(-1, hd) for n in range(2)], axis=1
        )
        for x in range(2):
            both = jnp.dot(xg[x], w, preferred_element_type=jnp.float32)
            for n in range(2):
                h = 2 * hp + n
                query = both[:, n * hd : (n + 1) * hd]
                query = (
                    query
                    * lax.rsqrt(jnp.mean(query * query, axis=-1, keepdims=True) + 1e-06)
                    * gain_ref[heads * side + h]
                )
                for i in range(frames):
                    q_own[h, x, i] = query[i * rows : (i + 1) * rows].T.astype(jnp.bfloat16)

    pl.loop(0, chunks)(lambda n: send_rows(n).wait_send())
    for g in range(2):
        w_finish(g)

    kk = lax.broadcasted_iota(jnp.int32, (rows, rows), 0)
    rr = lax.broadcasted_iota(jnp.int32, (rows, rows), 1)
    whole = kk >= 0
    band = jnp.concatenate([kk >= rr, whole, kk <= rr], axis=0)
    order = lax.broadcasted_iota(jnp.int32, (groups * frames, rows), 0)

    @pl.loop(0, heads)
    def _(h):
        pl.when(f >= 2)(lambda: past_pass(h, 1 - side))
        down(h).wait_recv()
        up(h).wait_recv()
        for x in range(2):
            past_arrived(at.f_core, h, x)
            pl.when(f >= 2)(lambda: past_arrived(at.f_diag, h, x))

        @pl.loop(0, 2 * frames)
        def _(n):
            i = lax.rem(n, frames)
            b = lax.rem(n // frames + 1 - side, 2)
            mine = f * frames + i
            q = q_own[h, b, i]
            keys = jnp.concatenate([win[h, b + j, 0, i] for j in range(3)], axis=0)
            score = jnp.dot(keys, q, preferred_element_type=jnp.float32) * inv
            score = jnp.where(band, score, -1e30)
            q32 = q.astype(jnp.float32)
            time = jnp.full(order.shape, -1e30, jnp.float32)
            for g in range(groups * frames):
                k_g = past[g // frames, h, b, 0, g % frames].astype(jnp.float32)
                t_g = jnp.sum(q32 * k_g, axis=0, keepdims=True) * inv
                time = jnp.where(jnp.logical_and(order == g, order < mine), t_g, time)
            top = jnp.maximum(
                jnp.max(score, axis=0, keepdims=True), jnp.max(time, axis=0, keepdims=True)
            )
            p = jnp.where(band, jnp.exp(score - top), 0.0)
            p_time = jnp.where(order < mine, jnp.exp(time - top), 0.0)
            total = jnp.sum(p, axis=0, keepdims=True) + jnp.sum(p_time, axis=0, keepdims=True)
            values = jnp.concatenate([win[h, b + j, 1, i] for j in range(3)], axis=1)
            acc = jnp.dot(values, p.astype(jnp.bfloat16), preferred_element_type=jnp.float32)
            p_time = p_time.astype(jnp.bfloat16).astype(jnp.float32)
            for g in range(groups * frames):
                v_g = past[g // frames, h, b, 1, g % frames].astype(jnp.float32)
                acc = acc + p_time[g : g + 1] * v_g
            o_own[b, h, i, :, :] = (acc / total).T.astype(jnp.bfloat16)

            @pl.when(n == frames - 1)
            def _():
                o_swap(h).start()

        og[side, h] = o_own[side, h]

        last = at.pairs - 1
        pl.loop(
            jnp.clip((h - 1) * last // 2, 0, last), jnp.clip(h * last // 2, 0, last)
        )(wo_pass_side)

    wo_pass_side(at.pairs - 1)

    @pl.loop(0, heads)
    def _(h):
        for copy in (down(h), up(h)):
            copy.wait_send()
        for x in range(2):
            past_core(h, x).wait_send()
            pl.when(f < 2)(lambda: past_far(h, x).wait_send())
            pl.when(f >= 2)(lambda: past_passed(h, x).wait_send())

    wo_complete()
    for h in range(heads):
        remote(
            o_own.at[0, h], og.at[1 - side, h], o_keep, o_recv.at[h], (f, at.s_side)
        ).wait_recv()

    attended = jnp.concatenate(
        [og[x, h].reshape(frames * rows, hd) for x in range(2) for h in range(heads)], axis=1
    )
    for c in range(cols):
        spot = slice(c * part, (c + 1) * part)
        w = wog[c].reshape(inner, part)
        proj = jnp.dot(attended, w, preferred_element_type=jnp.float32)
        for i in range(frames):
            x32 = x_ref[i, :, spot].astype(jnp.float32)
            eps = x32 + proj[i * rows : (i + 1) * rows]
            clean = (x32 - coef_ref[0, i] * eps) / coef_ref[1, i]
            done = (coef_ref[2, i] * clean + coef_ref[3, i] * eps).astype(jnp.bfloat16)
            if i == 0:
                leaving[c] = done
                leave(c).start()
            else:
                out_ref[i - 1, :, spot] = done

    @pl.when(f == 3)
    def _():
        out_ref[frames - 1] = fresh_ref[...]

    wo_finish()
    for h in range(heads):
        o_swap(h).wait_send()
    for c in range(cols):
        leave(c).wait_recv()

        @pl.when(f != 3)
        def _():
            out_ref[frames - 1, :, c * part : (c + 1) * part] = arriving[c]

    for c in range(cols):
        leave(c).wait_send()


def body(frames_in, levels, fresh, w_mod, w_qkv, q_gain, w_out):
    space = lax.axis_size("space")
    groups = lax.axis_size("frame")
    frames, rows, width = frames_in.shape
    heads = q_gain.shape[0]
    hd = w_qkv.shape[1] // (3 * heads)
    half = heads // 2
    bf16 = jnp.bfloat16
    vmem = pl.BlockSpec(memory_space=pltpu.VMEM)
    smem = pl.BlockSpec(memory_space=pltpu.SMEM)
    hbm = pl.BlockSpec(memory_space=pl.ANY)
    dma = pltpu.SemaphoreType.DMA

    emb = embed(levels, w_mod.shape[0])
    emb = jnp.pad(emb, ((0, 16 - frames), (0, 0)))
    later = jnp.maximum(levels - LEVELS // FRAMES, 0)
    a_now = alpha_bar(levels)
    a_later = alpha_bar(later)
    coefs = jnp.stack(
        [jnp.sqrt(1.0 - a_now), jnp.sqrt(a_now), jnp.sqrt(a_later), jnp.sqrt(1.0 - a_later)]
    )
    depth = w_qkv.shape[0]
    wo_depth = w_out.shape[0]
    return pl.pallas_call(
        functools.partial(step_kernel, space),
        out_shape=jax.ShapeDtypeStruct(frames_in.shape, bf16),
        in_specs=[smem, smem, vmem, vmem, vmem, hbm, hbm, hbm],
        out_specs=vmem,
        scratch_shapes=[
            pltpu.VMEM((2, frames * rows, width), bf16),
            pltpu.VMEM((half, space, 3, depth, hd), bf16),
            pltpu.VMEM((3, depth, hd), bf16),
            pltpu.VMEM((groups, space, wo_depth, width // groups), bf16),
            pltpu.VMEM((half, 4, 2, frames, rows, hd), bf16),
            pltpu.VMEM((groups, half, 2, 2, frames, rows, hd), bf16),
            pltpu.VMEM((half, 2, frames, hd, rows), bf16),
            pltpu.VMEM((2, half, frames, rows, hd), bf16),
            pltpu.VMEM((2, half, frames, rows, hd), bf16),
            pltpu.VMEM((16, 2 * width), jnp.float32),
            pltpu.VMEM(w_mod.shape, bf16),
            pltpu.VMEM((groups, rows, width // groups), bf16),
            pltpu.VMEM((groups, rows, width // groups), bf16),
            dma((3, half)), dma((3,)), dma((groups,)),
            dma((frames * rows // 32,)), dma((frames * rows // 32,)),
            dma((2,)), dma((2, space, 2)), dma((2, space)), dma((2, space)), dma((2, space)),
            dma((2, half, space)),
            dma((space, 2)), dma((space,)), dma((2, space)), dma((2, space)),
            dma((groups, space)),
            dma((2, half)), dma((2, half)), dma((3, half, 2)), dma((groups, half, 2)),
            dma, dma((half,)), dma((half,)), dma, dma((groups,)), dma((groups,)),
        ],
        compiler_params=pltpu.CompilerParams(
            collective_id=0, has_side_effects=True, vmem_limit_bytes=VMEM_LIMIT
        ),
        name="step",
    )(q_gain, coefs, emb, frames_in, fresh, w_qkv, w_out, w_mod)


def solution(mesh):
    return jax.shard_map(
        body,
        mesh=mesh,
        in_specs=(
            P("frame", "space", None),
            P("frame"),
            P("space", None),
            P(),
            P("space", None),
            P(),
            P("space", None),
        ),
        out_specs=P("frame", "space", None),
        check_vma=False,
    )
```

```python
import functools
import math

import jax
import jax.numpy as jnp
from jax import lax
from jax.experimental import pallas as pl
from jax.experimental.pallas import tpu as pltpu
from jax.sharding import PartitionSpec as P

LEVELS = 1000
FRAMES = 8
MESH = pl.DeviceIdType.MESH
VMEM_LIMIT = 56 * 1024 * 1024


def embed(levels, freq_count):
    half = freq_count // 2
    freqs = jnp.exp(-math.log(10000.0) * jnp.arange(half, dtype=jnp.float32) / half)
    angles = levels.astype(jnp.float32)[:, None] * freqs[None, :]
    return jnp.concatenate([jnp.cos(angles), jnp.sin(angles)], axis=1).astype(jnp.bfloat16)


def alpha_bar(steps):
    frac = steps.astype(jnp.float32) / LEVELS
    return jnp.cos((frac + 0.008) / 1.008 * (math.pi / 2)) ** 2


class Place:
    def __init__(self, space):
        self.pairs = space // 2
        self.f = lax.axis_index("frame")
        self.s = lax.axis_index("space")
        self.pair = self.s // 2
        self.side = self.s % 2
        core = self.f % 2
        self.f_core = self.f + 1 - 2 * core
        self.f_far = (self.f + 2) % 4
        self.f_diag = (self.f_core + 2) % 4
        self.s_side = self.s + 1 - 2 * self.side

    def beside(self, step):
        return 2 * lax.rem(self.pair + step + self.pairs, self.pairs) + self.side

    def onward(self, way, act):
        if way == 0:
            pl.when(self.pair + 1 < self.pairs)(lambda: act(self.s + 2))
        else:
            pl.when(self.pair >= 1)(lambda: act(self.s - 2))

    def at_distance(self, k, both_sides, act):
        sides = (self.side, 1 - self.side) if both_sides else (self.side,)

        @pl.when(self.pair >= k)
        def _():
            for side in sides:
                act(2 * (self.pair - k) + side, 0)

        @pl.when(self.pair + k < self.pairs)
        def _():
            for side in sides:
                act(2 * (self.pair + k) + side, 1)


def remote(src, dst, send_sem, recv_sem, device):
    return pltpu.make_async_remote_copy(
        src_ref=src,
        dst_ref=dst,
        send_sem=send_sem,
        recv_sem=recv_sem,
        device_id=device,
        device_id_type=MESH,
    )


def step_kernel(
    space, gain_ref, coef_ref, emb_ref, x_ref, fresh_ref, w_ref, wo_ref, w_mod_ref, out_ref,
    xg, wg, wx, wog, win, past, q_own, o_own, og, mod, w_mod_own, leaving, arriving,
    own_w_sem, stage_sem, own_wo_sem, xm_send, xm_recv,
    w_cross, w_chain, w_far, w_core, w_pass, w_recv,
    wo_chain, wo_far, wo_side, wo_core, wo_recv,
    halo_send, halo_recv, past_send, past_recv, o_keep, o_send, o_recv,
    mod_sem, leave_send, leave_recv,
):
    at = Place(space)
    frames, rows, width = x_ref.shape
    heads, hd = og.shape[1], og.shape[4]
    groups = wog.shape[0]
    assert rows == hd
    inner = 2 * heads * hd
    tokens = 2 * rows
    f, s, side = at.f, at.s, at.side
    inv = 1.0 / math.sqrt(hd)

    def columns(j, head):
        return w_ref.at[:, pl.ds(pl.multiple_of((j + 1) % 3 * inner + head * hd, hd), hd)]

    def own_w(j, h):
        return pltpu.make_async_copy(
            columns(j, heads * side + h), wg.at[h, s, j], own_w_sem.at[j, h]
        )

    def stage(j):
        return pltpu.make_async_copy(
            columns(j, heads * (1 - side) + f), wx.at[j], stage_sem.at[j]
        )

    slots = (pl.ds(0, 2), pl.ds(2, 1))

    def w_move(g, col, t, sem, device):
        piece = wg.at[col, t, slots[g]]
        return remote(piece, piece, sem, w_recv.at[g, col, t], device)

    def w_cross_copy(g):
        return remote(
            wx.at[slots[g]], wg.at[f, s, slots[g]], w_cross.at[g], w_recv.at[g, f, s],
            (f, at.s_side),
        )

    def w_next(g, t, way, to):
        return w_move(g, f, t, w_chain.at[g, t, way], (f, to))

    def w_to_far(g, t):
        return w_move(g, f, t, w_far.at[g, t], (at.f_far, s))

    def w_to_core(g, t):
        return w_move(g, f, t, w_core.at[g, t], (at.f_core, s))

    def w_passed(g, t):
        return w_move(g, at.f_far, t, w_pass.at[g, t], (at.f_core, s))

    def w_arrived(g, col, t):
        w_move(g, col, t, w_cross.at[g], (at.f_core, s)).wait_recv()

    def w_onward(g, t):
        for way in (0, 1):
            at.onward(way, lambda to: w_next(g, t, way, to).start())

    def w_share(g, t):
        w_to_far(g, t).start()
        w_to_core(g, t).start()

    def w_begin(g):
        w_arrived(g, f, at.s_side)
        w_onward(g, at.s_side)
        w_share(g, at.s_side)

    def w_take_far(g, t):
        w_arrived(g, at.f_far, t)
        w_passed(g, t).start()

    def w_step(g, k):
        def take(t, way):
            w_arrived(g, f, t)
            at.onward(way, lambda to: w_next(g, t, way, to).start())
            w_share(g, t)

        at.at_distance(k, True, take)
        pl.when(k == 1)(lambda: w_take_far(g, at.s_side))
        pl.when(k >= 2)(
            lambda: at.at_distance(k - 1, True, lambda t, way: w_take_far(g, t))
        )

    def w_end(g):
        at.at_distance(at.pairs - 1, True, lambda t, way: w_take_far(g, t))

    def others(act):
        @pl.loop(0, space)
        def _(t):
            pl.when(t != s)(lambda: act(t))

    def w_complete(g):
        def both(t):
            w_arrived(g, at.f_core, t)
            w_arrived(g, at.f_diag, t)

        others(both)

    def w_finish(g):
        w_cross_copy(g).wait_send()
        for t in (s, at.s_side):
            for way in (0, 1):
                at.onward(way, lambda to: w_next(g, t, way, to).wait_send())

        def chain(t, way):
            at.onward(way, lambda to: w_next(g, t, way, to).wait_send())

        @pl.loop(1, at.pairs)
        def _(k):
            at.at_distance(k, True, chain)

        def shared(t):
            w_to_far(g, t).wait_send()
            w_to_core(g, t).wait_send()
            w_passed(g, t).wait_send()

        others(shared)

    cols = wog.shape[0]
    part = width // cols

    def wo_block(col):
        return wo_ref.at[:, pl.ds(pl.multiple_of(col * part, part), part)]

    def own_wo(c):
        return pltpu.make_async_copy(wo_block(c), wog.at[c, s], own_wo_sem.at[c])

    def wo_move(col, t, sem, device):
        piece = wog.at[col, t]
        return remote(piece, piece, sem, wo_recv.at[col, t], device)

    def wo_first(way, to):
        return remote(
            wo_block(f), wog.at[f, s], wo_chain.at[s, way], wo_recv.at[f, s], (f, to)
        )

    def wo_own_side(n):
        col = (f, at.f_far)[n]
        return remote(
            wo_block(col), wog.at[col, s], wo_side.at[n, s], wo_recv.at[col, s], (f, at.s_side)
        )

    def wo_next(t, way, to):
        return wo_move(f, t, wo_chain.at[t, way], (f, to))

    def wo_to_far(t):
        return wo_move(f, t, wo_far.at[t], (at.f_far, s))

    def wo_to_side(n, t):
        return wo_move((f, at.f_far)[n], t, wo_side.at[n, t], (f, at.s_side))

    def wo_to_core(n, t):
        return wo_move((f, at.f_far)[n], t, wo_core.at[n, t], (at.f_core, s))

    def wo_arrived(col, t):
        wo_move(col, t, o_keep, (at.f_core, s)).wait_recv()

    def wo_start():
        for way in (0, 1):
            at.onward(way, lambda to: wo_first(way, to).start())
        for c in range(cols):
            own_wo(c).start()

    def wo_spread(k):
        def take(t, way):
            wo_arrived(f, t)
            at.onward(way, lambda to: wo_next(t, way, to).start())
            wo_to_far(t).start()
            wo_to_core(0, t).start()

        at.at_distance(k, False, take)

    def wo_over():
        for n in (0, 1):
            wo_own_side(n).start()

        @pl.loop(1, at.pairs)
        def _(k):
            at.at_distance(k, False, lambda t, way: wo_to_side(0, t).start())

    def wo_pass_far(k):
        def take(t, way):
            wo_arrived(at.f_far, t)
            wo_to_side(1, t).start()
            wo_to_core(1, t).start()

        at.at_distance(k, False, take)

    def wo_pass_side(k):
        def take(p):
            t = 2 * p + 1 - side
            for n in (0, 1):
                wo_arrived((f, at.f_far)[n], t)
                wo_to_core(n, t).start()

        pl.when(at.pair >= k)(lambda: take(at.pair - k))
        pl.when(jnp.logical_and(at.pair + k < at.pairs, k > 0))(lambda: take(at.pair + k))

    def wo_complete():
        def both(t):
            wo_arrived(at.f_core, t)
            wo_arrived(at.f_diag, t)

        others(both)
        for c in range(cols):
            own_wo(c).wait()

    def wo_finish():
        for way in (0, 1):
            at.onward(way, lambda to: wo_first(way, to).wait_send())
        for n in (0, 1):
            wo_own_side(n).wait_send()

        def chain(t, way):
            at.onward(way, lambda to: wo_next(t, way, to).wait_send())
            wo_to_far(t).wait_send()
            for n in (0, 1):
                wo_to_side(n, t).wait_send()

        @pl.loop(1, at.pairs)
        def _(k):
            at.at_distance(k, False, chain)

        def shared(t):
            for n in (0, 1):
                wo_to_core(n, t).wait_send()

        others(shared)

    def down(h):
        return remote(
            win.at[h, 1], win.at[h, 3],
            halo_send.at[0, h], halo_recv.at[0, h], (f, at.beside(-1)),
        )

    def up(h):
        return remote(
            win.at[h, 2], win.at[h, 0],
            halo_send.at[1, h], halo_recv.at[1, h], (f, at.beside(1)),
        )

    def past_move(g, h, x, n, device):
        piece = past.at[g, h, x]
        return remote(piece, piece, past_send.at[n, h, x], past_recv.at[g, h, x], device)

    def past_far(h, x):
        return past_move(f, h, x, 0, (at.f_far, s))

    def past_core(h, x):
        return past_move(f, h, x, 1, (at.f_core, s))

    def past_passed(h, x):
        return past_move(at.f_far, h, x, 2, (at.f_core, s))

    def past_arrived(g, h, x):
        piece = past.at[g, h, x]
        remote(piece, piece, o_keep, past_recv.at[g, h, x], (at.f_core, s)).wait_recv()

    def leave(c):
        return remote(
            leaving.at[c], arriving.at[c], leave_send.at[c], leave_recv.at[c],
            (lax.rem(f + 3, 4), s),
        )

    def o_swap(h):
        return remote(
            o_own.at[1 - side, h], og.at[side, h], o_send.at[h], o_recv.at[h], (f, at.s_side)
        )

    for j in range(3):
        stage(j).start()
    for h in range(heads):
        for j in range(3):
            own_w(j, h).start()
    fetch = pltpu.make_async_copy(w_mod_ref, w_mod_own, mod_sem)
    fetch.start()

    barrier = pltpu.get_barrier_semaphore()
    partners = (
        (f, at.beside(1)), (f, at.beside(-1)), (f, at.s_side), (at.f_far, s), (at.f_core, s),
        (at.f_diag, s),
    )
    for partner in partners:
        pl.semaphore_signal(barrier, inc=1, device_id=partner, device_id_type=MESH)
    for j in range(3):
        stage(j).wait()
    for h in range(heads):
        for j in range(3):
            own_w(j, h).wait()
    fetch.wait()

    @pl.when(f < 2)
    def _():
        past[2:] = jnp.zeros_like(past[2:])

    pl.semaphore_wait(barrier, len(partners))

    for g in range(2):
        w_cross_copy(g).start()
    w_onward(0, s)
    for c in range(0, 2 * width, width // 2):
        mod[:, c : c + width // 2] = jnp.dot(
            emb_ref[...], w_mod_own[:, c : c + width // 2], preferred_element_type=jnp.float32
        )

    chunk = 32
    chunks = frames * rows // chunk

    def chunk_of(x, n):
        return xg.at[x, pl.ds(pl.multiple_of(n * chunk, chunk), chunk)]

    def send_rows(n):
        own = chunk_of(side, n)
        return remote(own, own, xm_send.at[n], xm_recv.at[n], (f, at.s_side))

    def normalize(n):
        i = n // (rows // chunk)
        spot = pl.ds(pl.multiple_of(lax.rem(n, rows // chunk) * chunk, chunk), chunk)
        x32 = x_ref[i, spot, :].astype(jnp.float32)
        mean = jnp.mean(x32, axis=-1, keepdims=True)
        var = jnp.mean((x32 - mean) ** 2, axis=-1, keepdims=True)
        normed = (x32 - mean) * lax.rsqrt(var + 1e-06)
        xm = normed * (1.0 + mod[pl.ds(i, 1), width:]) + mod[pl.ds(i, 1), :width]
        xg[side, pl.ds(pl.multiple_of(n * chunk, chunk), chunk), :] = xm.astype(jnp.bfloat16)
        send_rows(n).start()

    per_step = (chunks + at.pairs - 1) // at.pairs
    pl.loop(0, per_step)(normalize)
    w_begin(0)

    @pl.loop(1, at.pairs)
    def _(k):
        pl.loop(k * per_step, jnp.minimum((k + 1) * per_step, chunks))(normalize)
        w_step(0, k)
        pl.when(k == 1)(lambda: w_onward(1, s))

    wo_start()
    w_end(0)
    w_complete(0)

    def keys_values(x, between):
        @pl.loop(0, heads)
        def _(h):
            w = jnp.concatenate([wg[h, :, j].reshape(-1, hd) for j in range(2)], axis=1)
            both = jnp.dot(xg[x], w, preferred_element_type=jnp.float32)
            key = both[:, :hd]
            key = key * lax.rsqrt(jnp.mean(key * key, axis=-1, keepdims=True) + 1e-06)
            for i in range(frames):
                own = slice(i * rows, (i + 1) * rows)
                key_t = key[own].T.astype(jnp.bfloat16)
                value_t = both[own, hd:].T.astype(jnp.bfloat16)
                win[h, 1 + x, 0, i] = key[own].astype(jnp.bfloat16)
                win[h, 1 + x, 1, i] = value_t
                past[f, h, x, 0, i] = key_t
                past[f, h, x, 1, i] = value_t
            pl.when(x == 0)(lambda: down(h).start())
            pl.when(x == 1)(lambda: up(h).start())
            pl.when(f < 2)(lambda: past_far(h, x).start())
            past_core(h, x).start()
            between(h)

    stride = (at.pairs - 1 + heads - 1) // heads

    def q_steps(h):
        @pl.loop(h * stride + 1, jnp.minimum((h + 1) * stride, at.pairs - 1) + 1)
        def _(k):
            w_step(1, k)
            wo_spread(k)

    def past_pass(h, x):
        past_arrived(at.f_far, h, x)
        past_passed(h, x).start()

    w_begin(1)
    keys_values(side, q_steps)
    w_end(1)
    @pl.loop(0, chunks)
    def _(n):
        other = chunk_of(1 - side, n)
        remote(other, other, xm_send.at[n], xm_recv.at[n], (f, at.s_side)).wait_recv()

    wo_over()
    keys_values(1 - side, lambda h: None)
    w_complete(1)

    @pl.loop(0, heads // 2)
    def _(hp):
        w = jnp.concatenate(
            [wg[2 * hp + n, :, 2].reshape(-1, hd) for n in range(2)], axis=1
        )
        for x in range(2):
            both = jnp.dot(xg[x], w, preferred_element_type=jnp.float32)
            for n in range(2):
                h = 2 * hp + n
                query = both[:, n * hd : (n + 1) * hd]
                query = (
                    query
                    * lax.rsqrt(jnp.mean(query * query, axis=-1, keepdims=True) + 1e-06)
                    * gain_ref[heads * side + h]
                )
                for i in range(frames):
                    q_own[h, x, i] = query[i * rows : (i + 1) * rows].T.astype(jnp.bfloat16)

    @pl.when(f >= 2)
    def _():
        for h in range(heads):
            past_pass(h, side)

    pl.loop(1, at.pairs)(wo_pass_far)
    pl.when(f >= 2)(lambda: past_pass(0, 1 - side))
    pl.loop(0, chunks)(lambda n: send_rows(n).wait_send())
    for g in range(2):
        w_finish(g)

    kk = lax.broadcasted_iota(jnp.int32, (rows, rows), 0)
    rr = lax.broadcasted_iota(jnp.int32, (rows, rows), 1)
    whole = kk >= 0
    band = jnp.concatenate([kk >= rr, whole, kk <= rr], axis=0)
    order = lax.broadcasted_iota(jnp.int32, (groups * frames, rows), 0)

    @pl.loop(0, heads)
    def _(h):
        down(h).wait_recv()
        up(h).wait_recv()
        for x in range(2):
            past_arrived(at.f_core, h, x)
            pl.when(f >= 2)(lambda: past_arrived(at.f_diag, h, x))

        @pl.loop(0, 2 * frames)
        def _(n):
            i = lax.rem(n, frames)
            b = lax.rem(n // frames + 1 - side, 2)
            mine = f * frames + i
            q = q_own[h, b, i]
            keys = jnp.concatenate([win[h, b + j, 0, i] for j in range(3)], axis=0)
            score = jnp.dot(keys, q, preferred_element_type=jnp.float32) * inv
            score = jnp.where(band, score, -1e30)
            q32 = q.astype(jnp.float32)
            time = jnp.full(order.shape, -1e30, jnp.float32)
            for g in range(groups * frames):
                k_g = past[g // frames, h, b, 0, g % frames].astype(jnp.float32)
                t_g = jnp.sum(q32 * k_g, axis=0, keepdims=True) * inv
                time = jnp.where(jnp.logical_and(order == g, order < mine), t_g, time)
            top = jnp.maximum(
                jnp.max(score, axis=0, keepdims=True), jnp.max(time, axis=0, keepdims=True)
            )
            p = jnp.where(band, jnp.exp(score - top), 0.0)
            p_time = jnp.where(order < mine, jnp.exp(time - top), 0.0)
            total = jnp.sum(p, axis=0, keepdims=True) + jnp.sum(p_time, axis=0, keepdims=True)
            values = jnp.concatenate([win[h, b + j, 1, i] for j in range(3)], axis=1)
            acc = jnp.dot(values, p.astype(jnp.bfloat16), preferred_element_type=jnp.float32)
            p_time = p_time.astype(jnp.bfloat16).astype(jnp.float32)
            for g in range(groups * frames):
                v_g = past[g // frames, h, b, 1, g % frames].astype(jnp.float32)
                acc = acc + p_time[g : g + 1] * v_g
            o_own[b, h, i, :, :] = (acc * (1.0 / total)).T.astype(jnp.bfloat16)

            @pl.when(n == frames - 1)
            def _():
                o_swap(h).start()
                pl.when(jnp.logical_and(f >= 2, h + 1 < heads))(
                    lambda: past_pass(h + 1, 1 - side)
                )

        og[side, h] = o_own[side, h]

        last = at.pairs - 1
        pl.loop(
            jnp.clip((h - 1) * last // 2, 0, last), jnp.clip(h * last // 2, 0, last)
        )(wo_pass_side)

    wo_pass_side(at.pairs - 1)

    @pl.loop(0, heads)
    def _(h):
        for copy in (down(h), up(h)):
            copy.wait_send()
        for x in range(2):
            past_core(h, x).wait_send()
            pl.when(f < 2)(lambda: past_far(h, x).wait_send())
            pl.when(f >= 2)(lambda: past_passed(h, x).wait_send())

    wo_complete()
    for h in range(heads):
        remote(
            o_own.at[0, h], og.at[1 - side, h], o_keep, o_recv.at[h], (f, at.s_side)
        ).wait_recv()

    attended = jnp.concatenate(
        [og[x, h].reshape(frames * rows, hd) for x in range(2) for h in range(heads)], axis=1
    )
    for c in range(cols):
        spot = slice(c * part, (c + 1) * part)
        w = wog[c].reshape(inner, part)
        proj = jnp.dot(attended, w, preferred_element_type=jnp.float32)
        for i in range(frames):
            x32 = x_ref[i, :, spot].astype(jnp.float32)
            eps = x32 + proj[i * rows : (i + 1) * rows]
            clean = (x32 - coef_ref[0, i] * eps) * coef_ref[1, i]
            done = (coef_ref[2, i] * clean + coef_ref[3, i] * eps).astype(jnp.bfloat16)
            if i == 0:
                leaving[c] = done
                leave(c).start()
            else:
                out_ref[i - 1, :, spot] = done

    @pl.when(f == 3)
    def _():
        out_ref[frames - 1] = fresh_ref[...]

    wo_finish()
    for h in range(heads):
        o_swap(h).wait_send()
    for c in range(cols):
        leave(c).wait_recv()

        @pl.when(f != 3)
        def _():
            out_ref[frames - 1, :, c * part : (c + 1) * part] = arriving[c]

    for c in range(cols):
        leave(c).wait_send()


def body(frames_in, levels, fresh, w_mod, w_qkv, q_gain, w_out):
    space = lax.axis_size("space")
    groups = lax.axis_size("frame")
    frames, rows, width = frames_in.shape
    heads = q_gain.shape[0]
    hd = w_qkv.shape[1] // (3 * heads)
    half = heads // 2
    bf16 = jnp.bfloat16
    vmem = pl.BlockSpec(memory_space=pltpu.VMEM)
    smem = pl.BlockSpec(memory_space=pltpu.SMEM)
    hbm = pl.BlockSpec(memory_space=pl.ANY)
    dma = pltpu.SemaphoreType.DMA

    emb = embed(levels, w_mod.shape[0])
    emb = jnp.pad(emb, ((0, 16 - frames), (0, 0)))
    later = jnp.maximum(levels - LEVELS // FRAMES, 0)
    a_now = alpha_bar(levels)
    a_later = alpha_bar(later)
    coefs = jnp.stack(
        [jnp.sqrt(1.0 - a_now), 1.0 / jnp.sqrt(a_now), jnp.sqrt(a_later), jnp.sqrt(1.0 - a_later)]
    )
    depth = w_qkv.shape[0]
    wo_depth = w_out.shape[0]
    return pl.pallas_call(
        functools.partial(step_kernel, space),
        out_shape=jax.ShapeDtypeStruct(frames_in.shape, bf16),
        in_specs=[smem, smem, vmem, vmem, vmem, hbm, hbm, hbm],
        out_specs=vmem,
        scratch_shapes=[
            pltpu.VMEM((2, frames * rows, width), bf16),
            pltpu.VMEM((half, space, 3, depth, hd), bf16),
            pltpu.VMEM((3, depth, hd), bf16),
            pltpu.VMEM((groups, space, wo_depth, width // groups), bf16),
            pltpu.VMEM((half, 4, 2, frames, rows, hd), bf16),
            pltpu.VMEM((groups, half, 2, 2, frames, rows, hd), bf16),
            pltpu.VMEM((half, 2, frames, hd, rows), bf16),
            pltpu.VMEM((2, half, frames, rows, hd), bf16),
            pltpu.VMEM((2, half, frames, rows, hd), bf16),
            pltpu.VMEM((16, 2 * width), jnp.float32),
            pltpu.VMEM(w_mod.shape, bf16),
            pltpu.VMEM((groups, rows, width // groups), bf16),
            pltpu.VMEM((groups, rows, width // groups), bf16),
            dma((3, half)), dma((3,)), dma((groups,)),
            dma((frames * rows // 32,)), dma((frames * rows // 32,)),
            dma((2,)), dma((2, space, 2)), dma((2, space)), dma((2, space)), dma((2, space)),
            dma((2, half, space)),
            dma((space, 2)), dma((space,)), dma((2, space)), dma((2, space)),
            dma((groups, space)),
            dma((2, half)), dma((2, half)), dma((3, half, 2)), dma((groups, half, 2)),
            dma, dma((half,)), dma((half,)), dma, dma((groups,)), dma((groups,)),
        ],
        compiler_params=pltpu.CompilerParams(
            collective_id=0, has_side_effects=True, vmem_limit_bytes=VMEM_LIMIT
        ),
        name="step",
    )(q_gain, coefs, emb, frames_in, fresh, w_qkv, w_out, w_mod)


def solution(mesh):
    return jax.shard_map(
        body,
        mesh=mesh,
        in_specs=(
            P("frame", "space", None),
            P("frame"),
            P("space", None),
            P(),
            P("space", None),
            P(),
            P("space", None),
        ),
        out_specs=P("frame", "space", None),
        check_vma=False,
    )
```

```python
import functools
import math

import jax
import jax.numpy as jnp
from jax import lax
from jax.experimental import pallas as pl
from jax.experimental.pallas import tpu as pltpu
from jax.sharding import PartitionSpec as P

LEVELS = 1000
FRAMES = 8
MESH = pl.DeviceIdType.MESH
VMEM_LIMIT = 56 * 1024 * 1024


def embed(levels, freq_count):
    half = freq_count // 2
    freqs = jnp.exp(-math.log(10000.0) * jnp.arange(half, dtype=jnp.float32) / half)
    angles = levels.astype(jnp.float32)[:, None] * freqs[None, :]
    return jnp.concatenate([jnp.cos(angles), jnp.sin(angles)], axis=1).astype(jnp.bfloat16)


def alpha_bar(steps):
    frac = steps.astype(jnp.float32) / LEVELS
    return jnp.cos((frac + 0.008) / 1.008 * (math.pi / 2)) ** 2


class Place:
    def __init__(self, space):
        self.pairs = space // 2
        self.f = lax.axis_index("frame")
        self.s = lax.axis_index("space")
        self.pair = self.s // 2
        self.side = self.s % 2
        core = self.f % 2
        self.f_core = self.f + 1 - 2 * core
        self.f_far = (self.f + 2) % 4
        self.f_diag = (self.f_core + 2) % 4
        self.s_side = self.s + 1 - 2 * self.side

    def beside(self, step):
        return 2 * lax.rem(self.pair + step + self.pairs, self.pairs) + self.side

    def onward(self, way, act):
        if way == 0:
            pl.when(self.pair + 1 < self.pairs)(lambda: act(self.s + 2))
        else:
            pl.when(self.pair >= 1)(lambda: act(self.s - 2))

    def at_distance(self, k, both_sides, act):
        sides = (self.side, 1 - self.side) if both_sides else (self.side,)

        @pl.when(self.pair >= k)
        def _():
            for side in sides:
                act(2 * (self.pair - k) + side, 0)

        @pl.when(self.pair + k < self.pairs)
        def _():
            for side in sides:
                act(2 * (self.pair + k) + side, 1)


def remote(src, dst, send_sem, recv_sem, device):
    return pltpu.make_async_remote_copy(
        src_ref=src,
        dst_ref=dst,
        send_sem=send_sem,
        recv_sem=recv_sem,
        device_id=device,
        device_id_type=MESH,
    )


def step_kernel(
    space, gain_ref, coef_ref, emb_ref, x_ref, fresh_ref, w_ref, wo_ref, w_mod_ref, out_ref,
    xg, wg, wx, wog, win, past, q_own, o_own, og, mod, w_mod_own, leaving, arriving,
    own_w_sem, stage_sem, own_wo_sem, xm_send, xm_recv,
    w_cross, w_chain, w_far, w_core, w_pass, w_recv,
    wo_chain, wo_far, wo_side, wo_core, wo_recv,
    halo_send, halo_recv, past_send, past_recv, o_keep, o_send, o_recv,
    mod_sem, leave_send, leave_recv,
):
    at = Place(space)
    frames, rows, width = x_ref.shape
    heads, hd = og.shape[1], og.shape[4]
    groups = wog.shape[0]
    assert rows == hd
    inner = 2 * heads * hd
    tokens = 2 * rows
    f, s, side = at.f, at.s, at.side
    inv = 1.0 / math.sqrt(hd)

    def columns(j, head):
        return w_ref.at[:, pl.ds(pl.multiple_of((j + 1) % 3 * inner + head * hd, hd), hd)]

    def own_w(j, h):
        return pltpu.make_async_copy(
            columns(j, heads * side + h), wg.at[h, s, j], own_w_sem.at[j, h]
        )

    def stage(j):
        return pltpu.make_async_copy(
            columns(j, heads * (1 - side) + f), wx.at[j], stage_sem.at[j]
        )

    slots = (pl.ds(0, 2), pl.ds(2, 1))

    def w_move(g, col, t, sem, device):
        piece = wg.at[col, t, slots[g]]
        return remote(piece, piece, sem, w_recv.at[g, col, t], device)

    def w_cross_copy(g):
        return remote(
            wx.at[slots[g]], wg.at[f, s, slots[g]], w_cross.at[g], w_recv.at[g, f, s],
            (f, at.s_side),
        )

    def w_next(g, t, way, to):
        return w_move(g, f, t, w_chain.at[g, t, way], (f, to))

    def w_to_far(g, t):
        return w_move(g, f, t, w_far.at[g, t], (at.f_far, s))

    def w_to_core(g, t):
        return w_move(g, f, t, w_core.at[g, t], (at.f_core, s))

    def w_passed(g, t):
        return w_move(g, at.f_far, t, w_pass.at[g, t], (at.f_core, s))

    def w_arrived(g, col, t):
        w_move(g, col, t, w_cross.at[g], (at.f_core, s)).wait_recv()

    def w_onward(g, t):
        for way in (0, 1):
            at.onward(way, lambda to: w_next(g, t, way, to).start())

    def w_share(g, t):
        w_to_far(g, t).start()
        w_to_core(g, t).start()

    def w_begin(g):
        w_arrived(g, f, at.s_side)
        w_onward(g, at.s_side)
        w_share(g, at.s_side)

    def w_take_far(g, t):
        w_arrived(g, at.f_far, t)
        w_passed(g, t).start()

    def w_step(g, k):
        def take(t, way):
            w_arrived(g, f, t)
            at.onward(way, lambda to: w_next(g, t, way, to).start())
            w_share(g, t)

        at.at_distance(k, True, take)
        pl.when(k == 1)(lambda: w_take_far(g, at.s_side))
        pl.when(k >= 2)(
            lambda: at.at_distance(k - 1, True, lambda t, way: w_take_far(g, t))
        )

    def w_end(g):
        at.at_distance(at.pairs - 1, True, lambda t, way: w_take_far(g, t))

    def others(act):
        @pl.loop(0, space)
        def _(t):
            pl.when(t != s)(lambda: act(t))

    def w_complete(g):
        def both(t):
            w_arrived(g, at.f_core, t)
            w_arrived(g, at.f_diag, t)

        others(both)

    def w_finish(g):
        w_cross_copy(g).wait_send()
        for t in (s, at.s_side):
            for way in (0, 1):
                at.onward(way, lambda to: w_next(g, t, way, to).wait_send())

        def chain(t, way):
            at.onward(way, lambda to: w_next(g, t, way, to).wait_send())

        @pl.loop(1, at.pairs)
        def _(k):
            at.at_distance(k, True, chain)

        def shared(t):
            w_to_far(g, t).wait_send()
            w_to_core(g, t).wait_send()
            w_passed(g, t).wait_send()

        others(shared)

    cols = wog.shape[0]
    part = width // cols

    def wo_block(col):
        return wo_ref.at[:, pl.ds(pl.multiple_of(col * part, part), part)]

    def own_wo(c):
        return pltpu.make_async_copy(wo_block(c), wog.at[c, s], own_wo_sem.at[c])

    def wo_move(col, t, sem, device):
        piece = wog.at[col, t]
        return remote(piece, piece, sem, wo_recv.at[col, t], device)

    def wo_first(way, to):
        return remote(
            wo_block(f), wog.at[f, s], wo_chain.at[s, way], wo_recv.at[f, s], (f, to)
        )

    def wo_own_side(n):
        col = (f, at.f_far)[n]
        return remote(
            wo_block(col), wog.at[col, s], wo_side.at[n, s], wo_recv.at[col, s], (f, at.s_side)
        )

    def wo_next(t, way, to):
        return wo_move(f, t, wo_chain.at[t, way], (f, to))

    def wo_to_far(t):
        return wo_move(f, t, wo_far.at[t], (at.f_far, s))

    def wo_to_side(n, t):
        return wo_move((f, at.f_far)[n], t, wo_side.at[n, t], (f, at.s_side))

    def wo_to_core(n, t):
        return wo_move((f, at.f_far)[n], t, wo_core.at[n, t], (at.f_core, s))

    def wo_arrived(col, t):
        wo_move(col, t, o_keep, (at.f_core, s)).wait_recv()

    def wo_start():
        for way in (0, 1):
            at.onward(way, lambda to: wo_first(way, to).start())
        for c in range(cols):
            own_wo(c).start()

    def wo_spread(k):
        def take(t, way):
            wo_arrived(f, t)
            at.onward(way, lambda to: wo_next(t, way, to).start())
            wo_to_far(t).start()
            wo_to_core(0, t).start()

        at.at_distance(k, False, take)

    def wo_over():
        for n in (0, 1):
            wo_own_side(n).start()

        @pl.loop(1, at.pairs)
        def _(k):
            at.at_distance(k, False, lambda t, way: wo_to_side(0, t).start())

    def wo_pass_far(k):
        def take(t, way):
            wo_arrived(at.f_far, t)
            wo_to_side(1, t).start()
            wo_to_core(1, t).start()

        at.at_distance(k, False, take)

    def wo_pass_side(k):
        def take(p):
            t = 2 * p + 1 - side
            for n in (0, 1):
                wo_arrived((f, at.f_far)[n], t)
                wo_to_core(n, t).start()

        pl.when(at.pair >= k)(lambda: take(at.pair - k))
        pl.when(jnp.logical_and(at.pair + k < at.pairs, k > 0))(lambda: take(at.pair + k))

    def wo_complete():
        def both(t):
            wo_arrived(at.f_core, t)
            wo_arrived(at.f_diag, t)

        others(both)
        for c in range(cols):
            own_wo(c).wait()

    def wo_finish():
        for way in (0, 1):
            at.onward(way, lambda to: wo_first(way, to).wait_send())
        for n in (0, 1):
            wo_own_side(n).wait_send()

        def chain(t, way):
            at.onward(way, lambda to: wo_next(t, way, to).wait_send())
            wo_to_far(t).wait_send()
            for n in (0, 1):
                wo_to_side(n, t).wait_send()

        @pl.loop(1, at.pairs)
        def _(k):
            at.at_distance(k, False, chain)

        def shared(t):
            for n in (0, 1):
                wo_to_core(n, t).wait_send()

        others(shared)

    def down(h):
        return remote(
            win.at[h, 1], win.at[h, 3],
            halo_send.at[0, h], halo_recv.at[0, h], (f, at.beside(-1)),
        )

    def up(h):
        return remote(
            win.at[h, 2], win.at[h, 0],
            halo_send.at[1, h], halo_recv.at[1, h], (f, at.beside(1)),
        )

    def past_move(g, h, x, n, device):
        piece = past.at[g, h, x]
        return remote(piece, piece, past_send.at[n, h, x], past_recv.at[g, h, x], device)

    def past_far(h, x):
        return past_move(f, h, x, 0, (at.f_far, s))

    def past_core(h, x):
        return past_move(f, h, x, 1, (at.f_core, s))

    def past_passed(h, x):
        return past_move(at.f_far, h, x, 2, (at.f_core, s))

    def past_arrived(g, h, x):
        piece = past.at[g, h, x]
        remote(piece, piece, o_keep, past_recv.at[g, h, x], (at.f_core, s)).wait_recv()

    def leave(c):
        return remote(
            leaving.at[c], arriving.at[c], leave_send.at[c], leave_recv.at[c],
            (lax.rem(f + 3, 4), s),
        )

    def o_swap(h):
        return remote(
            o_own.at[1 - side, h], og.at[side, h], o_send.at[h], o_recv.at[h], (f, at.s_side)
        )

    for j in range(3):
        stage(j).start()
    for h in range(heads):
        for j in range(3):
            own_w(j, h).start()
    fetch = pltpu.make_async_copy(w_mod_ref, w_mod_own, mod_sem)
    fetch.start()

    barrier = pltpu.get_barrier_semaphore()
    partners = (
        (f, at.beside(1)), (f, at.beside(-1)), (f, at.s_side), (at.f_far, s), (at.f_core, s),
        (at.f_diag, s),
    )
    for partner in partners:
        pl.semaphore_signal(barrier, inc=1, device_id=partner, device_id_type=MESH)
    for j in range(3):
        stage(j).wait()
    for h in range(heads):
        for j in range(3):
            own_w(j, h).wait()
    fetch.wait()

    @pl.when(f < 2)
    def _():
        past[2:] = jnp.zeros_like(past[2:])

    pl.semaphore_wait(barrier, len(partners))

    for g in range(2):
        w_cross_copy(g).start()
    w_onward(0, s)
    for c in range(0, 2 * width, width // 2):
        mod[:, c : c + width // 2] = jnp.dot(
            emb_ref[...], w_mod_own[:, c : c + width // 2], preferred_element_type=jnp.float32
        )

    chunk = 32
    chunks = frames * rows // chunk

    def chunk_of(x, n):
        return xg.at[x, pl.ds(pl.multiple_of(n * chunk, chunk), chunk)]

    def send_rows(n):
        own = chunk_of(side, n)
        return remote(own, own, xm_send.at[n], xm_recv.at[n], (f, at.s_side))

    def normalize(n):
        i = n // (rows // chunk)
        spot = pl.ds(pl.multiple_of(lax.rem(n, rows // chunk) * chunk, chunk), chunk)
        x32 = x_ref[i, spot, :].astype(jnp.float32)
        mean = jnp.mean(x32, axis=-1, keepdims=True)
        var = jnp.mean((x32 - mean) ** 2, axis=-1, keepdims=True)
        normed = (x32 - mean) * lax.rsqrt(var + 1e-06)
        xm = normed * (1.0 + mod[pl.ds(i, 1), width:]) + mod[pl.ds(i, 1), :width]
        xg[side, pl.ds(pl.multiple_of(n * chunk, chunk), chunk), :] = xm.astype(jnp.bfloat16)
        send_rows(n).start()

    per_step = (chunks + 1) // 2
    pl.loop(0, per_step)(normalize)
    w_begin(0)

    @pl.loop(1, at.pairs)
    def _(k):
        pl.loop(k * per_step, jnp.minimum((k + 1) * per_step, chunks))(normalize)
        w_step(0, k)
        pl.when(k == 1)(lambda: w_onward(1, s))

    wo_start()
    w_end(0)
    w_complete(0)

    def keys_values(x, between):
        @pl.loop(0, heads)
        def _(h):
            w = jnp.concatenate([wg[h, :, j].reshape(-1, hd) for j in range(2)], axis=1)
            both = jnp.dot(xg[x], w, preferred_element_type=jnp.float32)
            key = both[:, :hd]
            key = key * lax.rsqrt(jnp.mean(key * key, axis=-1, keepdims=True) + 1e-06)
            for i in range(frames):
                own = slice(i * rows, (i + 1) * rows)
                key_t = key[own].T.astype(jnp.bfloat16)
                value_t = both[own, hd:].T.astype(jnp.bfloat16)
                win[h, 1 + x, 0, i] = key[own].astype(jnp.bfloat16)
                win[h, 1 + x, 1, i] = value_t
                past[f, h, x, 0, i] = key_t
                past[f, h, x, 1, i] = value_t
            pl.when(x == 0)(lambda: down(h).start())
            pl.when(x == 1)(lambda: up(h).start())
            pl.when(f < 2)(lambda: past_far(h, x).start())
            past_core(h, x).start()
            between(h)

    stride = (at.pairs - 1 + heads - 1) // heads

    def q_steps(h):
        @pl.loop(h * stride + 1, jnp.minimum((h + 1) * stride, at.pairs - 1) + 1)
        def _(k):
            w_step(1, k)
            wo_spread(k)

    def past_pass(h, x):
        past_arrived(at.f_far, h, x)
        past_passed(h, x).start()

    w_begin(1)
    keys_values(side, q_steps)
    w_end(1)
    @pl.loop(0, chunks)
    def _(n):
        other = chunk_of(1 - side, n)
        remote(other, other, xm_send.at[n], xm_recv.at[n], (f, at.s_side)).wait_recv()

    wo_over()
    keys_values(1 - side, lambda h: None)
    w_complete(1)

    @pl.loop(0, heads // 2)
    def _(hp):
        w = jnp.concatenate(
            [wg[2 * hp + n, :, 2].reshape(-1, hd) for n in range(2)], axis=1
        )
        for x in range(2):
            both = jnp.dot(xg[x], w, preferred_element_type=jnp.float32)
            for n in range(2):
                h = 2 * hp + n
                query = both[:, n * hd : (n + 1) * hd]
                query = (
                    query
                    * lax.rsqrt(jnp.mean(query * query, axis=-1, keepdims=True) + 1e-06)
                    * gain_ref[heads * side + h]
                )
                for i in range(frames):
                    q_own[h, x, i] = query[i * rows : (i + 1) * rows].T.astype(jnp.bfloat16)

    @pl.when(f >= 2)
    def _():
        for h in range(heads):
            past_pass(h, side)

    pl.loop(1, at.pairs)(wo_pass_far)
    pl.when(f >= 2)(lambda: past_pass(0, 1 - side))
    pl.loop(0, chunks)(lambda n: send_rows(n).wait_send())
    for g in range(2):
        w_finish(g)

    kk = lax.broadcasted_iota(jnp.int32, (rows, rows), 0)
    rr = lax.broadcasted_iota(jnp.int32, (rows, rows), 1)
    whole = kk >= 0
    band = jnp.concatenate([kk >= rr, whole, kk <= rr], axis=0)
    order = lax.broadcasted_iota(jnp.int32, (groups * frames, rows), 0)

    @pl.loop(0, heads)
    def _(h):
        down(h).wait_recv()
        up(h).wait_recv()
        for x in range(2):
            past_arrived(at.f_core, h, x)
            pl.when(f >= 2)(lambda: past_arrived(at.f_diag, h, x))

        @pl.loop(0, 2 * frames)
        def _(n):
            i = lax.rem(n, frames)
            b = lax.rem(n // frames + 1 - side, 2)
            mine = f * frames + i
            q = q_own[h, b, i]
            keys = jnp.concatenate([win[h, b + j, 0, i] for j in range(3)], axis=0)
            score = jnp.dot(keys, q, preferred_element_type=jnp.float32) * inv
            score = jnp.where(band, score, -1e30)
            q32 = q.astype(jnp.float32)
            time = jnp.full(order.shape, -1e30, jnp.float32)
            for g in range(groups * frames):
                k_g = past[g // frames, h, b, 0, g % frames].astype(jnp.float32)
                t_g = jnp.sum(q32 * k_g, axis=0, keepdims=True) * inv
                time = jnp.where(jnp.logical_and(order == g, order < mine), t_g, time)
            top = jnp.maximum(
                jnp.max(score, axis=0, keepdims=True), jnp.max(time, axis=0, keepdims=True)
            )
            p = jnp.where(band, jnp.exp(score - top), 0.0)
            p_time = jnp.where(order < mine, jnp.exp(time - top), 0.0)
            total = jnp.sum(p, axis=0, keepdims=True) + jnp.sum(p_time, axis=0, keepdims=True)
            values = jnp.concatenate([win[h, b + j, 1, i] for j in range(3)], axis=1)
            acc = jnp.dot(values, p.astype(jnp.bfloat16), preferred_element_type=jnp.float32)
            p_time = p_time.astype(jnp.bfloat16).astype(jnp.float32)
            for g in range(groups * frames):
                v_g = past[g // frames, h, b, 1, g % frames].astype(jnp.float32)
                acc = acc + p_time[g : g + 1] * v_g
            o_own[b, h, i, :, :] = (acc * (1.0 / total)).T.astype(jnp.bfloat16)

            @pl.when(n == frames - 1)
            def _():
                o_swap(h).start()
                pl.when(jnp.logical_and(f >= 2, h + 1 < heads))(
                    lambda: past_pass(h + 1, 1 - side)
                )

        og[side, h] = o_own[side, h]

        last = at.pairs - 1
        pl.loop(
            jnp.clip((h - 1) * last // 2, 0, last), jnp.clip(h * last // 2, 0, last)
        )(wo_pass_side)

    wo_pass_side(at.pairs - 1)

    @pl.loop(0, heads)
    def _(h):
        for copy in (down(h), up(h)):
            copy.wait_send()
        for x in range(2):
            past_core(h, x).wait_send()
            pl.when(f < 2)(lambda: past_far(h, x).wait_send())
            pl.when(f >= 2)(lambda: past_passed(h, x).wait_send())

    wo_complete()
    for h in range(heads):
        remote(
            o_own.at[0, h], og.at[1 - side, h], o_keep, o_recv.at[h], (f, at.s_side)
        ).wait_recv()

    attended = jnp.concatenate(
        [og[x, h].reshape(frames * rows, hd) for x in range(2) for h in range(heads)], axis=1
    )
    for c in range(cols):
        spot = slice(c * part, (c + 1) * part)
        w = wog[c].reshape(inner, part)
        proj = jnp.dot(attended, w, preferred_element_type=jnp.float32)
        for i in range(frames):
            x32 = x_ref[i, :, spot].astype(jnp.float32)
            eps = x32 + proj[i * rows : (i + 1) * rows]
            clean = (x32 - coef_ref[0, i] * eps) * coef_ref[1, i]
            done = (coef_ref[2, i] * clean + coef_ref[3, i] * eps).astype(jnp.bfloat16)
            if i == 0:
                leaving[c] = done
                leave(c).start()
            else:
                out_ref[i - 1, :, spot] = done

    @pl.when(f == 3)
    def _():
        out_ref[frames - 1] = fresh_ref[...]

    wo_finish()
    for h in range(heads):
        o_swap(h).wait_send()
    for c in range(cols):
        leave(c).wait_recv()

        @pl.when(f != 3)
        def _():
            out_ref[frames - 1, :, c * part : (c + 1) * part] = arriving[c]

    for c in range(cols):
        leave(c).wait_send()


def body(frames_in, levels, fresh, w_mod, w_qkv, q_gain, w_out):
    space = lax.axis_size("space")
    groups = lax.axis_size("frame")
    frames, rows, width = frames_in.shape
    heads = q_gain.shape[0]
    hd = w_qkv.shape[1] // (3 * heads)
    half = heads // 2
    bf16 = jnp.bfloat16
    vmem = pl.BlockSpec(memory_space=pltpu.VMEM)
    smem = pl.BlockSpec(memory_space=pltpu.SMEM)
    hbm = pl.BlockSpec(memory_space=pl.ANY)
    dma = pltpu.SemaphoreType.DMA

    emb = embed(levels, w_mod.shape[0])
    emb = jnp.pad(emb, ((0, 16 - frames), (0, 0)))
    later = jnp.maximum(levels - LEVELS // FRAMES, 0)
    a_now = alpha_bar(levels)
    a_later = alpha_bar(later)
    coefs = jnp.stack(
        [jnp.sqrt(1.0 - a_now), 1.0 / jnp.sqrt(a_now), jnp.sqrt(a_later), jnp.sqrt(1.0 - a_later)]
    )
    depth = w_qkv.shape[0]
    wo_depth = w_out.shape[0]
    return pl.pallas_call(
        functools.partial(step_kernel, space),
        out_shape=jax.ShapeDtypeStruct(frames_in.shape, bf16),
        in_specs=[smem, smem, vmem, vmem, vmem, hbm, hbm, hbm],
        out_specs=vmem,
        scratch_shapes=[
            pltpu.VMEM((2, frames * rows, width), bf16),
            pltpu.VMEM((half, space, 3, depth, hd), bf16),
            pltpu.VMEM((3, depth, hd), bf16),
            pltpu.VMEM((groups, space, wo_depth, width // groups), bf16),
            pltpu.VMEM((half, 4, 2, frames, rows, hd), bf16),
            pltpu.VMEM((groups, half, 2, 2, frames, rows, hd), bf16),
            pltpu.VMEM((half, 2, frames, hd, rows), bf16),
            pltpu.VMEM((2, half, frames, rows, hd), bf16),
            pltpu.VMEM((2, half, frames, rows, hd), bf16),
            pltpu.VMEM((16, 2 * width), jnp.float32),
            pltpu.VMEM(w_mod.shape, bf16),
            pltpu.VMEM((groups, rows, width // groups), bf16),
            pltpu.VMEM((groups, rows, width // groups), bf16),
            dma((3, half)), dma((3,)), dma((groups,)),
            dma((frames * rows // 32,)), dma((frames * rows // 32,)),
            dma((2,)), dma((2, space, 2)), dma((2, space)), dma((2, space)), dma((2, space)),
            dma((2, half, space)),
            dma((space, 2)), dma((space,)), dma((2, space)), dma((2, space)),
            dma((groups, space)),
            dma((2, half)), dma((2, half)), dma((3, half, 2)), dma((groups, half, 2)),
            dma, dma((half,)), dma((half,)), dma, dma((groups,)), dma((groups,)),
        ],
        compiler_params=pltpu.CompilerParams(
            collective_id=0, has_side_effects=True, vmem_limit_bytes=VMEM_LIMIT
        ),
        name="step",
    )(q_gain, coefs, emb, frames_in, fresh, w_qkv, w_out, w_mod)


def solution(mesh):
    return jax.shard_map(
        body,
        mesh=mesh,
        in_specs=(
            P("frame", "space", None),
            P("frame"),
            P("space", None),
            P(),
            P("space", None),
            P(),
            P("space", None),
        ),
        out_specs=P("frame", "space", None),
        check_vma=False,
    )
```
